256 devices in a mesh: ctx: 32 (over x, y, core), tp: 8 (over z).
Axes of the slice: x: 4, y: 4, z: 8, core: 2. Of those that a mesh axis runs over, the one named last changes fastest.
Arguments:
- query_proj: bfloat16 [4096, 8192], P('ctx', 'tp'), may hold values from -6 to 6
- key_proj: bfloat16 [4096, 8192], P('ctx', 'tp'), may hold values from -6 to 6
- value_proj: bfloat16 [4096, 8192], P('ctx', 'tp'), may hold values from -6 to 6
- grad_out: bfloat16 [4096, 8192], P('ctx', 'tp'), may hold values from -6 to 6
- residues: float32 [512, 16], P(('ctx', 'tp')), may hold values from -1 to 1
- decay_time: float32 [512, 16], P(('ctx', 'tp')), may hold values from 30 to 20480
- doc_lengths: int32 [4], replicated, may hold values from 1 to 2048, 4096 in all
Outputs:
- mixed: bfloat16 [4096, 8192], P('ctx', 'tp')
- grad_query: bfloat16 [4096, 8192], P('ctx', 'tp')
- grad_key: bfloat16 [4096, 8192], P('ctx', 'tp')
- grad_value: bfloat16 [4096, 8192], P('ctx', 'tp')
- grad_residues: float32 [512, 16], P(('ctx', 'tp'))
The draws below stay inside these ranges and needn't reach their ends.
Inputs may be any that keep to these rules, and one draw needn't show every extreme that they name: `doc_lengths`: each document holds at least one token; the longest holds exactly half of 4096.
All inputs are finite; a program needn't handle non-finite values.
Results may differ from the reference program's by a relative error of at most 0.0015.
Values sent between devices are 32-bit elements; how exact they have to be, the bound alone decides.
A program may use at most 128 MiB of HBM per device.

```python
import math
import jax
import jax.numpy as jnp
import numpy as np
from jax import lax

D = 8192
GROUP = 16
MODES = 16
DOCS = 4
SEQ = 4096
GROUPS = 512


def mode_bands(key):
    order_key = jax.random.fold_in(key, 5)
    scores = jax.random.randint(order_key, (GROUPS, MODES), 0, 1 << 20) * MODES
    scores = scores + jnp.arange(MODES, dtype=jnp.int32)[None, :]
    return jnp.argsort(scores, axis=1).astype(jnp.int32)


def banded_times(key, bands, fast_bands):
    level_key = jax.random.fold_in(key, 7)
    offset = jax.random.uniform(level_key, (GROUPS, MODES))
    low = math.log(30.0)
    middle = math.log(0.5 * SEQ)
    high = math.log(5.0 * SEQ)
    band_float = bands.astype(jnp.float32)
    fast_level = (band_float + offset) / fast_bands
    slow_level = (band_float - fast_bands + offset) / (MODES - fast_bands)
    log_time = jnp.where(bands < fast_bands, low + fast_level * (middle - low), middle + slow_level * (high - middle))
    return jnp.minimum(jnp.exp(log_time), 5.0 * SEQ)


def even_bands():
    share = (math.log(0.5 * SEQ) - math.log(30.0)) / (math.log(5.0 * SEQ) - math.log(30.0))
    return max(1, min(MODES - 1, int(MODES * share + 0.5)))


def draw_decay_time(key, part):
    bands = mode_bands(key)
    times = banded_times(key, bands, even_bands())
    return times.astype(jnp.float32)


def draw_residues(key, part):
    bands = mode_bands(key)
    times = banded_times(key, bands, even_bands())
    key = jax.random.fold_in(key, 11)
    parity = 1.0 - 2.0 * (bands % 2).astype(jnp.float32)
    base = parity * jax.random.uniform(key, (GROUPS, MODES), minval=0.6, maxval=1.4)
    spread = jnp.sqrt((1.0 - jnp.exp(-2.0 / times)) / MODES)
    return (base * spread).astype(jnp.float32)


def shard_levels(stream_key, shape, shards, least, largest):
    level = 1.0
    for position, shards_of in shards:
        steps = jax.random.uniform(jax.random.fold_in(jax.random.fold_in(stream_key, 6), position), (shards_of,), jnp.float32, least / len(shards), largest / len(shards))
        level = level * jnp.repeat(jnp.exp(steps), shape[position] // shards_of).reshape((-1,) + (1,) * (len(shape) - 1 - position))
    return level


def split_up(number_of, total, bound, lean):
    loads = [(1 << 20) // math.isqrt(grade ** lean) + 1 for grade in range(2, number_of + 1)]
    spare, counts = total - bound - (number_of - 1), [1] * (number_of - 1)
    while spare > 0:
        movable = [i for i in range(number_of - 1) if counts[i] < bound]
        pool, remaining = sum([loads[i] for i in movable]), spare
        for i in movable:
            addition = min(bound - counts[i], max(1, remaining * loads[i] // pool), spare)
            counts[i] = counts[i] + addition
            spare = spare - addition
    return np.array([bound] + counts)


def ragged_sizes(key, count, total, bound, lean):
    if count == 2:
        one = jax.random.randint(key, (), max(1, total - bound), min(bound, total - 1) + 1)
        return jnp.stack([one, total - one])
    tallies = jnp.asarray(split_up(count, total, bound, lean), jnp.int32)
    twos = (count - 1) // 2
    giver, taker = tallies[1:1 + 2 * twos:2], tallies[2:2 + 2 * twos:2]
    room = jnp.minimum(giver - 1, bound - taker)
    moved = jax.random.randint(jax.random.fold_in(key, 1), (twos,), 0, 1 << 20) % (room + 1)
    tallies = tallies.at[1:1 + 2 * twos:2].set(giver - moved).at[2:2 + 2 * twos:2].set(taker + moved)
    return tallies[jax.random.permutation(jax.random.fold_in(key, 2), count)]


def bell_draw(key, shape, scale, reach, split=(), held_as=jnp.bfloat16):
    array = scale * jax.random.normal(key, shape, jnp.float32)
    if split:
        array = array * shard_levels(key, shape, split, -0.22, 0.18)
    return jnp.clip(array, -reach, reach).astype(held_as)


def setup_inputs(seed: int = 0) -> dict:
    arg_keys = jax.random.split(jax.random.key(seed), 8)
    return {
        "query_proj": bell_draw(arg_keys[0], (SEQ, D), 1.0, 6.0, ((0, 32), (1, 8))),
        "key_proj": bell_draw(arg_keys[1], (SEQ, D), 1.0, 6.0, ((0, 32), (1, 8))),
        "value_proj": bell_draw(arg_keys[2], (SEQ, D), 1.0, 6.0, ((0, 32), (1, 8))),
        "grad_out": bell_draw(arg_keys[3], (SEQ, D), 1.0, 6.0, ((0, 32), (1, 8))),
        "residues": draw_residues(jax.random.fold_in(arg_keys[7], 71), 0),
        "decay_time": draw_decay_time(jax.random.fold_in(arg_keys[7], 71), 0),
        "doc_lengths": ragged_sizes(arg_keys[6], DOCS, SEQ, SEQ // 2, 2).astype(jnp.int32),
    }


HIGHEST = lax.Precision.HIGHEST


def doc_index(positions, doc_lengths):
    doc_ends = jnp.cumsum(doc_lengths).astype(jnp.int32)
    return jnp.sum((positions[:, None] >= doc_ends[None, :]).astype(jnp.int32), axis=1)


def reference(query_proj, key_proj, value_proj, grad_out, residues, decay_time, doc_lengths):
    seq_len = query_proj.shape[0]
    positions = jnp.arange(seq_len, dtype=jnp.int32)
    doc_ids = doc_index(positions, doc_lengths)
    doc_before = doc_index(positions - 1, doc_lengths)
    doc_after = doc_index(positions + 1, doc_lengths)
    keep_prev = (doc_ids == doc_before).astype(jnp.float32)
    keep_next = (doc_ids == doc_after).astype(jnp.float32)
    decay = jnp.exp(-1.0 / decay_time)
    shape3 = (seq_len, GROUPS, GROUP)
    query3 = query_proj.reshape(shape3)
    key3 = key_proj.reshape(shape3)
    value3 = value_proj.reshape(shape3)
    grad3 = grad_out.reshape(shape3)

    def forward_step(carry, inputs):
        state, grad_acc = carry
        query_t, key_t, value_t, grad_t, keep = inputs
        mixture = key_t.astype(jnp.float32) * value_t.astype(jnp.float32)
        state = keep * decay[:, :, None] * state + mixture[:, None, :]
        convolved = jnp.einsum("gm,gmc->gc", residues, state, precision=HIGHEST)
        query_wide = query_t.astype(jnp.float32)
        grad_wide = grad_t.astype(jnp.float32)
        mixed = (query_wide * convolved).astype(jnp.bfloat16)
        grad_query = (grad_wide * convolved).astype(jnp.bfloat16)
        dconv = grad_wide * query_wide
        grad_acc = grad_acc + jnp.einsum("gc,gmc->gm", dconv, state, precision=HIGHEST)
        return (state, grad_acc), (mixed, grad_query)

    zero_state = jnp.zeros((GROUPS, MODES, GROUP), jnp.float32)
    zero_grad = jnp.zeros((GROUPS, MODES), jnp.float32)
    (_, grad_acc), (mixed, grad_query) = lax.scan(
        forward_step, (zero_state, zero_grad), (query3, key3, value3, grad3, keep_prev))

    def backward_step(state, inputs):
        query_t, key_t, value_t, grad_t, keep = inputs
        dconv = grad_t.astype(jnp.float32) * query_t.astype(jnp.float32)
        state = keep * decay[:, :, None] * state + dconv[:, None, :]
        dmix = jnp.einsum("gm,gmc->gc", residues, state, precision=HIGHEST)
        grad_key = (dmix * value_t.astype(jnp.float32)).astype(jnp.bfloat16)
        grad_value = (dmix * key_t.astype(jnp.float32)).astype(jnp.bfloat16)
        return state, (grad_key, grad_value)

    _, (grad_key, grad_value) = lax.scan(
        backward_step, zero_state, (query3, key3, value3, grad3, keep_next), reverse=True)
    full = (seq_len, GROUPS * GROUP)
    grad_residues = grad_acc / seq_len
    return (mixed.reshape(full), grad_query.reshape(full), grad_key.reshape(full),
            grad_value.reshape(full), grad_residues)
```

```python
import functools

import jax
import jax.numpy as jnp
from jax import lax
from jax.experimental import pallas as pl
from jax.experimental.pallas import tpu as pltpu
from jax.sharding import PartitionSpec as P

GROUP = 16
MODES = 16
LANES = 128
TILE_GROUPS = LANES // GROUP
OWN_GROUPS = 2
PIECES = TILE_GROUPS // OWN_GROUPS
ROWS = GROUP // PIECES

F32 = jnp.float32
BF16 = jnp.bfloat16
MESH = pl.DeviceIdType.MESH


def halves(x):
    high = x.astype(BF16)
    return high, (x - high.astype(F32)).astype(BF16)


def wide(x):
    return jnp.concatenate(halves(x), axis=1)


def fold(product):
    return product[:, :LANES] + product[:, LANES:]


def twice(x):
    return jnp.concatenate([x, x], axis=0)


def dot_wide(left, right):
    return fold(jnp.dot(left, twice(right), preferred_element_type=F32))


def dot_wide_nt(left, high, low):
    right = jnp.concatenate(
        [jnp.concatenate([high, high], axis=1), jnp.concatenate([low, low], axis=1)], axis=0
    )
    product = lax.dot_general(left, right, (((1,), (1,)), ((), ())), preferred_element_type=F32)
    return fold(product)


def iota(shape, dim):
    return lax.broadcasted_iota(jnp.int32, shape, dim)


def exchange_kernel(
    nctx,
    ntp,
    doc_ref,
    query_hbm,
    key_hbm,
    value_hbm,
    grad_hbm,
    res_hbm,
    time_hbm,
    conv_ref,
    dmix_ref,
    grad_res_ref,
    query,
    key,
    value,
    grad,
    res,
    time,
    par_send,
    par_recv,
    mix_wide,
    dconv_wide,
    mix_t,
    dconv_t,
    lead_wide,
    tail_wide,
    decay_wide,
    flip_wide,
    state_send,
    state_recv,
    carry_send,
    carry_recv,
    corr_send,
    corr_recv,
    part_send,
    part_recv,
    load_sem,
    send_sem,
    recv_sem,
):
    tokens, channels = query.shape
    tiles = channels // LANES
    seq_len = tokens * nctx
    c = lax.axis_index("ctx")
    p = lax.axis_index("tp")
    flat = c * ntp + p
    plane = flat // nctx
    mine = lax.rem(flat, nctx)
    owns_here = plane == p

    def owner(block):
        device = p * nctx + block
        return device // ntp, lax.rem(device, ntp)

    def push(src, dst, kind, ctx_to, tp_to):
        here = jnp.logical_and(ctx_to == c, tp_to == p)

        @pl.when(jnp.logical_not(here))
        def _():
            pltpu.make_async_remote_copy(
                src_ref=src,
                dst_ref=dst,
                send_sem=send_sem.at[kind],
                recv_sem=recv_sem.at[kind],
                device_id=(ctx_to, tp_to),
                device_id_type=MESH,
            ).start()

        @pl.when(here)
        def _():
            pltpu.make_async_copy(src, dst, recv_sem.at[kind]).start()

    def arrived(ref, kind):
        pltpu.make_async_copy(ref, ref, recv_sem.at[kind]).wait()

    def sent(ref, kind):
        pltpu.make_async_copy(ref, ref, send_sem.at[kind]).wait()

    sources = (query_hbm, key_hbm, value_hbm, grad_hbm, res_hbm, time_hbm)
    targets = (query, key, value, grad, res, time)
    loads = [
        pltpu.make_async_copy(src, dst, load_sem.at[i])
        for i, (src, dst) in enumerate(zip(sources, targets))
    ]
    for i in (4, 5, 1, 2, 0, 3):
        loads[i].start()

    barrier = pltpu.get_barrier_semaphore()

    def greet(i, _):
        block = lax.rem(mine + i, nctx)
        ctx_to, tp_to = owner(block)

        @pl.when(jnp.logical_not(jnp.logical_and(ctx_to == c, tp_to == p)))
        def _():
            pl.semaphore_signal(
                barrier, inc=1, device_id=(ctx_to, tp_to), device_id_type=MESH
            )

        return 0

    lax.fori_loop(0, nctx, greet, 0)

    loads[4].wait()
    loads[5].wait()
    rate = 1.0 / time[...]
    residue = res[...]
    par_send[0:1, :] = jnp.concatenate([rate[0:1], rate[1:2]] * PIECES, axis=1)
    par_send[1:2, :] = jnp.concatenate([residue[0:1], residue[1:2]] * PIECES, axis=1)

    @pl.when(owns_here)
    def _():
        pl.semaphore_wait(barrier, nctx - 1)

    @pl.when(jnp.logical_not(owns_here))
    def _():
        pl.semaphore_wait(barrier, nctx)

    def send_par(i, _):
        push(par_send, par_recv.at[mine], 0, lax.rem(c + i, nctx), plane)
        return 0

    lax.fori_loop(0, nctx, send_par, 0)

    first = c * tokens
    end0 = doc_ref[0]
    end1 = end0 + doc_ref[1]
    end2 = end1 + doc_ref[2]
    end3 = end2 + doc_ref[3]
    ends = (end0, end1, end2, end3)

    def doc_of(position):
        total = (position >= end0).astype(jnp.int32)
        for end in ends[1:]:
            total = total + (position >= end).astype(jnp.int32)
        return total

    square = (tokens, LANES)
    row = iota(square, 0)
    col = iota(square, 1)
    doc_row = doc_of(first + row)
    doc_col = doc_of(first + col)
    same = doc_row == doc_col
    upper = jnp.where(jnp.logical_and(same, col >= row), 1.0, 0.0)
    lower = jnp.where(jnp.logical_and(same, col <= row), 1.0, 0.0)
    flip_row = tokens - 1 - row
    turned = jnp.where(
        jnp.logical_and(doc_of(first + flip_row) == doc_col, col >= flip_row), 1.0, 0.0
    )
    turn = jnp.where(flip_row == col, 1.0, 0.0).astype(BF16)
    block_of = iota((1, LANES), 1) // GROUP

    for i in (1, 2, 0, 3):
        loads[i].wait()

    def lanes_of(q):
        return pl.ds(pl.multiple_of(q * LANES, LANES), LANES)

    def local(q, _):
        at = lanes_of(q)
        mixture = key[:, at].astype(F32) * value[:, at].astype(F32)
        dconv = grad[:, at].astype(F32) * query[:, at].astype(F32)
        mix_high, mix_low = halves(mixture)
        d_high, d_low = halves(dconv)
        mix_wide[q] = jnp.concatenate([mix_high, mix_low], axis=1)
        dconv_wide[q] = jnp.concatenate([d_high, d_low], axis=1)
        mix_t[q] = wide(mixture.T)
        dconv_t[q] = wide(dconv.T)
        right = jnp.concatenate(
            [jnp.concatenate([d_high, d_high], axis=1), jnp.concatenate([d_low, d_low], axis=1)],
            axis=0,
        )
        left = jnp.dot(
            turn, jnp.concatenate([mix_high, mix_low], axis=1), preferred_element_type=F32
        ).astype(BF16)
        lane_block = lax.rem(iota((1, 2 * LANES), 1), LANES) // GROUP
        for g in range(TILE_GROUPS):
            masked = jnp.where(lane_block == g, left, jnp.zeros_like(left))
            pairs = fold(
                lax.dot_general(masked, right, (((1,), (1,)), ((), ())), preferred_element_type=F32)
            )
            lags = pltpu.roll(pairs * turned, 1, 1, stride=1, stride_axis=0)
            corr_send[PIECES * q + g // OWN_GROUPS, g % OWN_GROUPS : g % OWN_GROUPS + 1, :] = (
                jnp.sum(lags, axis=0, keepdims=True)
            )
        return 0

    lax.fori_loop(0, tiles, local, 0)

    arrived(par_recv, 0)

    def par_row(q, which):
        lane_piece = iota((1, LANES), 1) // (LANES // PIECES)
        out = par_recv[PIECES * q, which : which + 1, :]
        for b in range(1, PIECES):
            out = jnp.where(lane_piece == b, par_recv[PIECES * q + b, which : which + 1, :], out)
        return out

    pos = row.astype(F32)
    doc_first = doc_of(first)
    doc_last = doc_of(first + tokens - 1)
    doc_before = doc_of(first - 1)
    doc_after = doc_of(first + tokens)
    at_start = jnp.where(doc_row == doc_first, 1.0, 0.0)
    at_end = jnp.where(doc_row == doc_last, 1.0, 0.0)
    with_before = jnp.where(doc_row == doc_before, 1.0, 0.0)
    with_after = jnp.where(doc_row == doc_after, 1.0, 0.0)

    def own_blocks(x):
        out = jnp.zeros((GROUP, LANES), F32)
        for g in range(TILE_GROUPS):
            out = jnp.where(block_of == g, x[g * GROUP : (g + 1) * GROUP, :], out)
        return out

    def states(step, _):
        q = lax.rem(c // PIECES + step, tiles)
        rate_row = par_row(q, 0)
        decay = jnp.exp(-pos * rate_row)
        flip = jnp.exp((pos - (tokens - 1.0)) * rate_row)
        decay_wide[q] = wide(decay)
        flip_wide[q] = wide(flip)
        end_state = own_blocks(dot_wide(mix_t[q], wide(flip * at_end)))
        start_state = own_blocks(dot_wide(dconv_t[q], wide(decay * at_start)))
        for r in range(PIECES):
            j = PIECES * q + r
            state_send[j, 0:ROWS, :] = end_state[r * ROWS : (r + 1) * ROWS, :]
            state_send[j, ROWS:, :] = start_state[r * ROWS : (r + 1) * ROWS, :]
            push(state_send.at[j], state_recv.at[c], 1, j, p)
        return 0

    lax.fori_loop(0, tiles, states, 0)

    def send_corr(i, _):
        block = lax.rem(mine + i, nctx)
        ctx_to, tp_to = owner(block)
        push(corr_send.at[block], corr_recv.at[c], 2, ctx_to, tp_to)
        return 0

    lax.fori_loop(0, nctx, send_corr, 0)

    def selected(q):
        res_row = par_row(q, 1)
        chosen = jnp.where(block_of == iota((TILE_GROUPS, LANES), 0), res_row, 0.0)
        return res_row, wide(chosen)

    def conv_local(q, _):
        rate_row = par_row(q, 0)
        res_row, chosen = selected(q)
        flip = flip_wide[q]
        taps = dot_wide_nt(chosen, flip[:, :LANES], flip[:, LANES:])
        right = mix_wide[q]
        total = jnp.zeros(square, F32)
        for g in range(TILE_GROUPS):
            spread = jnp.broadcast_to(taps[g : g + 1, :], square)
            toeplitz = pltpu.roll(spread, 1, 1, stride=1, stride_axis=0) * lower
            total = jnp.where(block_of == g, dot_wide(wide(toeplitz), right), total)
        conv_ref[:, lanes_of(q)] = total
        lead_wide[q] = wide(jnp.exp(-(pos + 1.0) * rate_row) * (res_row * with_before))
        return 0

    lax.fori_loop(0, tiles, conv_local, 0)

    arrived(state_recv, 1)
    my_rate = par_row(c // PIECES, 0)
    span = jnp.exp(-float(tokens) * my_rate)
    once = jnp.exp(-my_rate)
    piece = (2 * ROWS, LANES)
    cut_in = [jnp.full(piece, end // tokens, jnp.int32) for end in ends[:3]]
    cut_out = [jnp.full(piece, (end - 1) // tokens, jnp.int32) for end in ends[:3]]
    cut_at = [jnp.full(piece, end, jnp.int32) for end in ends[:3]]
    is_end = iota(piece, 0) < ROWS

    def kept(cuts, at, factor):
        hit = cuts[0] == at
        for cut in cuts[1:]:
            hit = jnp.logical_or(hit, cut == at)
        return jnp.where(hit, 0.0, factor)

    back = jnp.zeros(piece, F32)
    for i in range(nctx - 1, -1, -1):
        carry_send[i] = back
        back = kept(cut_out, i, span) * back + state_recv[i]
    ahead = jnp.zeros(piece, F32)
    carried = jnp.zeros(piece, F32)
    for i in range(nctx):
        here = state_recv[i]
        carry_send[i] = jnp.where(is_end, ahead, carry_send[i])
        push(carry_send.at[i], carry_recv.at[c], 3, i, p)
        begun = pltpu.roll(here, ROWS, 0)
        carried = carried + kept(cut_at, i * tokens, once) * (ahead * begun)
        ahead = kept(cut_in, i, span) * ahead + here
    carried = jnp.where(is_end, carried, 0.0)
    part_send[...] = jnp.sum(carried, axis=0, keepdims=True)
    for b in range(PIECES):
        block = (c // PIECES) * PIECES + b
        ctx_to, tp_to = owner(block)
        push(part_send, part_recv.at[lax.rem(c, PIECES)], 4, ctx_to, tp_to)

    def dmix_local(q, _):
        rate_row = par_row(q, 0)
        res_row, chosen = selected(q)
        decay = decay_wide[q]
        taps = dot_wide_nt(chosen, decay[:, :LANES], decay[:, LANES:])
        right = dconv_wide[q]
        total = jnp.zeros(square, F32)
        for g in range(TILE_GROUPS):
            spread = jnp.broadcast_to(taps[g : g + 1, :], square)
            toeplitz = pltpu.roll(spread, 0, 1, stride=1, stride_axis=0) * upper
            total = jnp.where(block_of == g, dot_wide(wide(toeplitz), right), total)
        dmix_ref[:, lanes_of(q)] = total
        tail_wide[q] = wide(jnp.exp((pos - float(tokens)) * rate_row) * (res_row * with_after))
        return 0

    lax.fori_loop(0, tiles, dmix_local, 0)

    arrived(corr_recv, 2)

    def add_corr(i, total):
        return total + corr_recv[i]

    corr = lax.fori_loop(0, nctx, add_corr, jnp.zeros((OWN_GROUPS, LANES), F32))
    powers = jnp.exp(-pos * par_send[0:1, :])
    by_mode = dot_wide(wide(jnp.concatenate([corr] * PIECES, axis=0)), wide(powers))
    lane = iota((1, LANES), 1)
    grad_row = jnp.where(lax.rem(lane // MODES, OWN_GROUPS) == 0, by_mode[0:1], by_mode[1:2])
    arrived(part_recv, 4)
    for r in range(PIECES):
        grad_row = grad_row + part_recv[r]
    step = LANES // PIECES
    grad_row = jnp.where(lane // step == lax.rem(mine, PIECES), grad_row / seq_len, 0.0)
    whole = grad_row
    for b in range(1, PIECES):
        whole = whole + pltpu.roll(grad_row, b * step, 1)
    grad_res_ref[0:1, :] = whole[:, :MODES]
    grad_res_ref[1:2, :] = pltpu.roll(whole, LANES - MODES, 1)[:, :MODES]

    arrived(carry_recv, 3)
    own = iota((LANES, LANES), 0) // GROUP == iota((LANES, LANES), 1) // MODES

    def spread_out(q, rows):
        state = jnp.concatenate(
            [carry_recv[PIECES * q + r, rows, :] for r in range(PIECES)], axis=0
        )
        state = jnp.where(own, jnp.concatenate([state] * TILE_GROUPS, axis=0), 0.0)
        return halves(state)

    def enter(q, _):
        at = lanes_of(q)
        conv_ref[:, at] += dot_wide_nt(lead_wide[q], *spread_out(q, slice(0, ROWS)))
        dmix_ref[:, at] += dot_wide_nt(tail_wide[q], *spread_out(q, slice(ROWS, 2 * ROWS)))
        return 0

    lax.fori_loop(0, tiles, enter, 0)

    sent(state_send.at[pl.ds(0, nctx - 1)], 1)
    sent(carry_send.at[pl.ds(0, nctx - 1)], 3)

    @pl.when(owns_here)
    def _():
        sent(par_recv.at[pl.ds(0, nctx - 1)], 0)
        sent(corr_send.at[pl.ds(0, nctx - 1)], 2)

    @pl.when(jnp.logical_not(owns_here))
    def _():
        sent(par_recv, 0)
        sent(corr_send, 2)

    to_self = jnp.logical_and(owns_here, mine // PIECES == c // PIECES)

    @pl.when(to_self)
    def _():
        sent(part_recv.at[pl.ds(0, PIECES - 1)], 4)

    @pl.when(jnp.logical_not(to_self))
    def _():
        sent(part_recv, 4)


def per_device(nctx, ntp, query, key, value, grad, residues, decay_time, doc_lengths):
    tokens, channels = query.shape
    tiles = channels // LANES
    vmem = pl.BlockSpec(memory_space=pltpu.VMEM)
    hbm = pl.BlockSpec(memory_space=pl.ANY)
    flat = jax.ShapeDtypeStruct((tokens, channels), F32)
    pair = pltpu.VMEM((tiles, LANES, 2 * LANES), BF16)
    piece = pltpu.VMEM((nctx, 2 * ROWS, LANES), F32)
    conv, dmix, grad_res = pl.pallas_call(
        functools.partial(exchange_kernel, nctx, ntp),
        out_shape=(flat, flat, jax.ShapeDtypeStruct(residues.shape, F32)),
        in_specs=[pl.BlockSpec(memory_space=pltpu.SMEM)] + [hbm] * 6,
        out_specs=(vmem, vmem, vmem),
        scratch_shapes=[pltpu.VMEM((tokens, channels), BF16)] * 4
        + [pltpu.VMEM((OWN_GROUPS, MODES), F32)] * 2
        + [pltpu.VMEM((OWN_GROUPS, LANES), F32), pltpu.VMEM((nctx, OWN_GROUPS, LANES), F32)]
        + [pair] * 8
        + [piece] * 4
        + [pltpu.VMEM((nctx, OWN_GROUPS, LANES), F32)] * 2
        + [pltpu.VMEM((1, LANES), F32), pltpu.VMEM((PIECES, 1, LANES), F32)]
        + [
            pltpu.SemaphoreType.DMA((6,)),
            pltpu.SemaphoreType.DMA((5,)),
            pltpu.SemaphoreType.DMA((5,)),
        ],
        compiler_params=pltpu.CompilerParams(
            collective_id=0, has_side_effects=True, vmem_limit_bytes=48 * 1024 * 1024
        ),
    )(doc_lengths, query, key, value, grad, residues, decay_time)
    mixed = (query.astype(F32) * conv).astype(BF16)
    grad_query = (grad.astype(F32) * conv).astype(BF16)
    grad_key = (dmix * value.astype(F32)).astype(BF16)
    grad_value = (dmix * key.astype(F32)).astype(BF16)
    return mixed, grad_query, grad_key, grad_value, grad_res


def solution(mesh):
    main = P("ctx", "tp")
    owned = P(("ctx", "tp"), None)
    return jax.shard_map(
        functools.partial(per_device, mesh.shape["ctx"], mesh.shape["tp"]),
        mesh=mesh,
        in_specs=(main, main, main, main, owned, owned, P()),
        out_specs=(main, main, main, main, owned),
        check_vma=False,
    )
```

```python
import functools

import jax
import jax.numpy as jnp
from jax import lax
from jax.experimental import pallas as pl
from jax.experimental.pallas import tpu as pltpu
from jax.sharding import PartitionSpec as P

GROUP = 16
MODES = 16
LANES = 128
SUB = 8
TILE_GROUPS = LANES // GROUP
OWN_GROUPS = 2
PIECES = TILE_GROUPS // OWN_GROUPS
ROWS = GROUP // PIECES

F32 = jnp.float32
BF16 = jnp.bfloat16
MESH = pl.DeviceIdType.MESH

PAR, STATE, CORR, CARRY, PART = range(5)


def halves(x):
    high = x.astype(BF16)
    return high, (x - high.astype(F32)).astype(BF16)


def wide(x):
    return jnp.concatenate(halves(x), axis=1)


def fold(product):
    return product[:, :LANES] + product[:, LANES:]


def twice(x):
    return jnp.concatenate([x, x], axis=0)


def dot(left, right):
    return jnp.dot(left, right, preferred_element_type=F32)


def dot_nt(left, right):
    return lax.dot_general(left, right, (((1,), (1,)), ((), ())), preferred_element_type=F32)


def iota(shape, dim):
    return lax.broadcasted_iota(jnp.int32, shape, dim)


def stack_halves(x):
    high, low = halves(x)
    parts = []
    for g in range(TILE_GROUPS):
        rows = slice(g * GROUP, (g + 1) * GROUP)
        parts += [high[rows], low[rows]]
    return jnp.concatenate(parts, axis=0)


def grid_of(nctx):
    chips = nctx // 2
    nx = 1
    while nx * nx * 4 <= chips:
        nx *= 2
    return nx, chips // nx


def far_first(n):
    return sorted(range(n), key=lambda d: -min(d, n - d))


def exchange_kernel(
    nctx,
    ntp,
    doc_hbm,
    query_hbm,
    key_hbm,
    value_hbm,
    grad_hbm,
    res_hbm,
    time_hbm,
    mixed_hbm,
    grad_query_hbm,
    grad_key_hbm,
    grad_value_hbm,
    grad_res_ref,
    doc_ref,
    query,
    key,
    value,
    grad,
    mixed,
    grad_query,
    grad_key,
    grad_value,
    raw,
    par_send,
    par_recv,
    rates,
    weights,
    own_par,
    mix_t,
    dconv_t,
    lead_wide,
    tail_wide,
    conv_t,
    dmix_t,
    state_send,
    state_recv,
    carry_send,
    carry_recv,
    corr_send,
    corr_recv,
    part_send,
    part_recv,
    load_sem,
    store_sem,
    raw_send_sem,
    raw_recv_sem,
    par_recv_sem,
    send_sem,
    recv_sem,
):
    tokens, channels = query.shape
    tiles = channels // LANES
    seq_len = tokens * nctx
    relays = nctx // ntp
    relay_tiles = tiles // relays
    nx, ny = grid_of(nctx)
    c = lax.axis_index("ctx")
    p = lax.axis_index("tp")
    plane = c // relays
    is_relay = plane == p
    mine = lax.rem(c, relays) * ntp + p
    piece_of = lax.rem(c, PIECES)
    tile_of = c // PIECES
    my_x = c // (2 * ny)
    my_y = lax.rem(c // 2, ny)
    my_core = lax.rem(c, 2)

    def remote(src, dst, send, recv, ctx_to, tp_to):
        return pltpu.make_async_remote_copy(
            src_ref=src,
            dst_ref=dst,
            send_sem=send,
            recv_sem=recv,
            device_id=(ctx_to, tp_to),
            device_id_type=MESH,
        )

    def push(src, dst, kind, ctx_to, tp_to):
        here = jnp.logical_and(ctx_to == c, tp_to == p)

        @pl.when(jnp.logical_not(here))
        def _():
            remote(src, dst, send_sem.at[kind], recv_sem.at[kind], ctx_to, tp_to).start()

        @pl.when(here)
        def _():
            pltpu.make_async_copy(src, dst, recv_sem.at[kind]).start()

    def arrived(ref, kind):
        pltpu.make_async_copy(ref, ref, recv_sem.at[kind]).wait()

    def sent(ref, kind):
        pltpu.make_async_copy(ref, ref, send_sem.at[kind]).wait()

    xs = [lax.rem(my_x + d, nx) * (2 * ny) for d in range(nx)]
    ys = [lax.rem(my_y + d, ny) * 2 for d in range(ny)]
    cores = [my_core, 1 - my_core]
    offsets = [(dx, dy, dk) for dx in range(nx) for dy in range(ny) for dk in range(2)]
    offsets.sort(key=lambda o: -(min(o[0], nx - o[0]) + min(o[1], ny - o[1]) + 0.1 * o[2]))
    around = [xs[dx] + ys[dy] + cores[dk] for dx, dy, dk in offsets if dx or dy or dk]

    barrier = pltpu.get_barrier_semaphore()

    def greet(ctx_to, tp_to):
        pl.semaphore_signal(barrier, inc=1, device_id=(ctx_to, tp_to), device_id_type=MESH)

    @pl.when(is_relay)
    def _():
        for d in far_first(ntp):
            if d:
                greet(c, lax.rem(p + d, ntp))

    for a in range(relays):
        relay = p * relays + a

        @pl.when(relay != c)
        def _():
            greet(relay, p)

    sources = (query_hbm, key_hbm, value_hbm, grad_hbm, doc_hbm, time_hbm, res_hbm)
    targets = (query, key, value, grad, doc_ref, own_par.at[0], own_par.at[1])
    loads = [
        pltpu.make_async_copy(src, dst, load_sem.at[i])
        for i, (src, dst) in enumerate(zip(sources, targets))
    ]
    for i in (4, 1, 2, 0, 3, 5, 6):
        loads[i].start()

    def send_raw():
        pl.semaphore_wait(barrier, 1)
        for k, src in enumerate((time_hbm, res_hbm)):
            remote(
                src, raw.at[k, p], raw_send_sem.at[k], raw_recv_sem.at[k, p], c, plane
            ).start()

    @pl.when(p > plane)
    def _():
        send_raw()

    @pl.when(is_relay)
    def _():
        for k, src in enumerate((time_hbm, res_hbm)):
            pltpu.make_async_copy(src, raw.at[k, p], raw_recv_sem.at[k, p]).start()

    first = c * tokens
    loads[4].wait()
    end0 = doc_ref[0]
    end1 = end0 + doc_ref[1]
    end2 = end1 + doc_ref[2]
    end3 = end2 + doc_ref[3]
    ends = (end0, end1, end2, end3)

    def doc_of(position):
        total = (position >= end0).astype(jnp.int32)
        for end in ends[1:]:
            total = total + (position >= end).astype(jnp.int32)
        return total

    square = (tokens, LANES)
    row = iota(square, 0)
    col = iota(square, 1)
    doc_row = doc_of(first + row)
    doc_col = doc_of(first + col)
    flip_row = tokens - 1 - row
    turned = jnp.where(
        jnp.logical_and(doc_of(first + flip_row) == doc_col, col >= flip_row), 1.0, 0.0
    )
    turn = jnp.where(flip_row == col, 1.0, 0.0).astype(BF16)
    block_of = iota((1, LANES), 1) // GROUP

    for i in range(4):
        loads[i].wait()

    def lanes_of(q):
        return pl.ds(pl.multiple_of(q * LANES, LANES), LANES)

    def local(q, _):
        at = lanes_of(q)
        mixture = key[:, at].astype(F32) * value[:, at].astype(F32)
        dconv = grad[:, at].astype(F32) * query[:, at].astype(F32)
        mix_t[q] = stack_halves(mixture.T)
        dconv_t[q] = stack_halves(dconv.T)
        d_high, d_low = halves(dconv)
        right = jnp.concatenate(
            [jnp.concatenate([d_high, d_high], axis=1), jnp.concatenate([d_low, d_low], axis=1)],
            axis=0,
        )
        left = dot(turn, wide(mixture)).astype(BF16)
        lane_block = lax.rem(iota((1, 2 * LANES), 1), LANES) // GROUP
        for g in range(TILE_GROUPS):
            masked = jnp.where(lane_block == g, left, jnp.zeros_like(left))
            lags = pltpu.roll(
                fold(dot_nt(masked, right)) * turned, 1, 1, stride=1, stride_axis=0
            )
            corr_send[PIECES * q + g // OWN_GROUPS, g % OWN_GROUPS : g % OWN_GROUPS + 1, :] = (
                jnp.sum(lags, axis=0, keepdims=True)
            )
        return 0

    lax.fori_loop(0, tiles, local, 0)

    @pl.when(p < plane)
    def _():
        send_raw()

    my_relay = lax.rem(c, relays)

    @pl.when(is_relay)
    def _():
        for k, src in enumerate((time_hbm, res_hbm)):
            for z in range(ntp):
                pltpu.make_async_copy(src, raw.at[k, z], raw_recv_sem.at[k, z]).wait()
        for t in range(relay_tiles):
            for k in range(2):
                parts = []
                for b in range(PIECES):
                    block = raw[k, t * PIECES + b]
                    parts += [block[0:1], block[1:2]]
                line = jnp.concatenate(parts, axis=1)
                at = 2 * t + k
                par_send[at : at + 1, :] = 1.0 / line if k == 0 else line
        pl.semaphore_wait(barrier, nctx - 1)
        for to in around:
            remote(
                par_send, par_recv.at[my_relay], send_sem.at[PAR], par_recv_sem.at[my_relay], to, p
            ).start()
        pltpu.make_async_copy(par_send, par_recv.at[my_relay], par_recv_sem.at[my_relay]).start()

    pos = iota((SUB, LANES), 0).astype(F32)
    eights = iota((tokens // SUB, LANES), 0).astype(F32) * SUB
    doc_first = doc_of(first)
    doc_last = doc_of(first + tokens - 1)
    at_start = jnp.where(doc_row == doc_first, 1.0, 0.0)
    at_end = jnp.where(doc_row == doc_last, 1.0, 0.0)

    def own_blocks(x):
        out = jnp.zeros((GROUP, LANES), F32)
        for g in range(TILE_GROUPS):
            both = x[2 * g * GROUP : (2 * g + 1) * GROUP] + x[(2 * g + 1) * GROUP : (2 * g + 2) * GROUP]
            out = jnp.where(block_of == g, fold(both), out)
        return out

    for a in range(relays):
        pltpu.make_async_copy(par_recv.at[a], par_recv.at[a], par_recv_sem.at[a]).wait()
        for t in range(relay_tiles):
            rates[a * relay_tiles + t] = par_recv[a, 2 * t : 2 * t + 1, :]
            weights[a * relay_tiles + t] = par_recv[a, 2 * t + 1 : 2 * t + 2, :]

    def states(q):
        rate_row = rates[q]
        tall = jnp.exp(-eights * rate_row)
        short = jnp.exp(-pos * rate_row)
        short_flip = jnp.exp((pos - (SUB - 1.0)) * rate_row)
        steps = tokens // SUB
        decay = jnp.concatenate([short * tall[i : i + 1] for i in range(steps)], axis=0)
        flip = jnp.concatenate(
            [short_flip * tall[steps - 1 - i : steps - i] for i in range(steps)], axis=0
        )
        end_state = own_blocks(dot(mix_t[q], wide(flip * at_end)))
        start_state = own_blocks(dot(dconv_t[q], wide(decay * at_start)))
        for r in range(PIECES):
            j = PIECES * q + r
            state_send[j, 0:ROWS, :] = end_state[r * ROWS : (r + 1) * ROWS, :]
            state_send[j, ROWS:, :] = start_state[r * ROWS : (r + 1) * ROWS, :]
        for r in range(PIECES):
            j = PIECES * q + r
            push(state_send.at[j], state_recv.at[c], STATE, j, p)

    sides = tiles // nx
    for dx in far_first(nx):
        for side in reversed(range(sides)):
            q_x = lax.rem(my_x + dx, nx) * sides
            states(q_x + lax.rem(lax.rem(tile_of, sides) + side, sides))

    for z in far_first(ntp):
        for a in range(relays):
            tp_to = lax.rem(p + z, ntp)
            push(corr_send.at[a * ntp + tp_to], corr_recv.at[c], CORR, p * relays + a, tp_to)

    lag = col.astype(F32)
    doc_before = doc_of(first - 1)
    doc_after = doc_of(first + tokens)
    upper = jnp.where(jnp.logical_and(doc_row == doc_col, col >= row), 1.0, 0.0)
    with_before = jnp.where(doc_col == doc_before, 1.0, 0.0)
    with_after = jnp.where(doc_col == doc_after, 1.0, 0.0)

    def quarters(x):
        return fold(x[:GROUP] + x[GROUP:])

    def inside(q, _):
        rate = jnp.broadcast_to(rates[q], square).T
        weight = jnp.broadcast_to(weights[q], square).T
        lead_wide[q] = wide(jnp.exp(-(lag + 1.0) * rate) * (weight * with_before))
        tail_wide[q] = wide(jnp.exp((lag - float(tokens)) * rate) * (weight * with_after))
        terms = jnp.exp(-lag * rate) * weight
        for g in range(TILE_GROUPS):
            taps = jnp.sum(terms[g * MODES : (g + 1) * MODES], axis=0, keepdims=True)
            spread = jnp.broadcast_to(taps, square)
            toeplitz = pltpu.roll(spread, 0, 1, stride=1, stride_axis=0) * upper
            high, low = halves(toeplitz)
            rows = slice(g * GROUP, (g + 1) * GROUP)
            both = slice(2 * g * GROUP, 2 * (g + 1) * GROUP)
            conv_t[q, rows, :] = quarters(
                dot(mix_t[q, both, :], jnp.concatenate([high, low], axis=1))
            )
            dmix_t[q, rows, :] = quarters(
                dot_nt(dconv_t[q, both, :], jnp.concatenate([high, low], axis=0))
            )
        return 0

    lax.fori_loop(0, tiles // 2, inside, 0)

    arrived(state_recv, STATE)
    my_rate = rates[tile_of]
    span = jnp.exp(-float(tokens) * my_rate)
    once = jnp.exp(-my_rate)
    piece = (2 * ROWS, LANES)
    cut_in = [jnp.full(piece, end // tokens, jnp.int32) for end in ends[:3]]
    cut_out = [jnp.full(piece, (end - 1) // tokens, jnp.int32) for end in ends[:3]]
    cut_at = [jnp.full(piece, end, jnp.int32) for end in ends[:3]]
    is_end = iota(piece, 0) < ROWS

    def kept(cuts, at, factor):
        hit = cuts[0] == at
        for cut in cuts[1:]:
            hit = jnp.logical_or(hit, cut == at)
        return jnp.where(hit, 0.0, factor)

    backs = [None] * nctx
    back = jnp.zeros(piece, F32)
    for i in range(nctx - 1, -1, -1):
        backs[i] = back
        back = kept(cut_out, i, span) * back + state_recv[i]
    ahead = jnp.zeros(piece, F32)
    carried = jnp.zeros(piece, F32)
    for i in range(nctx):
        here = state_recv[i]
        carry_send[i] = jnp.where(is_end, ahead, backs[i])
        begun = pltpu.roll(here, ROWS, 0)
        carried = carried + kept(cut_at, i * tokens, once) * (ahead * begun)
        ahead = kept(cut_in, i, span) * ahead + here
    for to in around:
        remote(
            carry_send.at[to], carry_recv.at[c], send_sem.at[CARRY], recv_sem.at[CARRY], to, p
        ).start()
    pltpu.make_async_copy(carry_send.at[c], carry_recv.at[c], recv_sem.at[CARRY]).start()
    carried = jnp.where(is_end, carried, 0.0)
    part_send[...] = jnp.sum(carried, axis=0, keepdims=True)
    for b in range(PIECES):
        block = tile_of * PIECES + b
        push(
            part_send,
            part_recv.at[piece_of],
            PART,
            p * relays + block // ntp,
            lax.rem(block, ntp),
        )

    lax.fori_loop(tiles // 2, tiles, inside, 0)

    loads[5].wait()
    loads[6].wait()
    arrived(corr_recv, CORR)

    def add_corr(i, total):
        return total + corr_recv[i]

    corr = lax.fori_loop(0, nctx, add_corr, jnp.zeros((OWN_GROUPS, LANES), F32))
    own_rate = 1.0 / own_par[0]
    own_rate = jnp.concatenate([own_rate[0:1], own_rate[1:2]] * PIECES, axis=1)
    powers = jnp.exp(-row.astype(F32) * own_rate)
    by_mode = fold(dot(wide(jnp.concatenate([corr] * PIECES, axis=0)), twice(wide(powers))))
    lane = iota((1, LANES), 1)
    grad_row = jnp.where(lax.rem(lane // MODES, OWN_GROUPS) == 0, by_mode[0:1], by_mode[1:2])
    arrived(part_recv, PART)
    for r in range(PIECES):
        grad_row = grad_row + part_recv[r]
    step = LANES // PIECES
    grad_row = jnp.where(lane // step == lax.rem(mine, PIECES), grad_row / seq_len, 0.0)
    whole = grad_row
    for b in range(1, PIECES):
        whole = whole + pltpu.roll(grad_row, b * step, 1)
    grad_res_ref[0:1, :] = whole[:, :MODES]
    grad_res_ref[1:2, :] = pltpu.roll(whole, LANES - MODES, 1)[:, :MODES]

    arrived(carry_recv, CARRY)

    def spread_out(q, rows):
        state = jnp.concatenate(
            [carry_recv[PIECES * q + r, rows, :] for r in range(PIECES)], axis=0
        )
        parts = []
        for half in halves(state):
            zero = jnp.zeros_like(half)
            parts.append(
                jnp.concatenate(
                    [jnp.where(block_of == g, half, zero) for g in range(TILE_GROUPS)], axis=0
                )
            )
        return jnp.concatenate(parts, axis=1)

    outs = (
        (mixed, mixed_hbm),
        (grad_query, grad_query_hbm),
        (grad_key, grad_key_hbm),
        (grad_value, grad_value_hbm),
    )
    stores = []
    for q in range(tiles):
        at = slice(q * LANES, (q + 1) * LANES)
        entered = fold(dot(spread_out(q, slice(0, ROWS)), twice(lead_wide[q])))
        conv = (conv_t[q] + entered).T
        mixed[:, at] = (query[:, at].astype(F32) * conv).astype(BF16)
        grad_query[:, at] = (grad[:, at].astype(F32) * conv).astype(BF16)
        left = fold(dot(spread_out(q, slice(ROWS, 2 * ROWS)), twice(tail_wide[q])))
        dmix = (dmix_t[q] + left).T
        grad_key[:, at] = (dmix * value[:, at].astype(F32)).astype(BF16)
        grad_value[:, at] = (dmix * key[:, at].astype(F32)).astype(BF16)
        for i, (src, dst) in enumerate(outs):
            copy = pltpu.make_async_copy(src.at[:, at], dst.at[:, at], store_sem.at[q, i])
            copy.start()
            stores.append(copy)

    sent(state_send.at[pl.ds(0, nctx - 1)], STATE)
    sent(carry_send.at[pl.ds(0, nctx - 1)], CARRY)

    @pl.when(is_relay)
    def _():
        for _ in range(nctx - 1):
            pltpu.make_async_copy(par_send, par_send, send_sem.at[PAR]).wait()
        sent(corr_send.at[pl.ds(0, nctx - 1)], CORR)

    @pl.when(jnp.logical_not(is_relay))
    def _():
        for k, src in enumerate((time_hbm, res_hbm)):
            pltpu.make_async_copy(src, src, raw_send_sem.at[k]).wait()
        sent(corr_send, CORR)

    to_self = jnp.logical_and(is_relay, mine // PIECES == tile_of)

    @pl.when(to_self)
    def _():
        sent(part_recv.at[pl.ds(0, PIECES - 1)], PART)

    @pl.when(jnp.logical_not(to_self))
    def _():
        sent(part_recv, PART)

    for copy in stores:
        copy.wait()


def copy_kernel(chunks, *refs):
    count = (len(refs) - 1) // 3
    sources, results = refs[:count], refs[count : 2 * count]
    stages, sem = refs[2 * count : 3 * count], refs[-1]
    loads, stores = [], []
    for i in range(count):
        rows = sources[i].shape[0]
        parts = chunks if rows % (16 * chunks) == 0 else 1
        for k in range(parts):
            at = pl.ds(k * (rows // parts), rows // parts)
            src, stage, dst = sources[i].at[at], stages[i].at[at], results[i].at[at]
            loads.append(pltpu.make_async_copy(src, stage, sem.at[0, i, k]))
            stores.append(pltpu.make_async_copy(stage, dst, sem.at[1, i, k]))
    for load in loads:
        load.start()
    for load, store in zip(loads, stores):
        load.wait()
        store.start()
    for store in stores:
        store.wait()


def per_device(nctx, ntp, query, key, value, grad, residues, decay_time, doc_lengths):
    tokens, channels = query.shape
    tiles = channels // LANES
    relays = nctx // ntp
    vmem = pl.BlockSpec(memory_space=pltpu.VMEM)
    hbm = pl.BlockSpec(memory_space=pl.ANY)
    flat = jax.ShapeDtypeStruct((tokens, channels), BF16)
    small = jax.ShapeDtypeStruct(residues.shape, F32)
    piece = pltpu.VMEM((nctx, 2 * ROWS, LANES), F32)
    lags = pltpu.VMEM((nctx, OWN_GROUPS, LANES), F32)
    line = pltpu.VMEM((tiles, 1, LANES), F32)
    outs = pl.pallas_call(
        functools.partial(exchange_kernel, nctx, ntp),
        out_shape=(flat, flat, flat, flat, small),
        in_specs=[hbm] * 7,
        out_specs=(hbm, hbm, hbm, hbm, vmem),
        scratch_shapes=[
            pltpu.SMEM(doc_lengths.shape, jnp.int32),
            *[pltpu.VMEM((tokens, channels), BF16)] * 8,
            pltpu.VMEM((2, ntp, OWN_GROUPS, MODES), F32),
            pltpu.VMEM((2 * tiles // relays, LANES), F32),
            pltpu.VMEM((relays, 2 * tiles // relays, LANES), F32),
            line,
            line,
            pltpu.VMEM((2, OWN_GROUPS, MODES), F32),
            *[pltpu.VMEM((tiles, 2 * LANES, tokens), BF16)] * 2,
            *[pltpu.VMEM((tiles, LANES, 2 * LANES), BF16)] * 2,
            *[pltpu.VMEM((tiles, LANES, LANES), F32)] * 2,
            piece,
            piece,
            piece,
            piece,
            lags,
            lags,
            pltpu.VMEM((1, LANES), F32),
            pltpu.VMEM((PIECES, 1, LANES), F32),
            pltpu.SemaphoreType.DMA((7,)),
            pltpu.SemaphoreType.DMA((tiles, 4)),
            pltpu.SemaphoreType.DMA((2,)),
            pltpu.SemaphoreType.DMA((2, ntp)),
            pltpu.SemaphoreType.DMA((relays,)),
            pltpu.SemaphoreType.DMA((5,)),
            pltpu.SemaphoreType.DMA((5,)),
        ],
        compiler_params=pltpu.CompilerParams(
            collective_id=0, has_side_effects=True, vmem_limit_bytes=64 * 1024 * 1024
        ),
    )(doc_lengths, query, key, value, grad, residues, decay_time)
    chunks = 1
    return tuple(
        pl.pallas_call(
            functools.partial(copy_kernel, chunks),
            out_shape=(flat, flat, flat, flat, small),
            in_specs=[hbm] * 5,
            out_specs=(hbm,) * 5,
            scratch_shapes=[
                *[pltpu.VMEM(flat.shape, BF16)] * 4,
                pltpu.VMEM(small.shape, F32),
                pltpu.SemaphoreType.DMA((2, 5, chunks)),
            ],
            compiler_params=pltpu.CompilerParams(vmem_limit_bytes=64 * 1024 * 1024),
        )(*outs)
    )


def solution(mesh):
    main = P("ctx", "tp")
    owned = P(("ctx", "tp"), None)
    return jax.shard_map(
        functools.partial(per_device, mesh.shape["ctx"], mesh.shape["tp"]),
        mesh=mesh,
        in_specs=(main, main, main, main, owned, owned, P()),
        out_specs=(main, main, main, main, owned),
        check_vma=False,
    )
```

```python
import functools

import jax
import jax.numpy as jnp
from jax import lax
from jax.experimental import pallas as pl
from jax.experimental.pallas import tpu as pltpu
from jax.sharding import PartitionSpec as P

GROUP = 16
MODES = 16
LANES = 128
SUB = 8
TILE_GROUPS = LANES // GROUP
OWN_GROUPS = 2
PIECES = TILE_GROUPS // OWN_GROUPS
SHARES = 4
ROWS = GROUP // SHARES

F32 = jnp.float32
BF16 = jnp.bfloat16
MESH = pl.DeviceIdType.MESH

PAR, STATE, CORR, CARRY, PART = range(5)


def halves(x):
    high = x.astype(BF16)
    return high, (x - high.astype(F32)).astype(BF16)


def wide(x):
    return jnp.concatenate(halves(x), axis=1)


def fold(product):
    return product[:, :LANES] + product[:, LANES:]


def twice(x):
    return jnp.concatenate([x, x], axis=0)


def dot(left, right):
    return jnp.dot(left, right, preferred_element_type=F32)


def dot_nt(left, right):
    return lax.dot_general(left, right, (((1,), (1,)), ((), ())), preferred_element_type=F32)


def iota(shape, dim):
    return lax.broadcasted_iota(jnp.int32, shape, dim)


def stack_halves(x):
    high, low = halves(x)
    parts = []
    for g in range(TILE_GROUPS):
        rows = slice(g * GROUP, (g + 1) * GROUP)
        parts += [high[rows], low[rows]]
    return jnp.concatenate(parts, axis=0)


def grid_of(nctx):
    chips = nctx // 2
    nx = 1
    while nx * nx * 4 <= chips:
        nx *= 2
    return nx, chips // nx


def far_first(n):
    return sorted(range(n), key=lambda d: -min(d, n - d))


def exchange_kernel(
    nctx,
    ntp,
    doc_hbm,
    query_hbm,
    key_hbm,
    value_hbm,
    grad_hbm,
    res_hbm,
    time_hbm,
    mixed,
    grad_query,
    grad_key,
    grad_value,
    grad_res_ref,
    doc_ref,
    query,
    key,
    value,
    grad,
    raw,
    par_send,
    par_recv,
    rates,
    weights,
    own_par,
    mix_t,
    dconv_t,
    mix_turned,
    lead_wide,
    tail_wide,
    conv_t,
    dmix_t,
    state_send,
    state_recv,
    carry_send,
    carry_recv,
    corr_send,
    corr_recv,
    part_send,
    part_recv,
    load_sem,
    raw_send_sem,
    raw_recv_sem,
    par_recv_sem,
    send_sem,
    recv_sem,
):
    tokens, channels = query.shape
    tiles = channels // LANES
    seq_len = tokens * nctx
    relays = nctx // ntp
    relay_tiles = tiles // relays
    nx, ny = grid_of(nctx)
    c = lax.axis_index("ctx")
    p = lax.axis_index("tp")
    plane = c // relays
    is_relay = plane == p
    mine = lax.rem(c, relays) * ntp + p
    share_of = lax.rem(c, SHARES)
    tile_of = c // SHARES
    my_x = c // (2 * ny)
    my_y = lax.rem(c // 2, ny)
    my_core = lax.rem(c, 2)

    def remote(src, dst, send, recv, ctx_to, tp_to):
        return pltpu.make_async_remote_copy(
            src_ref=src,
            dst_ref=dst,
            send_sem=send,
            recv_sem=recv,
            device_id=(ctx_to, tp_to),
            device_id_type=MESH,
        )

    def push(src, dst, kind, ctx_to, tp_to):
        here = jnp.logical_and(ctx_to == c, tp_to == p)

        @pl.when(jnp.logical_not(here))
        def _():
            remote(src, dst, send_sem.at[kind], recv_sem.at[kind], ctx_to, tp_to).start()

        @pl.when(here)
        def _():
            pltpu.make_async_copy(src, dst, recv_sem.at[kind]).start()

    def arrived(ref, kind):
        pltpu.make_async_copy(ref, ref, recv_sem.at[kind]).wait()

    def sent(ref, kind):
        pltpu.make_async_copy(ref, ref, send_sem.at[kind]).wait()

    xs = [lax.rem(my_x + d, nx) * (2 * ny) for d in range(nx)]
    ys = [lax.rem(my_y + d, ny) * 2 for d in range(ny)]
    cores = [my_core, 1 - my_core]
    offsets = [(dx, dy, dk) for dx in range(nx) for dy in range(ny) for dk in range(2)]
    offsets.sort(key=lambda o: -(min(o[0], nx - o[0]) + min(o[1], ny - o[1]) + 0.1 * o[2]))
    around = [xs[dx] + ys[dy] + cores[dk] for dx, dy, dk in offsets if dx or dy or dk]

    barrier = pltpu.get_barrier_semaphore()

    def greet(ctx_to, tp_to):
        pl.semaphore_signal(barrier, inc=1, device_id=(ctx_to, tp_to), device_id_type=MESH)

    @pl.when(is_relay)
    def _():
        for d in far_first(ntp):
            if d:
                greet(c, lax.rem(p + d, ntp))

    for a in range(relays):
        relay = p * relays + a

        @pl.when(relay != c)
        def _():
            greet(relay, p)

    sources = (query_hbm, key_hbm, value_hbm, grad_hbm, doc_hbm, time_hbm, res_hbm)
    targets = (query, key, value, grad, doc_ref, own_par.at[0], own_par.at[1])
    loads = [
        pltpu.make_async_copy(src, dst, load_sem.at[i])
        for i, (src, dst) in enumerate(zip(sources, targets))
    ]
    for i in (4, 1, 2, 0, 3, 5, 6):
        loads[i].start()

    def send_raw():
        pl.semaphore_wait(barrier, 1)
        for k, src in enumerate((time_hbm, res_hbm)):
            remote(
                src, raw.at[k, p], raw_send_sem.at[k], raw_recv_sem.at[k, p], c, plane
            ).start()

    rank = jnp.minimum(p, ntp // 2)
    behind = jnp.where(is_relay, -ntp, jnp.minimum(plane, ntp // 2) - rank)

    @pl.when(jnp.logical_and(jnp.logical_not(is_relay), behind <= 0))
    def _():
        send_raw()

    @pl.when(is_relay)
    def _():
        for k, src in enumerate((time_hbm, res_hbm)):
            pltpu.make_async_copy(src, raw.at[k, p], raw_recv_sem.at[k, p]).start()

    first = c * tokens
    loads[4].wait()
    end0 = doc_ref[0]
    end1 = end0 + doc_ref[1]
    end2 = end1 + doc_ref[2]
    end3 = end2 + doc_ref[3]
    ends = (end0, end1, end2, end3)

    def doc_of(position):
        total = (position >= end0).astype(jnp.int32)
        for end in ends[1:]:
            total = total + (position >= end).astype(jnp.int32)
        return total

    square = (tokens, LANES)
    row = iota(square, 0)
    col = iota(square, 1)
    doc_row = doc_of(first + row)
    doc_col = doc_of(first + col)
    flip_row = tokens - 1 - row
    turned = jnp.where(
        jnp.logical_and(doc_of(first + flip_row) == doc_col, col >= flip_row), 1.0, 0.0
    )
    turn = jnp.where(flip_row == col, 1.0, 0.0).astype(BF16)
    block_of = iota((1, LANES), 1) // GROUP

    for i in range(4):
        loads[i].wait()

    def lanes_of(q):
        return pl.ds(pl.multiple_of(q * LANES, LANES), LANES)

    def prepare(q, _):
        at = lanes_of(q)
        mixture = key[:, at].astype(F32) * value[:, at].astype(F32)
        dconv = grad[:, at].astype(F32) * query[:, at].astype(F32)
        mix_t[q] = stack_halves(mixture.T)
        dconv_t[q] = stack_halves(dconv.T)
        mix_turned[q] = dot(turn, wide(mixture)).astype(BF16)
        return 0

    lax.fori_loop(0, tiles, prepare, 0)

    def correlate(q, _):
        nothing = jnp.zeros((GROUP, LANES), BF16)
        half_groups = TILE_GROUPS // 2
        half_lanes = LANES // 2
        for h in range(2):
            high = mix_turned[q, :, h * half_lanes : (h + 1) * half_lanes]
            low = mix_turned[q, :, LANES + h * half_lanes : LANES + (h + 1) * half_lanes]
            left = jnp.concatenate([high, low, high, low], axis=1)
            for first_group in range(h * half_groups, (h + 1) * half_groups, 2):
                columns = []
                for g in (first_group, first_group + 1):
                    rows = []
                    for section in range(4):
                        at = (2 * g + section // 2) * GROUP
                        taken = dconv_t[q, at : at + GROUP, :]
                        for other in range(h * half_groups, (h + 1) * half_groups):
                            rows.append(taken if other == g else nothing)
                    columns.append(jnp.concatenate(rows, axis=0))
                pairs = dot(left, jnp.concatenate(columns, axis=1))
                for k in range(OWN_GROUPS):
                    lags = pltpu.roll(
                        pairs[:, k * LANES : (k + 1) * LANES] * turned,
                        1,
                        1,
                        stride=1,
                        stride_axis=0,
                    )
                    block = PIECES * q + first_group // OWN_GROUPS
                    corr_send[block, k : k + 1, :] = jnp.sum(lags, axis=0, keepdims=True)
        return 0

    early = jnp.where(behind > 2, tiles, 0)
    lax.fori_loop(0, early, correlate, 0)

    @pl.when(behind > 0)
    def _():
        send_raw()

    my_relay = lax.rem(c, relays)

    @pl.when(is_relay)
    def _():
        for k, src in enumerate((time_hbm, res_hbm)):
            for z in range(ntp):
                pltpu.make_async_copy(src, raw.at[k, z], raw_recv_sem.at[k, z]).wait()
        for t in range(relay_tiles):
            for k in range(2):
                parts = []
                for b in range(PIECES):
                    block = raw[k, t * PIECES + b]
                    parts += [block[0:1], block[1:2]]
                line = jnp.concatenate(parts, axis=1)
                at = 2 * t + k
                par_send[at : at + 1, :] = 1.0 / line if k == 0 else line
        pl.semaphore_wait(barrier, nctx - 1)
        for to in around:
            remote(
                par_send, par_recv.at[my_relay], send_sem.at[PAR], par_recv_sem.at[my_relay], to, p
            ).start()
        pltpu.make_async_copy(par_send, par_recv.at[my_relay], par_recv_sem.at[my_relay]).start()

    lax.fori_loop(early, tiles, correlate, 0)

    pos = iota((SUB, LANES), 0).astype(F32)
    eights = iota((tokens // SUB, LANES), 0).astype(F32) * SUB
    doc_first = doc_of(first)
    doc_last = doc_of(first + tokens - 1)
    at_start = jnp.where(doc_row == doc_first, 1.0, 0.0)
    at_end = jnp.where(doc_row == doc_last, 1.0, 0.0)

    def own_blocks(x):
        out = jnp.zeros((GROUP, LANES), F32)
        for g in range(TILE_GROUPS):
            both = x[2 * g * GROUP : (2 * g + 1) * GROUP] + x[(2 * g + 1) * GROUP : (2 * g + 2) * GROUP]
            out = jnp.where(block_of == g, fold(both), out)
        return out

    for a in range(relays):
        pltpu.make_async_copy(par_recv.at[a], par_recv.at[a], par_recv_sem.at[a]).wait()
        for t in range(relay_tiles):
            rates[a * relay_tiles + t] = par_recv[a, 2 * t : 2 * t + 1, :]
            weights[a * relay_tiles + t] = par_recv[a, 2 * t + 1 : 2 * t + 2, :]

    def states(q):
        rate_row = rates[q]
        tall = jnp.exp(-eights * rate_row)
        short = jnp.exp(-pos * rate_row)
        short_flip = jnp.exp((pos - (SUB - 1.0)) * rate_row)
        steps = tokens // SUB
        decay = jnp.concatenate([short * tall[i : i + 1] for i in range(steps)], axis=0)
        flip = jnp.concatenate(
            [short_flip * tall[steps - 1 - i : steps - i] for i in range(steps)], axis=0
        )
        end_state = own_blocks(dot(mix_t[q], wide(flip * at_end)))
        start_state = own_blocks(dot(dconv_t[q], wide(decay * at_start)))
        for h in range(SHARES):
            j = SHARES * q + h
            state_send[j, 0:ROWS, :] = end_state[h * ROWS : (h + 1) * ROWS, :]
            state_send[j, ROWS:, :] = start_state[h * ROWS : (h + 1) * ROWS, :]
        for h in range(SHARES):
            j = SHARES * q + h
            push(state_send.at[j], state_recv.at[c], STATE, j, p)

    sides = tiles // nx
    for dx in far_first(nx):
        for side in reversed(range(sides)):
            q_x = lax.rem(my_x + dx, nx) * sides
            states(q_x + lax.rem(lax.rem(tile_of, sides) + side, sides))

    for z in far_first(ntp):
        for a in range(relays):
            tp_to = lax.rem(p + z, ntp)
            push(corr_send.at[a * ntp + tp_to], corr_recv.at[c], CORR, p * relays + a, tp_to)

    lag = col.astype(F32)
    doc_before = doc_of(first - 1)
    doc_after = doc_of(first + tokens)
    upper = jnp.where(jnp.logical_and(doc_row == doc_col, col >= row), 1.0, 0.0)
    with_before = jnp.where(doc_col == doc_before, 1.0, 0.0)
    with_after = jnp.where(doc_col == doc_after, 1.0, 0.0)

    def quarters(x):
        return fold(x[:GROUP] + x[GROUP:])

    def inside(q, _):
        rate = jnp.broadcast_to(rates[q], square).T
        weight = jnp.broadcast_to(weights[q], square).T
        lead_wide[q] = wide(jnp.exp(-(lag + 1.0) * rate) * (weight * with_before))
        tail_wide[q] = wide(jnp.exp((lag - float(tokens)) * rate) * (weight * with_after))
        terms = jnp.exp(-lag * rate) * weight
        for g in range(TILE_GROUPS):
            taps = jnp.sum(terms[g * MODES : (g + 1) * MODES], axis=0, keepdims=True)
            spread = jnp.broadcast_to(taps, square)
            toeplitz = pltpu.roll(spread, 0, 1, stride=1, stride_axis=0) * upper
            high, low = halves(toeplitz)
            rows = slice(g * GROUP, (g + 1) * GROUP)
            both = slice(2 * g * GROUP, 2 * (g + 1) * GROUP)
            conv_t[q, rows, :] = quarters(
                dot(mix_t[q, both, :], jnp.concatenate([high, low], axis=1))
            )
            dmix_t[q, rows, :] = quarters(
                dot_nt(dconv_t[q, both, :], jnp.concatenate([high, low], axis=0))
            )
        return 0

    lax.fori_loop(0, tiles // 2, inside, 0)

    arrived(state_recv, STATE)
    my_rate = rates[tile_of]
    span = jnp.exp(-float(tokens) * my_rate)
    once = jnp.exp(-my_rate)
    piece = (2 * ROWS, LANES)
    cut_in = [jnp.full(piece, end // tokens, jnp.int32) for end in ends[:3]]
    cut_out = [jnp.full(piece, (end - 1) // tokens, jnp.int32) for end in ends[:3]]
    cut_at = [jnp.full(piece, end, jnp.int32) for end in ends[:3]]
    is_end = iota(piece, 0) < ROWS

    def kept(cuts, at, factor):
        hit = cuts[0] == at
        for cut in cuts[1:]:
            hit = jnp.logical_or(hit, cut == at)
        return jnp.where(hit, 0.0, factor)

    back = jnp.zeros(piece, F32)
    ahead = jnp.zeros(piece, F32)
    backs, aheads = [None] * nctx, [None] * nctx
    for i in range(nctx):
        j = nctx - 1 - i
        backs[j] = back
        back = kept(cut_out, j, span) * back + state_recv[j]
        aheads[i] = ahead
        ahead = kept(cut_in, i, span) * ahead + state_recv[i]
    carried = jnp.zeros(piece, F32)
    for i in range(nctx):
        carry_send[i] = jnp.where(is_end, aheads[i], backs[i])
        begun = pltpu.roll(state_recv[i], ROWS, 0)
        carried = carried + kept(cut_at, i * tokens, once) * (aheads[i] * begun)
    part_send[...] = jnp.sum(jnp.where(is_end, carried, 0.0), axis=0, keepdims=True)
    for b in range(PIECES):
        block = tile_of * PIECES + b
        push(
            part_send,
            part_recv.at[share_of],
            PART,
            p * relays + block // ntp,
            lax.rem(block, ntp),
        )
    for to in around:
        remote(
            carry_send.at[to], carry_recv.at[c], send_sem.at[CARRY], recv_sem.at[CARRY], to, p
        ).start()
    pltpu.make_async_copy(carry_send.at[c], carry_recv.at[c], recv_sem.at[CARRY]).start()

    lax.fori_loop(tiles // 2, tiles, inside, 0)

    arrived(carry_recv, CARRY)

    def spread_out(q, rows):
        state = jnp.concatenate(
            [carry_recv[SHARES * q + h, rows, :] for h in range(SHARES)], axis=0
        )
        parts = []
        for half in halves(state):
            zero = jnp.zeros_like(half)
            parts.append(
                jnp.concatenate(
                    [jnp.where(block_of == g, half, zero) for g in range(TILE_GROUPS)], axis=0
                )
            )
        return jnp.concatenate(parts, axis=1)

    for q in range(tiles):
        at = slice(q * LANES, (q + 1) * LANES)
        entered = fold(dot(spread_out(q, slice(0, ROWS)), twice(lead_wide[q])))
        conv = (conv_t[q] + entered).T
        mixed[:, at] = (query[:, at].astype(F32) * conv).astype(BF16)
        grad_query[:, at] = (grad[:, at].astype(F32) * conv).astype(BF16)
        left = fold(dot(spread_out(q, slice(ROWS, 2 * ROWS)), twice(tail_wide[q])))
        dmix = (dmix_t[q] + left).T
        grad_key[:, at] = (dmix * value[:, at].astype(F32)).astype(BF16)
        grad_value[:, at] = (dmix * key[:, at].astype(F32)).astype(BF16)

    loads[5].wait()
    loads[6].wait()
    arrived(corr_recv, CORR)

    def add_corr(i, total):
        return total + corr_recv[i]

    corr = lax.fori_loop(0, nctx, add_corr, jnp.zeros((OWN_GROUPS, LANES), F32))
    own_rate = 1.0 / own_par[0]
    own_rate = jnp.concatenate([own_rate[0:1], own_rate[1:2]] * PIECES, axis=1)
    powers = jnp.exp(-row.astype(F32) * own_rate)
    by_mode = fold(dot(wide(jnp.concatenate([corr] * PIECES, axis=0)), twice(wide(powers))))
    lane = iota((1, LANES), 1)
    grad_row = jnp.where(lax.rem(lane // MODES, OWN_GROUPS) == 0, by_mode[0:1], by_mode[1:2])
    arrived(part_recv, PART)
    for h in range(SHARES):
        grad_row = grad_row + part_recv[h]
    step = LANES // PIECES
    grad_row = jnp.where(lane // step == lax.rem(mine, PIECES), grad_row / seq_len, 0.0)
    whole = grad_row
    for b in range(1, PIECES):
        whole = whole + pltpu.roll(grad_row, b * step, 1)
    grad_res_ref[0:1, :] = whole[:, :MODES]
    grad_res_ref[1:2, :] = pltpu.roll(whole, LANES - MODES, 1)[:, :MODES]

    sent(state_send.at[pl.ds(0, nctx - 1)], STATE)
    sent(carry_send.at[pl.ds(0, nctx - 1)], CARRY)
    to_self = jnp.logical_and(is_relay, mine // PIECES == tile_of)

    @pl.when(to_self)
    def _():
        sent(part_recv.at[pl.ds(0, PIECES - 1)], PART)

    @pl.when(jnp.logical_not(to_self))
    def _():
        sent(part_recv, PART)

    @pl.when(is_relay)
    def _():
        for _ in range(nctx - 1):
            pltpu.make_async_copy(par_send, par_send, send_sem.at[PAR]).wait()
        sent(corr_send.at[pl.ds(0, nctx - 1)], CORR)

    @pl.when(jnp.logical_not(is_relay))
    def _():
        for k, src in enumerate((time_hbm, res_hbm)):
            pltpu.make_async_copy(src, src, raw_send_sem.at[k]).wait()
        sent(corr_send, CORR)


def copy_kernel(*refs):
    count = (len(refs) - 1) // 2
    copies = [
        pltpu.make_async_copy(refs[i], refs[count + i], refs[-1].at[i]) for i in range(count)
    ]
    for copy in copies:
        copy.start()
    for copy in copies:
        copy.wait()


def per_device(nctx, ntp, query, key, value, grad, residues, decay_time, doc_lengths):
    tokens, channels = query.shape
    tiles = channels // LANES
    relays = nctx // ntp
    vmem = pl.BlockSpec(memory_space=pltpu.VMEM)
    hbm = pl.BlockSpec(memory_space=pl.ANY)
    flat = jax.ShapeDtypeStruct((tokens, channels), BF16)
    small = jax.ShapeDtypeStruct(residues.shape, F32)
    by_device = pltpu.VMEM((nctx, 2 * ROWS, LANES), F32)
    lags = pltpu.VMEM((nctx, OWN_GROUPS, LANES), F32)
    line = pltpu.VMEM((tiles, 1, LANES), F32)
    arguments = (doc_lengths, query, key, value, grad, residues, decay_time)
    outs = pl.pallas_call(
        functools.partial(exchange_kernel, nctx, ntp),
        out_shape=(*[pltpu.VMEM(flat.shape, BF16)] * 4, pltpu.VMEM(small.shape, F32)),
        in_specs=[hbm] * 7,
        out_specs=(vmem,) * 5,
        scratch_shapes=[
            pltpu.SMEM(doc_lengths.shape, jnp.int32),
            *[pltpu.VMEM((tokens, channels), BF16)] * 4,
            pltpu.VMEM((2, ntp, OWN_GROUPS, MODES), F32),
            pltpu.VMEM((2 * tiles // relays, LANES), F32),
            pltpu.VMEM((relays, 2 * tiles // relays, LANES), F32),
            line,
            line,
            pltpu.VMEM((2, OWN_GROUPS, MODES), F32),
            *[pltpu.VMEM((tiles, 2 * LANES, tokens), BF16)] * 2,
            *[pltpu.VMEM((tiles, LANES, 2 * LANES), BF16)] * 3,
            *[pltpu.VMEM((tiles, LANES, LANES), F32)] * 2,
            *[by_device] * 4,
            lags,
            lags,
            pltpu.VMEM((1, LANES), F32),
            pltpu.VMEM((SHARES, 1, LANES), F32),
            pltpu.SemaphoreType.DMA((7,)),
            pltpu.SemaphoreType.DMA((2,)),
            pltpu.SemaphoreType.DMA((2, ntp)),
            pltpu.SemaphoreType.DMA((relays,)),
            pltpu.SemaphoreType.DMA((5,)),
            pltpu.SemaphoreType.DMA((5,)),
        ],
        compiler_params=pltpu.CompilerParams(
            collective_id=0, has_side_effects=True, vmem_limit_bytes=32 * 1024 * 1024
        ),
    )(*[pltpu.with_memory_space_constraint(x, pltpu.HBM) for x in arguments])
    return tuple(
        pl.pallas_call(
            copy_kernel,
            out_shape=(flat, flat, flat, flat, small),
            in_specs=[hbm] * 5,
            out_specs=(hbm,) * 5,
            scratch_shapes=[pltpu.SemaphoreType.DMA((5,))],
            compiler_params=pltpu.CompilerParams(vmem_limit_bytes=1024 * 1024),
        )(*[pltpu.with_memory_space_constraint(x, pltpu.VMEM) for x in outs])
    )


def solution(mesh):
    main = P("ctx", "tp")
    owned = P(("ctx", "tp"), None)
    return jax.shard_map(
        functools.partial(per_device, mesh.shape["ctx"], mesh.shape["tp"]),
        mesh=mesh,
        in_specs=(main, main, main, main, owned, owned, P()),
        out_specs=(main, main, main, main, owned),
        check_vma=False,
    )
```

```python
import functools

import jax
import jax.numpy as jnp
from jax import lax
from jax.experimental import pallas as pl
from jax.experimental.pallas import tpu as pltpu
from jax.sharding import PartitionSpec as P

GROUP = 16
MODES = 16
LANES = 128
SUB = 8
TILE_GROUPS = LANES // GROUP
OWN_GROUPS = 2
PIECES = TILE_GROUPS // OWN_GROUPS
SHARES = 4
ROWS = GROUP // SHARES

F32 = jnp.float32
BF16 = jnp.bfloat16
MESH = pl.DeviceIdType.MESH

PAR, STATE, CORR, CARRY, PART = range(5)


def halves(x):
    high = x.astype(BF16)
    return high, (x - high.astype(F32)).astype(BF16)


def wide(x):
    return jnp.concatenate(halves(x), axis=1)


def fold(product):
    return product[:, :LANES] + product[:, LANES:]


def twice(x):
    return jnp.concatenate([x, x], axis=0)


def dot(left, right):
    return jnp.dot(left, right, preferred_element_type=F32)


def dot_nt(left, right):
    return lax.dot_general(left, right, (((1,), (1,)), ((), ())), preferred_element_type=F32)


def iota(shape, dim):
    return lax.broadcasted_iota(jnp.int32, shape, dim)


def stack_halves(x):
    high, low = halves(x)
    parts = []
    for g in range(TILE_GROUPS):
        rows = slice(g * GROUP, (g + 1) * GROUP)
        parts += [high[rows], low[rows]]
    return jnp.concatenate(parts, axis=0)


def grid_of(nctx):
    chips = nctx // 2
    nx = 1
    while nx * nx * 4 <= chips:
        nx *= 2
    return nx, chips // nx


def far_first(n):
    return sorted(range(n), key=lambda d: -min(d, n - d))


def scan_places(tiles, nx, ny):
    if (tiles, nx, ny) == (8, 4, 4):
        return (
            ((0, 0), (0, 3)),
            ((2, 0), (1, 3)),
            ((1, 0), (3, 0)),
            ((3, 3), (2, 3)),
            ((0, 1), (0, 2)),
            ((2, 1), (1, 2)),
            ((1, 1), (3, 1)),
            ((3, 2), (2, 2)),
        )
    return tuple(tuple(divmod(2 * q + k, ny) for k in range(2)) for q in range(tiles))


def exchange_kernel(
    nctx,
    ntp,
    doc_hbm,
    query_hbm,
    key_hbm,
    value_hbm,
    grad_hbm,
    res_hbm,
    time_hbm,
    mixed,
    grad_query,
    grad_key,
    grad_value,
    grad_res_ref,
    doc_ref,
    query,
    key,
    value,
    grad,
    raw,
    par_send,
    par_recv,
    rates,
    weights,
    own_par,
    mix_t,
    dconv_t,
    mix_k,
    dconv_k,
    mix_turned,
    lead_wide,
    tail_wide,
    conv_t,
    dmix_t,
    state_send,
    state_recv,
    carry_send,
    carry_recv,
    corr_send,
    corr_recv,
    part_send,
    part_recv,
    load_sem,
    raw_send_sem,
    raw_recv_sem,
    par_recv_sem,
    send_sem,
    recv_sem,
):
    tokens, channels = query.shape
    tiles = channels // LANES
    seq_len = tokens * nctx
    relays = nctx // ntp
    relay_tiles = tiles // relays
    nx, ny = grid_of(nctx)
    c = lax.axis_index("ctx")
    p = lax.axis_index("tp")
    plane = c // relays
    is_relay = plane == p
    mine = lax.rem(c, relays) * ntp + p
    my_x = c // (2 * ny)
    my_y = lax.rem(c // 2, ny)
    my_core = lax.rem(c, 2)

    def remote(src, dst, send, recv, ctx_to, tp_to):
        return pltpu.make_async_remote_copy(
            src_ref=src,
            dst_ref=dst,
            send_sem=send,
            recv_sem=recv,
            device_id=(ctx_to, tp_to),
            device_id_type=MESH,
        )

    def push(src, dst, kind, ctx_to, tp_to):
        here = jnp.logical_and(ctx_to == c, tp_to == p)

        @pl.when(jnp.logical_not(here))
        def _():
            remote(src, dst, send_sem.at[kind], recv_sem.at[kind], ctx_to, tp_to).start()

        @pl.when(here)
        def _():
            pltpu.make_async_copy(src, dst, recv_sem.at[kind]).start()

    def arrived(ref, kind):
        pltpu.make_async_copy(ref, ref, recv_sem.at[kind]).wait()

    def sent(ref, kind):
        pltpu.make_async_copy(ref, ref, send_sem.at[kind]).wait()

    sources = (query_hbm, key_hbm, value_hbm, grad_hbm, doc_hbm, time_hbm, res_hbm)
    targets = (query, key, value, grad, doc_ref, own_par.at[0], own_par.at[1])
    loads = [
        pltpu.make_async_copy(src, dst, load_sem.at[i])
        for i, (src, dst) in enumerate(zip(sources, targets))
    ]
    for i in (5, 6, 4, 1, 2, 0, 3):
        loads[i].start()
    barrier = pltpu.get_barrier_semaphore()

    def greet(ctx_to, tp_to):
        pl.semaphore_signal(barrier, inc=1, device_id=(ctx_to, tp_to), device_id_type=MESH)

    @pl.when(is_relay)
    def _():
        for d in far_first(ntp):
            if d:
                greet(c, lax.rem(p + d, ntp))

    for a in range(relays):
        relay = p * relays + a

        @pl.when(relay != c)
        def _():
            greet(relay, p)

    loads[5].wait()
    loads[6].wait()

    base_x = (p * relays // 2) // ny
    base_y = lax.rem(p * relays // 2, ny)
    places = scan_places(tiles, nx, ny)

    def scanner(q, h):
        dx, dy = places[q][h // 2]
        x, y = lax.rem(base_x + dx, nx), lax.rem(base_y + dy, ny)
        return (x * ny + y) * 2 + h % 2

    tile_of = jnp.int32(0)
    share_of = my_core
    for q in range(tiles):
        for k in range(2):
            hit = scanner(q, 2 * k) == c - my_core
            tile_of = jnp.where(hit, q, tile_of)
            share_of = jnp.where(hit, 2 * k + my_core, share_of)

    xs = [lax.rem(my_x + d, nx) * (2 * ny) for d in range(nx)]
    ys = [lax.rem(my_y + d, ny) * 2 for d in range(ny)]
    cores = [my_core, 1 - my_core]
    offsets = [(dx, dy, dk) for dx in range(nx) for dy in range(ny) for dk in range(2)]
    offsets.sort(key=lambda o: -(min(o[0], nx - o[0]) + min(o[1], ny - o[1]) + 0.1 * o[2]))
    around = [xs[dx] + ys[dy] + cores[dk] for dx, dy, dk in offsets if dx or dy or dk]

    def send_raw():
        pl.semaphore_wait(barrier, 1)
        remote(own_par, raw.at[p], raw_send_sem, raw_recv_sem.at[p], c, plane).start()

    rank = jnp.minimum(p, ntp // 2)
    behind = jnp.where(is_relay, -ntp, jnp.minimum(plane, ntp // 2) - rank)

    @pl.when(jnp.logical_and(jnp.logical_not(is_relay), behind <= 0))
    def _():
        send_raw()

    @pl.when(is_relay)
    def _():
        raw[p] = own_par[...]

    first = c * tokens
    loads[4].wait()
    end0 = doc_ref[0]
    end1 = end0 + doc_ref[1]
    end2 = end1 + doc_ref[2]
    end3 = end2 + doc_ref[3]
    ends = (end0, end1, end2, end3)

    def doc_of(position):
        total = (position >= end0).astype(jnp.int32)
        for end in ends[1:]:
            total = total + (position >= end).astype(jnp.int32)
        return total

    square = (tokens, LANES)
    row = iota(square, 0)
    col = iota(square, 1)
    doc_row = doc_of(first + row)
    doc_col = doc_of(first + col)
    flip_row = tokens - 1 - row
    turned = jnp.where(
        jnp.logical_and(doc_of(first + flip_row) == doc_col, col >= flip_row), 1.0, 0.0
    )
    turn = jnp.where(flip_row == col, 1.0, 0.0).astype(BF16)
    block_of = iota((1, LANES), 1) // GROUP

    for i in range(4):
        loads[i].wait()

    def lanes_of(q):
        return pl.ds(pl.multiple_of(q * LANES, LANES), LANES)

    def prepare(q, _):
        at = lanes_of(q)
        mixture = key[:, at].astype(F32) * value[:, at].astype(F32)
        dconv = grad[:, at].astype(F32) * query[:, at].astype(F32)
        mix_t[q] = stack_halves(mixture.T)
        mix_k[q] = wide(mixture.T)
        dconv_t[q] = stack_halves(dconv.T)
        dconv_k[q] = wide(dconv.T)
        mix_turned[q] = dot(turn, wide(mixture)).astype(BF16)
        return 0

    lax.fori_loop(0, tiles, prepare, 0)

    def correlate(q, _):
        nothing = jnp.zeros((GROUP, LANES), BF16)
        half_groups = TILE_GROUPS // 2
        half_lanes = LANES // 2
        for h in range(2):
            high = mix_turned[q, :, h * half_lanes : (h + 1) * half_lanes]
            low = mix_turned[q, :, LANES + h * half_lanes : LANES + (h + 1) * half_lanes]
            left = jnp.concatenate([high, low, high, low], axis=1)
            for first_group in range(h * half_groups, (h + 1) * half_groups, 2):
                columns = []
                for g in (first_group, first_group + 1):
                    rows = []
                    for section in range(4):
                        at = (2 * g + section // 2) * GROUP
                        taken = dconv_t[q, at : at + GROUP, :]
                        for other in range(h * half_groups, (h + 1) * half_groups):
                            rows.append(taken if other == g else nothing)
                    columns.append(jnp.concatenate(rows, axis=0))
                pairs = dot(left, jnp.concatenate(columns, axis=1))
                for k in range(OWN_GROUPS):
                    lags = pltpu.roll(
                        pairs[:, k * LANES : (k + 1) * LANES] * turned,
                        1,
                        1,
                        stride=1,
                        stride_axis=0,
                    )
                    block = PIECES * q + first_group // OWN_GROUPS
                    corr_send[block, k : k + 1, :] = jnp.sum(lags, axis=0, keepdims=True)
        return 0

    early = jnp.where(behind > 2, tiles, 0)
    lax.fori_loop(0, early, correlate, 0)

    @pl.when(behind > 0)
    def _():
        send_raw()

    my_relay = lax.rem(c, relays)

    @pl.when(is_relay)
    def _():
        for d in range(1, ntp):
            z = lax.rem(p + d, ntp)
            pltpu.make_async_copy(own_par, raw.at[z], raw_recv_sem.at[z]).wait()
        for t in range(relay_tiles):
            for k in range(2):
                parts = []
                for b in range(PIECES):
                    block = raw[t * PIECES + b, k]
                    parts += [block[0:1], block[1:2]]
                line = jnp.concatenate(parts, axis=1)
                at = 2 * t + k
                par_send[at : at + 1, :] = 1.0 / line if k == 0 else line
        pl.semaphore_wait(barrier, nctx - 1)
        for to in around:
            remote(
                par_send, par_recv.at[my_relay], send_sem.at[PAR], par_recv_sem.at[my_relay], to, p
            ).start()
        pltpu.make_async_copy(par_send, par_recv.at[my_relay], par_recv_sem.at[my_relay]).start()

    lax.fori_loop(early, tiles, correlate, 0)

    pos = iota((SUB, LANES), 0).astype(F32)
    eights = iota((tokens // SUB, LANES), 0).astype(F32) * SUB
    doc_first = doc_of(first)
    doc_last = doc_of(first + tokens - 1)
    at_start = jnp.where(doc_row == doc_first, 1.0, 0.0)
    at_end = jnp.where(doc_row == doc_last, 1.0, 0.0)

    def own_blocks(x):
        out = jnp.zeros((GROUP, LANES), F32)
        for g in range(TILE_GROUPS):
            out = jnp.where(block_of == g, fold(x[g * GROUP : (g + 1) * GROUP]), out)
        return out

    for a in range(relays):
        pltpu.make_async_copy(par_recv.at[a], par_recv.at[a], par_recv_sem.at[a]).wait()
        for t in range(relay_tiles):
            rates[a * relay_tiles + t] = par_recv[a, 2 * t : 2 * t + 1, :]
            weights[a * relay_tiles + t] = par_recv[a, 2 * t + 1 : 2 * t + 2, :]

    def states(q):
        rate_row = rates[q]
        tall = jnp.exp(-eights * rate_row)
        short = jnp.exp(-pos * rate_row)
        short_flip = jnp.exp((pos - (SUB - 1.0)) * rate_row)
        steps = tokens // SUB
        decay = jnp.concatenate([short * tall[i : i + 1] for i in range(steps)], axis=0)
        flip = jnp.concatenate(
            [short_flip * tall[steps - 1 - i : steps - i] for i in range(steps)], axis=0
        )
        end_state = own_blocks(dot(mix_k[q], twice(wide(flip * at_end))))
        start_state = own_blocks(dot(dconv_k[q], twice(wide(decay * at_start))))
        for h in range(SHARES):
            to = scanner(q, h)
            state_send[to, 0:ROWS, :] = end_state[h * ROWS : (h + 1) * ROWS, :]
            state_send[to, ROWS:, :] = start_state[h * ROWS : (h + 1) * ROWS, :]

    for q in range(tiles):
        states(q)
    for to in around:
        remote(
            state_send.at[to], state_recv.at[c], send_sem.at[STATE], recv_sem.at[STATE], to, p
        ).start()
    pltpu.make_async_copy(state_send.at[c], state_recv.at[c], recv_sem.at[STATE]).start()

    for z in far_first(ntp):
        for a in range(relays):
            tp_to = lax.rem(p + z, ntp)
            push(corr_send.at[a * ntp + tp_to], corr_recv.at[c], CORR, p * relays + a, tp_to)

    lag = col.astype(F32)
    doc_before = doc_of(first - 1)
    doc_after = doc_of(first + tokens)
    upper = jnp.where(jnp.logical_and(doc_row == doc_col, col >= row), 1.0, 0.0)
    with_before = jnp.where(doc_col == doc_before, 1.0, 0.0)
    with_after = jnp.where(doc_col == doc_after, 1.0, 0.0)

    def quarters(x):
        return fold(x[:GROUP] + x[GROUP:])

    def inside(q, _):
        rate = jnp.broadcast_to(rates[q], square).T
        weight = jnp.broadcast_to(weights[q], square).T
        lead_wide[q] = wide(jnp.exp(-(lag + 1.0) * rate) * (weight * with_before))
        tail_wide[q] = wide(jnp.exp((lag - float(tokens)) * rate) * (weight * with_after))
        terms = jnp.exp(-lag * rate) * weight
        for g in range(TILE_GROUPS):
            taps = jnp.sum(terms[g * MODES : (g + 1) * MODES], axis=0, keepdims=True)
            spread = jnp.broadcast_to(taps, square)
            toeplitz = pltpu.roll(spread, 0, 1, stride=1, stride_axis=0) * upper
            high, low = halves(toeplitz)
            rows = slice(g * GROUP, (g + 1) * GROUP)
            both = slice(2 * g * GROUP, 2 * (g + 1) * GROUP)
            conv_t[q, rows, :] = quarters(
                dot(mix_t[q, both, :], jnp.concatenate([high, low], axis=1))
            )
            dmix_t[q, rows, :] = quarters(
                dot_nt(dconv_t[q, both, :], jnp.concatenate([high, low], axis=0))
            )
        return 0

    lax.fori_loop(0, tiles // 2, inside, 0)

    arrived(state_recv, STATE)
    my_rate = rates[tile_of]
    span = jnp.exp(-float(tokens) * my_rate)
    once = jnp.exp(-my_rate)
    piece = (2 * ROWS, LANES)
    cut_in = [jnp.full(piece, end // tokens, jnp.int32) for end in ends[:3]]
    cut_out = [jnp.full(piece, (end - 1) // tokens, jnp.int32) for end in ends[:3]]
    cut_at = [jnp.full(piece, end, jnp.int32) for end in ends[:3]]
    is_end = iota(piece, 0) < ROWS

    def kept(cuts, at, factor):
        hit = cuts[0] == at
        for cut in cuts[1:]:
            hit = jnp.logical_or(hit, cut == at)
        return jnp.where(hit, 0.0, factor)

    back = jnp.zeros(piece, F32)
    ahead = jnp.zeros(piece, F32)
    backs, aheads = [None] * nctx, [None] * nctx
    for i in range(nctx):
        j = nctx - 1 - i
        backs[j] = back
        back = kept(cut_out, j, span) * back + state_recv[j]
        aheads[i] = ahead
        ahead = kept(cut_in, i, span) * ahead + state_recv[i]
    carried = jnp.zeros(piece, F32)
    for i in range(nctx):
        carry_send[i] = jnp.where(is_end, aheads[i], backs[i])
        begun = pltpu.roll(state_recv[i], ROWS, 0)
        carried = carried + kept(cut_at, i * tokens, once) * (aheads[i] * begun)
    part_send[...] = jnp.sum(jnp.where(is_end, carried, 0.0), axis=0, keepdims=True)
    for b in range(PIECES):
        block = tile_of * PIECES + b
        push(
            part_send,
            part_recv.at[share_of],
            PART,
            p * relays + block // ntp,
            lax.rem(block, ntp),
        )
    for to in around:
        remote(
            carry_send.at[to], carry_recv.at[c], send_sem.at[CARRY], recv_sem.at[CARRY], to, p
        ).start()
    pltpu.make_async_copy(carry_send.at[c], carry_recv.at[c], recv_sem.at[CARRY]).start()

    lax.fori_loop(tiles // 2, tiles, inside, 0)

    arrived(carry_recv, CARRY)

    def spread_out(q, rows):
        state = jnp.concatenate(
            [carry_recv[scanner(q, h), rows, :] for h in range(SHARES)], axis=0
        )
        parts = []
        for half in halves(state):
            zero = jnp.zeros_like(half)
            parts.append(
                jnp.concatenate(
                    [jnp.where(block_of == g, half, zero) for g in range(TILE_GROUPS)], axis=0
                )
            )
        return jnp.concatenate(parts, axis=1)

    for q in range(tiles):
        at = slice(q * LANES, (q + 1) * LANES)
        entered = fold(dot(spread_out(q, slice(0, ROWS)), twice(lead_wide[q])))
        conv = (conv_t[q] + entered).T
        mixed[:, at] = (query[:, at].astype(F32) * conv).astype(BF16)
        grad_query[:, at] = (grad[:, at].astype(F32) * conv).astype(BF16)
        left = fold(dot(spread_out(q, slice(ROWS, 2 * ROWS)), twice(tail_wide[q])))
        dmix = (dmix_t[q] + left).T
        grad_key[:, at] = (dmix * value[:, at].astype(F32)).astype(BF16)
        grad_value[:, at] = (dmix * key[:, at].astype(F32)).astype(BF16)

    arrived(corr_recv, CORR)

    def add_corr(i, total):
        return total + corr_recv[i]

    corr = lax.fori_loop(0, nctx, add_corr, jnp.zeros((OWN_GROUPS, LANES), F32))
    own_rate = 1.0 / own_par[0]
    own_rate = jnp.concatenate([own_rate[0:1], own_rate[1:2]] * PIECES, axis=1)
    powers = jnp.exp(-row.astype(F32) * own_rate)
    by_mode = fold(dot(wide(jnp.concatenate([corr] * PIECES, axis=0)), twice(wide(powers))))
    lane = iota((1, LANES), 1)
    grad_row = jnp.where(lax.rem(lane // MODES, OWN_GROUPS) == 0, by_mode[0:1], by_mode[1:2])
    arrived(part_recv, PART)
    for h in range(SHARES):
        grad_row = grad_row + part_recv[h]
    step = LANES // PIECES
    grad_row = jnp.where(lane // step == lax.rem(mine, PIECES), grad_row / seq_len, 0.0)
    whole = grad_row
    for b in range(1, PIECES):
        whole = whole + pltpu.roll(grad_row, b * step, 1)
    grad_res_ref[0:1, :] = whole[:, :MODES]
    grad_res_ref[1:2, :] = pltpu.roll(whole, LANES - MODES, 1)[:, :MODES]

    sent(state_send.at[pl.ds(0, nctx - 1)], STATE)
    sent(carry_send.at[pl.ds(0, nctx - 1)], CARRY)
    to_self = jnp.logical_and(is_relay, mine // PIECES == tile_of)

    @pl.when(to_self)
    def _():
        sent(part_recv.at[pl.ds(0, PIECES - 1)], PART)

    @pl.when(jnp.logical_not(to_self))
    def _():
        sent(part_recv, PART)

    @pl.when(is_relay)
    def _():
        for _ in range(nctx - 1):
            pltpu.make_async_copy(par_send, par_send, send_sem.at[PAR]).wait()
        sent(corr_send.at[pl.ds(0, nctx - 1)], CORR)

    @pl.when(jnp.logical_not(is_relay))
    def _():
        pltpu.make_async_copy(own_par, own_par, raw_send_sem).wait()
        sent(corr_send, CORR)


def copy_kernel(*refs):
    count = (len(refs) - 1) // 2
    copies = [
        pltpu.make_async_copy(refs[i], refs[count + i], refs[-1].at[i]) for i in range(count)
    ]
    for copy in copies:
        copy.start()
    for copy in copies:
        copy.wait()


def per_device(nctx, ntp, query, key, value, grad, residues, decay_time, doc_lengths):
    tokens, channels = query.shape
    tiles = channels // LANES
    relays = nctx // ntp
    vmem = pl.BlockSpec(memory_space=pltpu.VMEM)
    hbm = pl.BlockSpec(memory_space=pl.ANY)
    flat = jax.ShapeDtypeStruct((tokens, channels), BF16)
    small = jax.ShapeDtypeStruct(residues.shape, F32)
    by_device = pltpu.VMEM((nctx, 2 * ROWS, LANES), F32)
    lags = pltpu.VMEM((nctx, OWN_GROUPS, LANES), F32)
    line = pltpu.VMEM((tiles, 1, LANES), F32)
    arguments = (doc_lengths, query, key, value, grad, residues, decay_time)
    outs = pl.pallas_call(
        functools.partial(exchange_kernel, nctx, ntp),
        out_shape=(*[pltpu.VMEM(flat.shape, BF16)] * 4, pltpu.VMEM(small.shape, F32)),
        in_specs=[hbm] * 7,
        out_specs=(vmem,) * 5,
        scratch_shapes=[
            pltpu.SMEM(doc_lengths.shape, jnp.int32),
            *[pltpu.VMEM((tokens, channels), BF16)] * 4,
            pltpu.VMEM((ntp, 2, OWN_GROUPS, MODES), F32),
            pltpu.VMEM((2 * tiles // relays, LANES), F32),
            pltpu.VMEM((relays, 2 * tiles // relays, LANES), F32),
            line,
            line,
            pltpu.VMEM((2, OWN_GROUPS, MODES), F32),
            *[pltpu.VMEM((tiles, 2 * LANES, tokens), BF16)] * 2,
            *[pltpu.VMEM((tiles, LANES, 2 * LANES), BF16)] * 5,
            *[pltpu.VMEM((tiles, LANES, LANES), F32)] * 2,
            *[by_device] * 4,
            lags,
            lags,
            pltpu.VMEM((1, LANES), F32),
            pltpu.VMEM((SHARES, 1, LANES), F32),
            pltpu.SemaphoreType.DMA((7,)),
            pltpu.SemaphoreType.DMA,
            pltpu.SemaphoreType.DMA((ntp,)),
            pltpu.SemaphoreType.DMA((relays,)),
            pltpu.SemaphoreType.DMA((5,)),
            pltpu.SemaphoreType.DMA((5,)),
        ],
        compiler_params=pltpu.CompilerParams(
            collective_id=0, has_side_effects=True, vmem_limit_bytes=32 * 1024 * 1024
        ),
    )(*[pltpu.with_memory_space_constraint(x, pltpu.HBM) for x in arguments])
    return tuple(
        pl.pallas_call(
            copy_kernel,
            out_shape=(flat, flat, flat, flat, small),
            in_specs=[hbm] * 5,
            out_specs=(hbm,) * 5,
            scratch_shapes=[pltpu.SemaphoreType.DMA((5,))],
            compiler_params=pltpu.CompilerParams(vmem_limit_bytes=1024 * 1024),
        )(*[pltpu.with_memory_space_constraint(x, pltpu.VMEM) for x in outs])
    )


def solution(mesh):
    main = P("ctx", "tp")
    owned = P(("ctx", "tp"), None)
    return jax.shard_map(
        functools.partial(per_device, mesh.shape["ctx"], mesh.shape["tp"]),
        mesh=mesh,
        in_specs=(main, main, main, main, owned, owned, P()),
        out_specs=(main, main, main, main, owned),
        check_vma=False,
    )
```

```python
import functools

import jax
import jax.numpy as jnp
from jax import lax
from jax.experimental import pallas as pl
from jax.experimental.pallas import tpu as pltpu
from jax.sharding import PartitionSpec as P

GROUP = 16
MODES = 16
LANES = 128
SUB = 8
TILE_GROUPS = LANES // GROUP
OWN_GROUPS = 2
PIECES = TILE_GROUPS // OWN_GROUPS
SHARES = 4
ROWS = GROUP // SHARES

F32 = jnp.float32
BF16 = jnp.bfloat16
MESH = pl.DeviceIdType.MESH

PAR, STATE, CORR, CARRY, PART = range(5)


def halves(x):
    high = x.astype(BF16)
    return high, (x - high.astype(F32)).astype(BF16)


def wide(x):
    return jnp.concatenate(halves(x), axis=1)


def fold(product):
    return product[:, :LANES] + product[:, LANES:]


def twice(x):
    return jnp.concatenate([x, x], axis=0)


def dot(left, right):
    return jnp.dot(left, right, preferred_element_type=F32)


def dot_nt(left, right):
    return lax.dot_general(left, right, (((1,), (1,)), ((), ())), preferred_element_type=F32)


def iota(shape, dim):
    return lax.broadcasted_iota(jnp.int32, shape, dim)


def stack_halves(x):
    high, low = halves(x)
    parts = []
    for g in range(TILE_GROUPS):
        rows = slice(g * GROUP, (g + 1) * GROUP)
        parts += [high[rows], low[rows]]
    return jnp.concatenate(parts, axis=0)


def grid_of(nctx):
    chips = nctx // 2
    nx = 1
    while nx * nx * 4 <= chips:
        nx *= 2
    return nx, chips // nx


def far_first(n):
    return sorted(range(n), key=lambda d: -min(d, n - d))


def scan_places(tiles, nx, ny):
    if (tiles, nx, ny) == (8, 4, 4):
        return (
            ((0, 0), (0, 3)),
            ((2, 0), (1, 3)),
            ((1, 0), (3, 0)),
            ((3, 3), (2, 3)),
            ((0, 1), (0, 2)),
            ((2, 1), (1, 2)),
            ((1, 1), (3, 1)),
            ((3, 2), (2, 2)),
        )
    return tuple(tuple(divmod(2 * q + k, ny) for k in range(2)) for q in range(tiles))


def exchange_kernel(
    nctx,
    ntp,
    doc_hbm,
    query_hbm,
    key_hbm,
    value_hbm,
    grad_hbm,
    res_hbm,
    time_hbm,
    mixed,
    grad_query,
    grad_key,
    grad_value,
    grad_res_ref,
    doc_ref,
    query,
    key,
    value,
    grad,
    raw,
    par_send,
    par_recv,
    rates,
    weights,
    own_par,
    mix_t,
    dconv_t,
    mix_k,
    dconv_k,
    mix_turned,
    lead_wide,
    tail_wide,
    conv_t,
    dmix_t,
    state_send,
    state_recv,
    carry_send,
    carry_recv,
    corr_send,
    corr_recv,
    powers_wide,
    part_send,
    part_recv,
    load_sem,
    raw_send_sem,
    raw_recv_sem,
    par_recv_sem,
    send_sem,
    recv_sem,
):
    tokens, channels = query.shape
    tiles = channels // LANES
    seq_len = tokens * nctx
    relays = nctx // ntp
    relay_tiles = tiles // relays
    nx, ny = grid_of(nctx)
    c = lax.axis_index("ctx")
    p = lax.axis_index("tp")
    plane = c // relays
    is_relay = plane == p
    mine = lax.rem(c, relays) * ntp + p
    my_x = c // (2 * ny)
    my_y = lax.rem(c // 2, ny)
    my_core = lax.rem(c, 2)

    def remote(src, dst, send, recv, ctx_to, tp_to):
        return pltpu.make_async_remote_copy(
            src_ref=src,
            dst_ref=dst,
            send_sem=send,
            recv_sem=recv,
            device_id=(ctx_to, tp_to),
            device_id_type=MESH,
        )

    def push(src, dst, kind, ctx_to, tp_to):
        here = jnp.logical_and(ctx_to == c, tp_to == p)

        @pl.when(jnp.logical_not(here))
        def _():
            remote(src, dst, send_sem.at[kind], recv_sem.at[kind], ctx_to, tp_to).start()

        @pl.when(here)
        def _():
            pltpu.make_async_copy(src, dst, recv_sem.at[kind]).start()

    def arrived(ref, kind):
        pltpu.make_async_copy(ref, ref, recv_sem.at[kind]).wait()

    def sent(ref, kind):
        pltpu.make_async_copy(ref, ref, send_sem.at[kind]).wait()

    sources = (query_hbm, key_hbm, value_hbm, grad_hbm, doc_hbm, time_hbm, res_hbm)
    targets = (query, key, value, grad, doc_ref, own_par.at[0], own_par.at[1])
    loads = [
        pltpu.make_async_copy(src, dst, load_sem.at[i])
        for i, (src, dst) in enumerate(zip(sources, targets))
    ]
    for i in (5, 6, 4, 1, 2, 0, 3):
        loads[i].start()
    barrier = pltpu.get_barrier_semaphore()

    def greet(ctx_to, tp_to):
        pl.semaphore_signal(barrier, inc=1, device_id=(ctx_to, tp_to), device_id_type=MESH)

    half = ntp // 2
    hub = jnp.where(plane < 3 * ntp // 4, ntp // 4, 0)
    by_hub = plane >= half
    is_hub = jnp.logical_and(by_hub, p == hub)
    low = jnp.logical_and(by_hub, p < half)

    @pl.when(is_relay)
    def _():
        for d in far_first(ntp):
            if d:
                z = lax.rem(p + d, ntp)

                @pl.when(jnp.logical_not(jnp.logical_and(by_hub, jnp.logical_and(z < half, z != hub))))
                def _():
                    greet(c, z)

    @pl.when(is_hub)
    def _():
        for z in range(half):

            @pl.when(z != hub)
            def _():
                greet(c, z)

    for a in range(relays):
        relay = p * relays + a

        @pl.when(relay != c)
        def _():
            greet(relay, p)


    base_x = (p * relays // 2) // ny
    base_y = lax.rem(p * relays // 2, ny)
    places = scan_places(tiles, nx, ny)

    def scanner(q, h):
        dx, dy = places[q][h // 2]
        x, y = lax.rem(base_x + dx, nx), lax.rem(base_y + dy, ny)
        return (x * ny + y) * 2 + h % 2

    tile_of = jnp.int32(0)
    share_of = my_core
    for q in range(tiles):
        for k in range(2):
            hit = scanner(q, 2 * k) == c - my_core
            tile_of = jnp.where(hit, q, tile_of)
            share_of = jnp.where(hit, 2 * k + my_core, share_of)

    xs = [lax.rem(my_x + d, nx) * (2 * ny) for d in range(nx)]
    ys = [lax.rem(my_y + d, ny) * 2 for d in range(ny)]
    cores = [my_core, 1 - my_core]
    offsets = [(dx, dy, dk) for dx in range(nx) for dy in range(ny) for dk in range(2)]
    offsets.sort(key=lambda o: -(min(o[0], nx - o[0]) + min(o[1], ny - o[1]) + 0.1 * o[2]))
    around = [xs[dx] + ys[dy] + cores[dk] for dx, dy, dk in offsets if dx or dy or dk]

    def send_raw():
        pl.semaphore_wait(barrier, 1)
        remote(own_par, raw.at[p], raw_send_sem, raw_recv_sem.at[p], c, raw_to).start()

    collects = jnp.logical_or(is_relay, is_hub)
    raw_to = jnp.where(low, hub, plane)
    behind = jnp.where(collects, -ntp, jnp.minimum(raw_to, half) - jnp.minimum(p, half))

    @pl.when(jnp.logical_and(jnp.logical_not(collects), behind < 0))
    def _():
        pl.semaphore_wait(barrier, 1)
        for k, src in enumerate((time_hbm, res_hbm)):
            remote(src, raw.at[p, k], raw_send_sem, raw_recv_sem.at[p], c, raw_to).start()

    loads[5].wait()
    loads[6].wait()

    @pl.when(behind == 0)
    def _():
        send_raw()

    @pl.when(collects)
    def _():
        raw[p] = own_par[...]

    first = c * tokens
    loads[4].wait()
    end0 = doc_ref[0]
    end1 = end0 + doc_ref[1]
    end2 = end1 + doc_ref[2]
    end3 = end2 + doc_ref[3]
    ends = (end0, end1, end2, end3)

    def doc_of(position):
        total = (position >= end0).astype(jnp.int32)
        for end in ends[1:]:
            total = total + (position >= end).astype(jnp.int32)
        return total

    square = (tokens, LANES)
    row = iota(square, 0)
    col = iota(square, 1)
    doc_row = doc_of(first + row)
    doc_col = doc_of(first + col)
    flip_row = tokens - 1 - row
    turned = jnp.where(
        jnp.logical_and(doc_of(first + flip_row) == doc_col, col >= flip_row), 1.0, 0.0
    )
    turn = jnp.where(flip_row == col, 1.0, 0.0).astype(BF16)
    block_of = iota((1, LANES), 1) // GROUP

    for i in range(4):
        loads[i].wait()

    def lanes_of(q):
        return pl.ds(pl.multiple_of(q * LANES, LANES), LANES)

    def prepare(q, _):
        at = lanes_of(q)
        mixture = key[:, at].astype(F32) * value[:, at].astype(F32)
        dconv = grad[:, at].astype(F32) * query[:, at].astype(F32)
        mix_t[q] = stack_halves(mixture.T)
        mix_k[q] = wide(mixture.T)
        dconv_t[q] = stack_halves(dconv.T)
        dconv_k[q] = wide(dconv.T)
        mix_turned[q] = dot(turn, wide(mixture)).astype(BF16)
        return 0

    lax.fori_loop(0, tiles, prepare, 0)

    def correlate(q, _):
        nothing = jnp.zeros((GROUP, LANES), BF16)
        half_groups = TILE_GROUPS // 2
        half_lanes = LANES // 2
        for h in range(2):
            high = mix_turned[q, :, h * half_lanes : (h + 1) * half_lanes]
            low = mix_turned[q, :, LANES + h * half_lanes : LANES + (h + 1) * half_lanes]
            left = jnp.concatenate([high, low, high, low], axis=1)
            for first_group in range(h * half_groups, (h + 1) * half_groups, 2):
                columns = []
                for g in (first_group, first_group + 1):
                    rows = []
                    for section in range(4):
                        at = (2 * g + section // 2) * GROUP
                        taken = dconv_t[q, at : at + GROUP, :]
                        for other in range(h * half_groups, (h + 1) * half_groups):
                            rows.append(taken if other == g else nothing)
                    columns.append(jnp.concatenate(rows, axis=0))
                pairs = dot(left, jnp.concatenate(columns, axis=1))
                for k in range(OWN_GROUPS):
                    lags = pltpu.roll(
                        pairs[:, k * LANES : (k + 1) * LANES] * turned,
                        1,
                        1,
                        stride=1,
                        stride_axis=0,
                    )
                    block = PIECES * q + first_group // OWN_GROUPS
                    corr_send[block, k : k + 1, :] = jnp.sum(lags, axis=0, keepdims=True)
        return 0

    early = jnp.where(behind > 2, tiles, 0)
    lax.fori_loop(0, early, correlate, 0)

    @pl.when(behind > 0)
    def _():
        send_raw()

    lower = raw.at[pl.ds(0, half)]

    @pl.when(is_hub)
    def _():
        for z in range(half):

            @pl.when(z != hub)
            def _():
                pltpu.make_async_copy(own_par, raw.at[z], raw_recv_sem.at[z]).wait()

        pl.semaphore_wait(barrier, 1)
        remote(lower, lower, raw_send_sem, raw_recv_sem.at[hub], c, plane).start()

    my_relay = lax.rem(c, relays)

    @pl.when(is_relay)
    def _():
        for z in range(half):

            @pl.when(jnp.logical_not(jnp.logical_or(by_hub, z == p)))
            def _():
                pltpu.make_async_copy(own_par, raw.at[z], raw_recv_sem.at[z]).wait()

        @pl.when(by_hub)
        def _():
            pltpu.make_async_copy(lower, lower, raw_recv_sem.at[hub]).wait()

        for z in range(half, ntp):

            @pl.when(z != p)
            def _():
                pltpu.make_async_copy(own_par, raw.at[z], raw_recv_sem.at[z]).wait()

        for t in range(relay_tiles):
            for k in range(2):
                parts = []
                for b in range(PIECES):
                    block = raw[t * PIECES + b, k]
                    parts += [block[0:1], block[1:2]]
                line = jnp.concatenate(parts, axis=1)
                at = 2 * t + k
                par_send[at : at + 1, :] = 1.0 / line if k == 0 else line
        pl.semaphore_wait(barrier, nctx - 1)
        for to in around:
            remote(
                par_send, par_recv.at[my_relay], send_sem.at[PAR], par_recv_sem.at[my_relay], to, p
            ).start()
        pltpu.make_async_copy(par_send, par_recv.at[my_relay], par_recv_sem.at[my_relay]).start()

    lax.fori_loop(early, tiles, correlate, 0)

    pos = iota((SUB, LANES), 0).astype(F32)
    eights = iota((tokens // SUB, LANES), 0).astype(F32) * SUB
    doc_first = doc_of(first)
    doc_last = doc_of(first + tokens - 1)
    at_start = jnp.where(doc_row == doc_first, 1.0, 0.0)
    at_end = jnp.where(doc_row == doc_last, 1.0, 0.0)

    def own_blocks(x):
        out = jnp.zeros((GROUP, LANES), F32)
        for g in range(TILE_GROUPS):
            out = jnp.where(block_of == g, fold(x[g * GROUP : (g + 1) * GROUP]), out)
        return out

    for a in range(relays):
        pltpu.make_async_copy(par_recv.at[a], par_recv.at[a], par_recv_sem.at[a]).wait()
        for t in range(relay_tiles):
            rates[a * relay_tiles + t] = par_recv[a, 2 * t : 2 * t + 1, :]
            weights[a * relay_tiles + t] = par_recv[a, 2 * t + 1 : 2 * t + 2, :]

    def states(q):
        rate_row = rates[q]
        tall = jnp.exp(-eights * rate_row)
        short = jnp.exp(-pos * rate_row)
        short_flip = jnp.exp((pos - (SUB - 1.0)) * rate_row)
        steps = tokens // SUB
        decay = jnp.concatenate([short * tall[i : i + 1] for i in range(steps)], axis=0)
        flip = jnp.concatenate(
            [short_flip * tall[steps - 1 - i : steps - i] for i in range(steps)], axis=0
        )
        end_state = own_blocks(dot(mix_k[q], twice(wide(flip * at_end))))
        start_state = own_blocks(dot(dconv_k[q], twice(wide(decay * at_start))))
        for h in range(SHARES):
            to = scanner(q, h)
            state_send[to, 0:ROWS, :] = end_state[h * ROWS : (h + 1) * ROWS, :]
            state_send[to, ROWS:, :] = start_state[h * ROWS : (h + 1) * ROWS, :]

    for q in range(tiles):
        states(q)
    for to in around:
        remote(
            state_send.at[to], state_recv.at[c], send_sem.at[STATE], recv_sem.at[STATE], to, p
        ).start()
    pltpu.make_async_copy(state_send.at[c], state_recv.at[c], recv_sem.at[STATE]).start()

    for z in far_first(ntp):
        for a in range(relays):
            tp_to = lax.rem(p + z, ntp)
            push(corr_send.at[a * ntp + tp_to], corr_recv.at[c], CORR, p * relays + a, tp_to)

    lag = col.astype(F32)
    doc_before = doc_of(first - 1)
    doc_after = doc_of(first + tokens)
    upper = jnp.where(jnp.logical_and(doc_row == doc_col, col >= row), 1.0, 0.0)
    with_before = jnp.where(doc_col == doc_before, 1.0, 0.0)
    with_after = jnp.where(doc_col == doc_after, 1.0, 0.0)

    def quarters(x):
        return fold(x[:GROUP] + x[GROUP:])

    def inside(q, _):
        rate = jnp.broadcast_to(rates[q], square).T
        weight = jnp.broadcast_to(weights[q], square).T
        lead_wide[q] = wide(jnp.exp(-(lag + 1.0) * rate) * (weight * with_before))
        tail_wide[q] = wide(jnp.exp((lag - float(tokens)) * rate) * (weight * with_after))
        terms = jnp.exp(-lag * rate) * weight
        for g in range(TILE_GROUPS):
            taps = jnp.sum(terms[g * MODES : (g + 1) * MODES], axis=0, keepdims=True)
            spread = jnp.broadcast_to(taps, square)
            toeplitz = pltpu.roll(spread, 0, 1, stride=1, stride_axis=0) * upper
            high, low = halves(toeplitz)
            rows = slice(g * GROUP, (g + 1) * GROUP)
            both = slice(2 * g * GROUP, 2 * (g + 1) * GROUP)
            conv_t[q, rows, :] = quarters(
                dot(mix_t[q, both, :], jnp.concatenate([high, low], axis=1))
            )
            dmix_t[q, rows, :] = quarters(
                dot_nt(dconv_t[q, both, :], jnp.concatenate([high, low], axis=0))
            )
        return 0

    lax.fori_loop(0, tiles // 2, inside, 0)

    arrived(state_recv, STATE)
    my_rate = rates[tile_of]
    span = jnp.exp(-float(tokens) * my_rate)
    once = jnp.exp(-my_rate)
    piece = (2 * ROWS, LANES)
    cut_in = [jnp.full(piece, end // tokens, jnp.int32) for end in ends[:3]]
    cut_out = [jnp.full(piece, (end - 1) // tokens, jnp.int32) for end in ends[:3]]
    cut_at = [jnp.full(piece, end, jnp.int32) for end in ends[:3]]
    is_end = iota(piece, 0) < ROWS

    def kept(cuts, at, factor):
        hit = cuts[0] == at
        for cut in cuts[1:]:
            hit = jnp.logical_or(hit, cut == at)
        return jnp.where(hit, 0.0, factor)

    back = jnp.zeros(piece, F32)
    ahead = jnp.zeros(piece, F32)
    backs, aheads = [None] * nctx, [None] * nctx
    for i in range(nctx):
        j = nctx - 1 - i
        backs[j] = back
        back = kept(cut_out, j, span) * back + state_recv[j]
        aheads[i] = ahead
        ahead = kept(cut_in, i, span) * ahead + state_recv[i]
    carried = jnp.zeros(piece, F32)
    for i in range(nctx):
        carry_send[i] = jnp.where(is_end, aheads[i], backs[i])
        begun = pltpu.roll(state_recv[i], ROWS, 0)
        carried = carried + kept(cut_at, i * tokens, once) * (aheads[i] * begun)
    part_send[...] = jnp.sum(jnp.where(is_end, carried, 0.0), axis=0, keepdims=True)
    for b in range(PIECES):
        block = tile_of * PIECES + b
        push(
            part_send,
            part_recv.at[share_of],
            PART,
            p * relays + block // ntp,
            lax.rem(block, ntp),
        )
    for to in around:
        remote(
            carry_send.at[to], carry_recv.at[c], send_sem.at[CARRY], recv_sem.at[CARRY], to, p
        ).start()
    pltpu.make_async_copy(carry_send.at[c], carry_recv.at[c], recv_sem.at[CARRY]).start()

    lax.fori_loop(tiles // 2, tiles, inside, 0)

    own_rate = 1.0 / own_par[0]
    own_rate = jnp.concatenate([own_rate[0:1], own_rate[1:2]] * PIECES, axis=1)
    powers = jnp.exp(-row.astype(F32) * own_rate)
    powers_wide[...] = wide(powers)

    arrived(carry_recv, CARRY)

    def spread_out(q, rows):
        state = jnp.concatenate(
            [carry_recv[scanner(q, h), rows, :] for h in range(SHARES)], axis=0
        )
        parts = []
        for half in halves(state):
            zero = jnp.zeros_like(half)
            parts.append(
                jnp.concatenate(
                    [jnp.where(block_of == g, half, zero) for g in range(TILE_GROUPS)], axis=0
                )
            )
        return jnp.concatenate(parts, axis=1)

    for q in range(tiles):
        at = slice(q * LANES, (q + 1) * LANES)
        entered = fold(dot(spread_out(q, slice(0, ROWS)), twice(lead_wide[q])))
        conv = (conv_t[q] + entered).T
        mixed[:, at] = (query[:, at].astype(F32) * conv).astype(BF16)
        grad_query[:, at] = (grad[:, at].astype(F32) * conv).astype(BF16)
        left = fold(dot(spread_out(q, slice(ROWS, 2 * ROWS)), twice(tail_wide[q])))
        dmix = (dmix_t[q] + left).T
        grad_key[:, at] = (dmix * value[:, at].astype(F32)).astype(BF16)
        grad_value[:, at] = (dmix * key[:, at].astype(F32)).astype(BF16)

    arrived(corr_recv, CORR)

    sums = [corr_recv[i] for i in range(nctx)]
    while len(sums) > 1:
        sums = [sums[i] + sums[i + 1] for i in range(0, len(sums), 2)]
    corr = sums[0]
    by_mode = fold(dot(wide(jnp.concatenate([corr] * PIECES, axis=0)), twice(powers_wide[...])))
    lane = iota((1, LANES), 1)
    grad_row = jnp.where(lax.rem(lane // MODES, OWN_GROUPS) == 0, by_mode[0:1], by_mode[1:2])
    arrived(part_recv, PART)
    for h in range(SHARES):
        grad_row = grad_row + part_recv[h]
    step = LANES // PIECES
    grad_row = jnp.where(lane // step == lax.rem(mine, PIECES), grad_row / seq_len, 0.0)
    whole = grad_row
    for b in range(1, PIECES):
        whole = whole + pltpu.roll(grad_row, b * step, 1)
    grad_res_ref[0:1, :] = whole[:, :MODES]
    grad_res_ref[1:2, :] = pltpu.roll(whole, LANES - MODES, 1)[:, :MODES]

    sent(state_send.at[pl.ds(0, nctx - 1)], STATE)
    sent(carry_send.at[pl.ds(0, nctx - 1)], CARRY)
    to_self = jnp.logical_and(is_relay, mine // PIECES == tile_of)

    @pl.when(to_self)
    def _():
        sent(part_recv.at[pl.ds(0, PIECES - 1)], PART)

    @pl.when(jnp.logical_not(to_self))
    def _():
        sent(part_recv, PART)

    @pl.when(is_relay)
    def _():
        for _ in range(nctx - 1):
            pltpu.make_async_copy(par_send, par_send, send_sem.at[PAR]).wait()
        sent(corr_send.at[pl.ds(0, nctx - 1)], CORR)

    @pl.when(jnp.logical_not(is_relay))
    def _():
        sent(corr_send, CORR)

    @pl.when(jnp.logical_not(collects))
    def _():
        pltpu.make_async_copy(own_par, own_par, raw_send_sem).wait()

    @pl.when(is_hub)
    def _():
        pltpu.make_async_copy(lower, lower, raw_send_sem).wait()


def copy_kernel(*refs):
    count = (len(refs) - 1) // 2
    copies = [
        pltpu.make_async_copy(refs[i], refs[count + i], refs[-1].at[i]) for i in range(count)
    ]
    for copy in copies:
        copy.start()
    for copy in copies:
        copy.wait()


def per_device(nctx, ntp, query, key, value, grad, residues, decay_time, doc_lengths):
    tokens, channels = query.shape
    tiles = channels // LANES
    relays = nctx // ntp
    vmem = pl.BlockSpec(memory_space=pltpu.VMEM)
    hbm = pl.BlockSpec(memory_space=pl.ANY)
    flat = jax.ShapeDtypeStruct((tokens, channels), BF16)
    small = jax.ShapeDtypeStruct(residues.shape, F32)
    by_device = pltpu.VMEM((nctx, 2 * ROWS, LANES), F32)
    lags = pltpu.VMEM((nctx, OWN_GROUPS, LANES), F32)
    line = pltpu.VMEM((tiles, 1, LANES), F32)
    arguments = (doc_lengths, query, key, value, grad, residues, decay_time)
    outs = pl.pallas_call(
        functools.partial(exchange_kernel, nctx, ntp),
        out_shape=(*[pltpu.VMEM(flat.shape, BF16)] * 4, pltpu.VMEM(small.shape, F32)),
        in_specs=[hbm] * 7,
        out_specs=(vmem,) * 5,
        scratch_shapes=[
            pltpu.SMEM(doc_lengths.shape, jnp.int32),
            *[pltpu.VMEM((tokens, channels), BF16)] * 4,
            pltpu.VMEM((ntp, 2, OWN_GROUPS, MODES), F32),
            pltpu.VMEM((2 * tiles // relays, LANES), F32),
            pltpu.VMEM((relays, 2 * tiles // relays, LANES), F32),
            line,
            line,
            pltpu.VMEM((2, OWN_GROUPS, MODES), F32),
            *[pltpu.VMEM((tiles, 2 * LANES, tokens), BF16)] * 2,
            *[pltpu.VMEM((tiles, LANES, 2 * LANES), BF16)] * 5,
            *[pltpu.VMEM((tiles, LANES, LANES), F32)] * 2,
            *[by_device] * 4,
            lags,
            lags,
            pltpu.VMEM((tokens, 2 * LANES), BF16),
            pltpu.VMEM((1, LANES), F32),
            pltpu.VMEM((SHARES, 1, LANES), F32),
            pltpu.SemaphoreType.DMA((7,)),
            pltpu.SemaphoreType.DMA,
            pltpu.SemaphoreType.DMA((ntp,)),
            pltpu.SemaphoreType.DMA((relays,)),
            pltpu.SemaphoreType.DMA((5,)),
            pltpu.SemaphoreType.DMA((5,)),
        ],
        compiler_params=pltpu.CompilerParams(
            collective_id=0, has_side_effects=True, vmem_limit_bytes=32 * 1024 * 1024
        ),
    )(*[pltpu.with_memory_space_constraint(x, pltpu.HBM) for x in arguments])
    return tuple(
        pl.pallas_call(
            copy_kernel,
            out_shape=(flat, flat, flat, flat, small),
            in_specs=[hbm] * 5,
            out_specs=(hbm,) * 5,
            scratch_shapes=[pltpu.SemaphoreType.DMA((5,))],
            compiler_params=pltpu.CompilerParams(vmem_limit_bytes=1024 * 1024),
        )(*[pltpu.with_memory_space_constraint(x, pltpu.VMEM) for x in outs])
    )


def solution(mesh):
    main = P("ctx", "tp")
    owned = P(("ctx", "tp"), None)
    return jax.shard_map(
        functools.partial(per_device, mesh.shape["ctx"], mesh.shape["tp"]),
        mesh=mesh,
        in_specs=(main, main, main, main, owned, owned, P()),
        out_specs=(main, main, main, main, owned),
        check_vma=False,
    )
```

```python
import functools

import jax
import jax.numpy as jnp
from jax import lax
from jax.experimental import pallas as pl
from jax.experimental.pallas import tpu as pltpu
from jax.sharding import PartitionSpec as P

GROUP = 16
MODES = 16
LANES = 128
SUB = 8
TILE_GROUPS = LANES // GROUP
OWN_GROUPS = 2
PIECES = TILE_GROUPS // OWN_GROUPS
SHARES = 4
ROWS = GROUP // SHARES

F32 = jnp.float32
BF16 = jnp.bfloat16
MESH = pl.DeviceIdType.MESH

PAR, STATE, CORR, CARRY, PART = range(5)


def halves(x):
    high = x.astype(BF16)
    return high, (x - high.astype(F32)).astype(BF16)


def wide(x):
    return jnp.concatenate(halves(x), axis=1)


def fold(product):
    return product[:, :LANES] + product[:, LANES:]


def twice(x):
    return jnp.concatenate([x, x], axis=0)


def dot(left, right):
    return jnp.dot(left, right, preferred_element_type=F32)


def dot_nt(left, right):
    return lax.dot_general(left, right, (((1,), (1,)), ((), ())), preferred_element_type=F32)


def iota(shape, dim):
    return lax.broadcasted_iota(jnp.int32, shape, dim)


def stack_halves(x):
    high, low = halves(x)
    parts = []
    for g in range(TILE_GROUPS):
        rows = slice(g * GROUP, (g + 1) * GROUP)
        parts += [high[rows], low[rows]]
    return jnp.concatenate(parts, axis=0)


def grid_of(nctx):
    chips = nctx // 2
    nx = 1
    while nx * nx * 4 <= chips:
        nx *= 2
    return nx, chips // nx


def far_first(n):
    return sorted(range(n), key=lambda d: -min(d, n - d))


def scan_places(tiles, nx, ny):
    if (tiles, nx, ny) == (8, 4, 4):
        return (
            ((0, 0), (0, 3)),
            ((2, 0), (1, 3)),
            ((1, 0), (3, 0)),
            ((3, 3), (2, 3)),
            ((0, 1), (0, 2)),
            ((2, 1), (1, 2)),
            ((1, 1), (3, 1)),
            ((3, 2), (2, 2)),
        )
    return tuple(tuple(divmod(2 * q + k, ny) for k in range(2)) for q in range(tiles))


def exchange_kernel(
    nctx,
    ntp,
    doc_hbm,
    query_hbm,
    key_hbm,
    value_hbm,
    grad_hbm,
    res_hbm,
    time_hbm,
    mixed,
    grad_query,
    grad_key,
    grad_value,
    grad_res_ref,
    doc_ref,
    query,
    key,
    value,
    grad,
    raw,
    par_send,
    par_recv,
    rates,
    weights,
    own_par,
    mix_t,
    dconv_t,
    mix_k,
    dconv_k,
    mix_turned,
    lead_wide,
    tail_wide,
    conv_t,
    dmix_t,
    state_send,
    state_recv,
    carry_send,
    carry_recv,
    corr_send,
    corr_recv,
    powers_wide,
    part_send,
    part_recv,
    load_sem,
    raw_send_sem,
    raw_recv_sem,
    par_recv_sem,
    send_sem,
    recv_sem,
):
    tokens, channels = query.shape
    tiles = channels // LANES
    seq_len = tokens * nctx
    relays = nctx // ntp
    relay_tiles = tiles // relays
    nx, ny = grid_of(nctx)
    c = lax.axis_index("ctx")
    p = lax.axis_index("tp")
    plane = c // relays
    is_relay = plane == p
    mine = lax.rem(c, relays) * ntp + p
    my_x = c // (2 * ny)
    my_y = lax.rem(c // 2, ny)
    my_core = lax.rem(c, 2)

    def remote(src, dst, send, recv, ctx_to, tp_to):
        return pltpu.make_async_remote_copy(
            src_ref=src,
            dst_ref=dst,
            send_sem=send,
            recv_sem=recv,
            device_id=(ctx_to, tp_to),
            device_id_type=MESH,
        )

    def push(src, dst, kind, ctx_to, tp_to):
        here = jnp.logical_and(ctx_to == c, tp_to == p)

        @pl.when(jnp.logical_not(here))
        def _():
            remote(src, dst, send_sem.at[kind], recv_sem.at[kind], ctx_to, tp_to).start()

        @pl.when(here)
        def _():
            pltpu.make_async_copy(src, dst, recv_sem.at[kind]).start()

    def arrived(ref, kind):
        pltpu.make_async_copy(ref, ref, recv_sem.at[kind]).wait()

    def sent(ref, kind):
        pltpu.make_async_copy(ref, ref, send_sem.at[kind]).wait()

    barrier = pltpu.get_barrier_semaphore()

    def greet(ctx_to, tp_to):
        pl.semaphore_signal(barrier, inc=1, device_id=(ctx_to, tp_to), device_id_type=MESH)

    half = ntp // 2
    hub = jnp.where(plane == 4, 2, 0)
    by_hub = plane >= half
    is_hub = jnp.logical_and(by_hub, p == hub)
    low = jnp.logical_and(by_hub, p < half)

    @pl.when(is_relay)
    def _():
        for d in far_first(ntp):
            if d:
                z = lax.rem(p + d, ntp)

                @pl.when(jnp.logical_not(jnp.logical_and(by_hub, jnp.logical_and(z < half, z != hub))))
                def _():
                    greet(c, z)

    @pl.when(is_hub)
    def _():
        for z in range(half):

            @pl.when(z != hub)
            def _():
                greet(c, z)

    for a in range(relays):
        relay = p * relays + a

        @pl.when(relay != c)
        def _():
            greet(relay, p)


    collects = jnp.logical_or(is_relay, is_hub)
    raw_to = jnp.where(low, hub, plane)
    behind = jnp.where(collects, -ntp, jnp.minimum(raw_to, half) - jnp.minimum(p, half))

    @pl.when(jnp.logical_and(jnp.logical_not(collects), behind < 0))
    def _():
        pl.semaphore_wait(barrier, 1)
        for k, src in enumerate((time_hbm, res_hbm)):
            remote(src, raw.at[p, k], raw_send_sem, raw_recv_sem.at[p], c, raw_to).start()

    sources = (query_hbm, key_hbm, value_hbm, grad_hbm, doc_hbm, time_hbm, res_hbm)
    targets = (query, key, value, grad, doc_ref, own_par.at[0], own_par.at[1])
    loads = [
        pltpu.make_async_copy(src, dst, load_sem.at[i])
        for i, (src, dst) in enumerate(zip(sources, targets))
    ]
    for i in (5, 6, 4, 1, 2, 0, 3):
        loads[i].start()
    base_x = (p * relays // 2) // ny
    base_y = lax.rem(p * relays // 2, ny)
    places = scan_places(tiles, nx, ny)

    def scanner(q, h):
        dx, dy = places[q][h // 2]
        x, y = lax.rem(base_x + dx, nx), lax.rem(base_y + dy, ny)
        return (x * ny + y) * 2 + h % 2

    tile_of = jnp.int32(0)
    share_of = my_core
    for q in range(tiles):
        for k in range(2):
            hit = scanner(q, 2 * k) == c - my_core
            tile_of = jnp.where(hit, q, tile_of)
            share_of = jnp.where(hit, 2 * k + my_core, share_of)

    xs = [lax.rem(my_x + d, nx) * (2 * ny) for d in range(nx)]
    ys = [lax.rem(my_y + d, ny) * 2 for d in range(ny)]
    cores = [my_core, 1 - my_core]
    offsets = [(dx, dy, dk) for dx in range(nx) for dy in range(ny) for dk in range(2)]
    offsets.sort(key=lambda o: -(min(o[0], nx - o[0]) + min(o[1], ny - o[1]) + 0.1 * o[2]))
    around = [xs[dx] + ys[dy] + cores[dk] for dx, dy, dk in offsets if dx or dy or dk]

    def send_raw():
        pl.semaphore_wait(barrier, 1)
        remote(own_par, raw.at[p], raw_send_sem, raw_recv_sem.at[p], c, raw_to).start()

    loads[5].wait()
    loads[6].wait()

    @pl.when(behind == 0)
    def _():
        send_raw()

    @pl.when(collects)
    def _():
        raw[p] = own_par[...]

    first = c * tokens
    loads[4].wait()
    end0 = doc_ref[0]
    end1 = end0 + doc_ref[1]
    end2 = end1 + doc_ref[2]
    end3 = end2 + doc_ref[3]
    ends = (end0, end1, end2, end3)

    def doc_of(position):
        total = (position >= end0).astype(jnp.int32)
        for end in ends[1:]:
            total = total + (position >= end).astype(jnp.int32)
        return total

    square = (tokens, LANES)
    row = iota(square, 0)
    col = iota(square, 1)
    doc_row = doc_of(first + row)
    doc_col = doc_of(first + col)
    flip_row = tokens - 1 - row
    turned = jnp.where(
        jnp.logical_and(doc_of(first + flip_row) == doc_col, col >= flip_row), 1.0, 0.0
    )
    turn = jnp.where(flip_row == col, 1.0, 0.0).astype(BF16)
    block_of = iota((1, LANES), 1) // GROUP

    for i in range(4):
        loads[i].wait()

    def lanes_of(q):
        return pl.ds(pl.multiple_of(q * LANES, LANES), LANES)

    def prepare(q, _):
        at = lanes_of(q)
        mixture = key[:, at].astype(F32) * value[:, at].astype(F32)
        dconv = grad[:, at].astype(F32) * query[:, at].astype(F32)
        mix_t[q] = stack_halves(mixture.T)
        mix_k[q] = wide(mixture.T)
        dconv_t[q] = stack_halves(dconv.T)
        dconv_k[q] = wide(dconv.T)
        mix_turned[q] = dot(turn, wide(mixture)).astype(BF16)
        return 0

    lax.fori_loop(0, tiles, prepare, 0)

    def correlate(q, _):
        nothing = jnp.zeros((GROUP, LANES), BF16)
        half_groups = TILE_GROUPS // 2
        half_lanes = LANES // 2
        for h in range(2):
            high = mix_turned[q, :, h * half_lanes : (h + 1) * half_lanes]
            low = mix_turned[q, :, LANES + h * half_lanes : LANES + (h + 1) * half_lanes]
            left = jnp.concatenate([high, low, high, low], axis=1)
            for first_group in range(h * half_groups, (h + 1) * half_groups, 2):
                columns = []
                for g in (first_group, first_group + 1):
                    rows = []
                    for section in range(4):
                        at = (2 * g + section // 2) * GROUP
                        taken = dconv_t[q, at : at + GROUP, :]
                        for other in range(h * half_groups, (h + 1) * half_groups):
                            rows.append(taken if other == g else nothing)
                    columns.append(jnp.concatenate(rows, axis=0))
                pairs = dot(left, jnp.concatenate(columns, axis=1))
                for k in range(OWN_GROUPS):
                    lags = pltpu.roll(
                        pairs[:, k * LANES : (k + 1) * LANES] * turned,
                        1,
                        1,
                        stride=1,
                        stride_axis=0,
                    )
                    block = PIECES * q + first_group // OWN_GROUPS
                    corr_send[block, k : k + 1, :] = jnp.sum(lags, axis=0, keepdims=True)
        return 0

    early = jnp.where(behind > 2, tiles, 0)
    lax.fori_loop(0, early, correlate, 0)

    @pl.when(behind > 0)
    def _():
        send_raw()

    lower = raw.at[pl.ds(0, half)]

    @pl.when(is_hub)
    def _():
        for z in range(half):

            @pl.when(z != hub)
            def _():
                pltpu.make_async_copy(own_par, raw.at[z], raw_recv_sem.at[z]).wait()

        pl.semaphore_wait(barrier, 1)
        remote(lower, lower, raw_send_sem, raw_recv_sem.at[hub], c, plane).start()

    my_relay = lax.rem(c, relays)

    @pl.when(is_relay)
    def _():
        for z in range(half):

            @pl.when(jnp.logical_not(jnp.logical_or(by_hub, z == p)))
            def _():
                pltpu.make_async_copy(own_par, raw.at[z], raw_recv_sem.at[z]).wait()

        @pl.when(by_hub)
        def _():
            pltpu.make_async_copy(lower, lower, raw_recv_sem.at[hub]).wait()

        for z in range(half, ntp):

            @pl.when(z != p)
            def _():
                pltpu.make_async_copy(own_par, raw.at[z], raw_recv_sem.at[z]).wait()

        for t in range(relay_tiles):
            for k in range(2):
                parts = []
                for b in range(PIECES):
                    block = raw[t * PIECES + b, k]
                    parts += [block[0:1], block[1:2]]
                line = jnp.concatenate(parts, axis=1)
                at = 2 * t + k
                par_send[at : at + 1, :] = 1.0 / line if k == 0 else line
        pl.semaphore_wait(barrier, nctx - 1)
        for to in around:
            remote(
                par_send, par_recv.at[my_relay], send_sem.at[PAR], par_recv_sem.at[my_relay], to, p
            ).start()
        pltpu.make_async_copy(par_send, par_recv.at[my_relay], par_recv_sem.at[my_relay]).start()

    lax.fori_loop(early, tiles, correlate, 0)

    pos = iota((SUB, LANES), 0).astype(F32)
    eights = iota((tokens // SUB, LANES), 0).astype(F32) * SUB
    doc_first = doc_of(first)
    doc_last = doc_of(first + tokens - 1)
    at_start = jnp.where(doc_row == doc_first, 1.0, 0.0)
    at_end = jnp.where(doc_row == doc_last, 1.0, 0.0)

    def own_blocks(x):
        out = jnp.zeros((GROUP, LANES), F32)
        for g in range(TILE_GROUPS):
            out = jnp.where(block_of == g, fold(x[g * GROUP : (g + 1) * GROUP]), out)
        return out

    for a in range(relays):
        pltpu.make_async_copy(par_recv.at[a], par_recv.at[a], par_recv_sem.at[a]).wait()
        for t in range(relay_tiles):
            rates[a * relay_tiles + t] = par_recv[a, 2 * t : 2 * t + 1, :]
            weights[a * relay_tiles + t] = par_recv[a, 2 * t + 1 : 2 * t + 2, :]

    def states(q):
        rate_row = rates[q]
        tall = jnp.exp(-eights * rate_row)
        short = jnp.exp(-pos * rate_row)
        short_flip = jnp.exp((pos - (SUB - 1.0)) * rate_row)
        steps = tokens // SUB
        decay = jnp.concatenate([short * tall[i : i + 1] for i in range(steps)], axis=0)
        flip = jnp.concatenate(
            [short_flip * tall[steps - 1 - i : steps - i] for i in range(steps)], axis=0
        )
        end_state = own_blocks(dot(mix_k[q], twice(wide(flip * at_end))))
        start_state = own_blocks(dot(dconv_k[q], twice(wide(decay * at_start))))
        for h in range(SHARES):
            to = scanner(q, h)
            state_send[to, 0:ROWS, :] = end_state[h * ROWS : (h + 1) * ROWS, :]
            state_send[to, ROWS:, :] = start_state[h * ROWS : (h + 1) * ROWS, :]

    for q in range(tiles):
        states(q)
    for to in around:
        remote(
            state_send.at[to], state_recv.at[c], send_sem.at[STATE], recv_sem.at[STATE], to, p
        ).start()
    pltpu.make_async_copy(state_send.at[c], state_recv.at[c], recv_sem.at[STATE]).start()

    for z in far_first(ntp):
        for a in range(relays):
            tp_to = lax.rem(p + z, ntp)
            push(corr_send.at[a * ntp + tp_to], corr_recv.at[c], CORR, p * relays + a, tp_to)

    lag = col.astype(F32)
    doc_before = doc_of(first - 1)
    doc_after = doc_of(first + tokens)
    upper = jnp.where(jnp.logical_and(doc_row == doc_col, col >= row), 1.0, 0.0)
    with_before = jnp.where(doc_col == doc_before, 1.0, 0.0)
    with_after = jnp.where(doc_col == doc_after, 1.0, 0.0)

    def quarters(x):
        return fold(x[:GROUP] + x[GROUP:])

    def inside(q, _):
        rate = jnp.broadcast_to(rates[q], square).T
        weight = jnp.broadcast_to(weights[q], square).T
        lead_wide[q] = wide(jnp.exp(-(lag + 1.0) * rate) * (weight * with_before))
        tail_wide[q] = wide(jnp.exp((lag - float(tokens)) * rate) * (weight * with_after))
        terms = jnp.exp(-lag * rate) * weight
        for g in range(TILE_GROUPS):
            taps = jnp.sum(terms[g * MODES : (g + 1) * MODES], axis=0, keepdims=True)
            spread = jnp.broadcast_to(taps, square)
            toeplitz = pltpu.roll(spread, 0, 1, stride=1, stride_axis=0) * upper
            high, low = halves(toeplitz)
            rows = slice(g * GROUP, (g + 1) * GROUP)
            both = slice(2 * g * GROUP, 2 * (g + 1) * GROUP)
            conv_t[q, rows, :] = quarters(
                dot(mix_t[q, both, :], jnp.concatenate([high, low], axis=1))
            )
            dmix_t[q, rows, :] = quarters(
                dot_nt(dconv_t[q, both, :], jnp.concatenate([high, low], axis=0))
            )
        return 0

    lax.fori_loop(0, tiles // 2, inside, 0)

    arrived(state_recv, STATE)
    my_rate = rates[tile_of]
    span = jnp.exp(-float(tokens) * my_rate)
    once = jnp.exp(-my_rate)
    piece = (2 * ROWS, LANES)
    cut_in = [jnp.full(piece, end // tokens, jnp.int32) for end in ends[:3]]
    cut_out = [jnp.full(piece, (end - 1) // tokens, jnp.int32) for end in ends[:3]]
    cut_at = [jnp.full(piece, end, jnp.int32) for end in ends[:3]]
    is_end = iota(piece, 0) < ROWS

    def kept(cuts, at, factor):
        hit = cuts[0] == at
        for cut in cuts[1:]:
            hit = jnp.logical_or(hit, cut == at)
        return jnp.where(hit, 0.0, factor)

    back = jnp.zeros(piece, F32)
    ahead = jnp.zeros(piece, F32)
    backs, aheads = [None] * nctx, [None] * nctx
    for i in range(nctx):
        j = nctx - 1 - i
        backs[j] = back
        back = kept(cut_out, j, span) * back + state_recv[j]
        aheads[i] = ahead
        ahead = kept(cut_in, i, span) * ahead + state_recv[i]
    carried = jnp.zeros(piece, F32)
    for i in range(nctx):
        carry_send[i] = jnp.where(is_end, aheads[i], backs[i])
        begun = pltpu.roll(state_recv[i], ROWS, 0)
        carried = carried + kept(cut_at, i * tokens, once) * (aheads[i] * begun)
    part_send[...] = jnp.sum(jnp.where(is_end, carried, 0.0), axis=0, keepdims=True)
    for b in range(PIECES):
        block = tile_of * PIECES + b
        push(
            part_send,
            part_recv.at[share_of],
            PART,
            p * relays + block // ntp,
            lax.rem(block, ntp),
        )
    for to in range(nctx):

        @pl.when(to != c)
        def _():
            remote(
                carry_send.at[to], carry_recv.at[c], send_sem.at[CARRY], recv_sem.at[CARRY], to, p
            ).start()

    pltpu.make_async_copy(carry_send.at[c], carry_recv.at[c], recv_sem.at[CARRY]).start()

    lax.fori_loop(tiles // 2, tiles, inside, 0)

    own_rate = 1.0 / own_par[0]
    own_rate = jnp.concatenate([own_rate[0:1], own_rate[1:2]] * PIECES, axis=1)
    powers = jnp.exp(-row.astype(F32) * own_rate)
    powers_wide[...] = wide(powers)

    arrived(carry_recv, CARRY)

    def spread_out(q, rows):
        state = jnp.concatenate(
            [carry_recv[scanner(q, h), rows, :] for h in range(SHARES)], axis=0
        )
        parts = []
        for half in halves(state):
            zero = jnp.zeros_like(half)
            parts.append(
                jnp.concatenate(
                    [jnp.where(block_of == g, half, zero) for g in range(TILE_GROUPS)], axis=0
                )
            )
        return jnp.concatenate(parts, axis=1)

    for q in range(tiles):
        at = slice(q * LANES, (q + 1) * LANES)
        entered = fold(dot(spread_out(q, slice(0, ROWS)), twice(lead_wide[q])))
        conv = (conv_t[q] + entered).T
        mixed[:, at] = (query[:, at].astype(F32) * conv).astype(BF16)
        grad_query[:, at] = (grad[:, at].astype(F32) * conv).astype(BF16)
        left = fold(dot(spread_out(q, slice(ROWS, 2 * ROWS)), twice(tail_wide[q])))
        dmix = (dmix_t[q] + left).T
        grad_key[:, at] = (dmix * value[:, at].astype(F32)).astype(BF16)
        grad_value[:, at] = (dmix * key[:, at].astype(F32)).astype(BF16)

    arrived(corr_recv, CORR)

    sums = [corr_recv[i] for i in range(nctx)]
    while len(sums) > 1:
        sums = [sums[i] + sums[i + 1] for i in range(0, len(sums), 2)]
    corr = sums[0]
    by_mode = fold(dot(wide(jnp.concatenate([corr] * PIECES, axis=0)), twice(powers_wide[...])))
    lane = iota((1, LANES), 1)
    grad_row = jnp.where(lax.rem(lane // MODES, OWN_GROUPS) == 0, by_mode[0:1], by_mode[1:2])
    arrived(part_recv, PART)
    for h in range(SHARES):
        grad_row = grad_row + part_recv[h]
    step = LANES // PIECES
    grad_row = jnp.where(lane // step == lax.rem(mine, PIECES), grad_row / seq_len, 0.0)
    whole = grad_row
    for b in range(1, PIECES):
        whole = whole + pltpu.roll(grad_row, b * step, 1)
    grad_res_ref[0:1, :] = whole[:, :MODES]
    grad_res_ref[1:2, :] = pltpu.roll(whole, LANES - MODES, 1)[:, :MODES]

    sent(state_send.at[pl.ds(0, nctx - 1)], STATE)
    sent(carry_send.at[pl.ds(0, nctx - 1)], CARRY)
    to_self = jnp.logical_and(is_relay, mine // PIECES == tile_of)

    @pl.when(to_self)
    def _():
        sent(part_recv.at[pl.ds(0, PIECES - 1)], PART)

    @pl.when(jnp.logical_not(to_self))
    def _():
        sent(part_recv, PART)

    @pl.when(is_relay)
    def _():
        for _ in range(nctx - 1):
            pltpu.make_async_copy(par_send, par_send, send_sem.at[PAR]).wait()
        sent(corr_send.at[pl.ds(0, nctx - 1)], CORR)

    @pl.when(jnp.logical_not(is_relay))
    def _():
        sent(corr_send, CORR)

    @pl.when(jnp.logical_not(collects))
    def _():
        pltpu.make_async_copy(own_par, own_par, raw_send_sem).wait()

    @pl.when(is_hub)
    def _():
        pltpu.make_async_copy(lower, lower, raw_send_sem).wait()


def copy_kernel(*refs):
    count = (len(refs) - 1) // 2
    copies = [
        pltpu.make_async_copy(refs[i], refs[count + i], refs[-1].at[i]) for i in range(count)
    ]
    for copy in copies:
        copy.start()
    for copy in copies:
        copy.wait()


def per_device(nctx, ntp, query, key, value, grad, residues, decay_time, doc_lengths):
    tokens, channels = query.shape
    tiles = channels // LANES
    relays = nctx // ntp
    vmem = pl.BlockSpec(memory_space=pltpu.VMEM)
    hbm = pl.BlockSpec(memory_space=pl.ANY)
    flat = jax.ShapeDtypeStruct((tokens, channels), BF16)
    small = jax.ShapeDtypeStruct(residues.shape, F32)
    by_device = pltpu.VMEM((nctx, 2 * ROWS, LANES), F32)
    lags = pltpu.VMEM((nctx, OWN_GROUPS, LANES), F32)
    line = pltpu.VMEM((tiles, 1, LANES), F32)
    arguments = (doc_lengths, query, key, value, grad, residues, decay_time)
    outs = pl.pallas_call(
        functools.partial(exchange_kernel, nctx, ntp),
        out_shape=(*[pltpu.VMEM(flat.shape, BF16)] * 4, pltpu.VMEM(small.shape, F32)),
        in_specs=[hbm] * 7,
        out_specs=(vmem,) * 5,
        scratch_shapes=[
            pltpu.SMEM(doc_lengths.shape, jnp.int32),
            *[pltpu.VMEM((tokens, channels), BF16)] * 4,
            pltpu.VMEM((ntp, 2, OWN_GROUPS, MODES), F32),
            pltpu.VMEM((2 * tiles // relays, LANES), F32),
            pltpu.VMEM((relays, 2 * tiles // relays, LANES), F32),
            line,
            line,
            pltpu.VMEM((2, OWN_GROUPS, MODES), F32),
            *[pltpu.VMEM((tiles, 2 * LANES, tokens), BF16)] * 2,
            *[pltpu.VMEM((tiles, LANES, 2 * LANES), BF16)] * 5,
            *[pltpu.VMEM((tiles, LANES, LANES), F32)] * 2,
            *[by_device] * 4,
            lags,
            lags,
            pltpu.VMEM((tokens, 2 * LANES), BF16),
            pltpu.VMEM((1, LANES), F32),
            pltpu.VMEM((SHARES, 1, LANES), F32),
            pltpu.SemaphoreType.DMA((7,)),
            pltpu.SemaphoreType.DMA,
            pltpu.SemaphoreType.DMA((ntp,)),
            pltpu.SemaphoreType.DMA((relays,)),
            pltpu.SemaphoreType.DMA((5,)),
            pltpu.SemaphoreType.DMA((5,)),
        ],
        compiler_params=pltpu.CompilerParams(
            collective_id=0, has_side_effects=True, vmem_limit_bytes=32 * 1024 * 1024
        ),
    )(*[pltpu.with_memory_space_constraint(x, pltpu.HBM) for x in arguments])
    return tuple(
        pl.pallas_call(
            copy_kernel,
            out_shape=(flat, flat, flat, flat, small),
            in_specs=[hbm] * 5,
            out_specs=(hbm,) * 5,
            scratch_shapes=[pltpu.SemaphoreType.DMA((5,))],
            compiler_params=pltpu.CompilerParams(vmem_limit_bytes=1024 * 1024),
        )(*[pltpu.with_memory_space_constraint(x, pltpu.VMEM) for x in outs])
    )


def solution(mesh):
    main = P("ctx", "tp")
    owned = P(("ctx", "tp"), None)
    return jax.shard_map(
        functools.partial(per_device, mesh.shape["ctx"], mesh.shape["tp"]),
        mesh=mesh,
        in_specs=(main, main, main, main, owned, owned, P()),
        out_specs=(main, main, main, main, owned),
        check_vma=False,
    )
```

```python
import functools

import jax
import jax.numpy as jnp
from jax import lax
from jax.experimental import pallas as pl
from jax.experimental.pallas import tpu as pltpu
from jax.sharding import PartitionSpec as P

GROUP = 16
MODES = 16
LANES = 128
SUB = 8
TILE_GROUPS = LANES // GROUP
OWN_GROUPS = 2
PIECES = TILE_GROUPS // OWN_GROUPS
SHARES = 4
ROWS = GROUP // SHARES

F32 = jnp.float32
BF16 = jnp.bfloat16
MESH = pl.DeviceIdType.MESH

PAR, STATE, CORR, CARRY, PART = range(5)


def halves(x):
    high = x.astype(BF16)
    return high, (x - high.astype(F32)).astype(BF16)


def wide(x):
    return jnp.concatenate(halves(x), axis=1)


def fold(product):
    return product[:, :LANES] + product[:, LANES:]


def twice(x):
    return jnp.concatenate([x, x], axis=0)


def dot(left, right):
    return jnp.dot(left, right, preferred_element_type=F32)


def dot_nt(left, right):
    return lax.dot_general(left, right, (((1,), (1,)), ((), ())), preferred_element_type=F32)


def iota(shape, dim):
    return lax.broadcasted_iota(jnp.int32, shape, dim)


def stack_halves(x):
    high, low = halves(x)
    parts = []
    for g in range(TILE_GROUPS):
        rows = slice(g * GROUP, (g + 1) * GROUP)
        parts += [high[rows], low[rows]]
    return jnp.concatenate(parts, axis=0)


def grid_of(nctx):
    chips = nctx // 2
    nx = 1
    while nx * nx * 4 <= chips:
        nx *= 2
    return nx, chips // nx


def far_first(n):
    return sorted(range(n), key=lambda d: -min(d, n - d))


def scan_places(tiles, nx, ny):
    if (tiles, nx, ny) == (8, 4, 4):
        return (
            ((0, 0), (0, 3)),
            ((2, 0), (1, 3)),
            ((1, 0), (3, 0)),
            ((3, 3), (2, 3)),
            ((0, 1), (0, 2)),
            ((2, 1), (1, 2)),
            ((1, 1), (3, 1)),
            ((3, 2), (2, 2)),
        )
    return tuple(tuple(divmod(2 * q + k, ny) for k in range(2)) for q in range(tiles))


def exchange_kernel(
    nctx,
    ntp,
    doc_hbm,
    query_hbm,
    key_hbm,
    value_hbm,
    grad_hbm,
    res_hbm,
    time_hbm,
    mixed,
    grad_query,
    grad_key,
    grad_value,
    grad_res_ref,
    doc_ref,
    query,
    key,
    value,
    grad,
    raw,
    par_send,
    par_recv,
    rates,
    weights,
    own_par,
    mix_t,
    dconv_t,
    mix_k,
    dconv_k,
    mix_turned,
    lead_wide,
    tail_wide,
    conv_t,
    dmix_t,
    state_send,
    state_recv,
    carry_send,
    carry_recv,
    corr_send,
    corr_recv,
    powers_wide,
    part_send,
    part_recv,
    load_sem,
    raw_send_sem,
    raw_recv_sem,
    par_recv_sem,
    send_sem,
    recv_sem,
):
    tokens, channels = query.shape
    tiles = channels // LANES
    seq_len = tokens * nctx
    relays = nctx // ntp
    relay_tiles = tiles // relays
    nx, ny = grid_of(nctx)
    c = lax.axis_index("ctx")
    p = lax.axis_index("tp")
    plane = c // relays
    is_relay = plane == p
    mine = lax.rem(c, relays) * ntp + p
    my_x = c // (2 * ny)
    my_y = lax.rem(c // 2, ny)
    my_core = lax.rem(c, 2)

    def remote(src, dst, send, recv, ctx_to, tp_to):
        return pltpu.make_async_remote_copy(
            src_ref=src,
            dst_ref=dst,
            send_sem=send,
            recv_sem=recv,
            device_id=(ctx_to, tp_to),
            device_id_type=MESH,
        )

    def push(src, dst, kind, ctx_to, tp_to):
        here = jnp.logical_and(ctx_to == c, tp_to == p)

        @pl.when(jnp.logical_not(here))
        def _():
            remote(src, dst, send_sem.at[kind], recv_sem.at[kind], ctx_to, tp_to).start()

        @pl.when(here)
        def _():
            pltpu.make_async_copy(src, dst, recv_sem.at[kind]).start()

    def arrived(ref, kind):
        pltpu.make_async_copy(ref, ref, recv_sem.at[kind]).wait()

    def sent(ref, kind):
        pltpu.make_async_copy(ref, ref, send_sem.at[kind]).wait()

    barrier = pltpu.get_barrier_semaphore()

    def greet(ctx_to, tp_to):
        pl.semaphore_signal(barrier, inc=1, device_id=(ctx_to, tp_to), device_id_type=MESH)

    half = ntp // 2
    hub = jnp.where(plane == 4, 2, 0)
    by_hub = plane >= half
    is_hub = jnp.logical_and(by_hub, p == hub)
    low = jnp.logical_and(by_hub, p < half)

    @pl.when(is_relay)
    def _():
        for d in far_first(ntp):
            if d:
                z = lax.rem(p + d, ntp)

                @pl.when(jnp.logical_not(jnp.logical_and(by_hub, jnp.logical_and(z < half, z != hub))))
                def _():
                    greet(c, z)

    @pl.when(is_hub)
    def _():
        for z in range(half):

            @pl.when(z != hub)
            def _():
                greet(c, z)

    for a in range(relays):
        relay = p * relays + a

        @pl.when(relay != c)
        def _():
            greet(relay, p)


    collects = jnp.logical_or(is_relay, is_hub)
    raw_to = jnp.where(low, hub, plane)
    behind = jnp.where(collects, -ntp, jnp.minimum(raw_to, half) - jnp.minimum(p, half))

    @pl.when(jnp.logical_and(jnp.logical_not(collects), behind < 0))
    def _():
        pl.semaphore_wait(barrier, 1)
        for k, src in enumerate((time_hbm, res_hbm)):
            remote(src, raw.at[p, k], raw_send_sem, raw_recv_sem.at[p], c, raw_to).start()

    sources = (query_hbm, key_hbm, value_hbm, grad_hbm, doc_hbm, time_hbm, res_hbm)
    targets = (query, key, value, grad, doc_ref, own_par.at[0], own_par.at[1])
    loads = [
        pltpu.make_async_copy(src, dst, load_sem.at[i])
        for i, (src, dst) in enumerate(zip(sources, targets))
    ]
    for i in (5, 6, 4, 1, 2, 0, 3):
        loads[i].start()
    base_x = (p * relays // 2) // ny
    base_y = lax.rem(p * relays // 2, ny)
    places = scan_places(tiles, nx, ny)

    def scanner(q, h):
        dx, dy = places[q][h // 2]
        x, y = lax.rem(base_x + dx, nx), lax.rem(base_y + dy, ny)
        return (x * ny + y) * 2 + h % 2

    tile_of = jnp.int32(0)
    share_of = my_core
    for q in range(tiles):
        for k in range(2):
            hit = scanner(q, 2 * k) == c - my_core
            tile_of = jnp.where(hit, q, tile_of)
            share_of = jnp.where(hit, 2 * k + my_core, share_of)

    xs = [lax.rem(my_x + d, nx) * (2 * ny) for d in range(nx)]
    ys = [lax.rem(my_y + d, ny) * 2 for d in range(ny)]
    cores = [my_core, 1 - my_core]
    offsets = [(dx, dy, dk) for dx in range(nx) for dy in range(ny) for dk in range(2)]
    offsets.sort(key=lambda o: -(min(o[0], nx - o[0]) + min(o[1], ny - o[1]) + 0.1 * o[2]))
    around = [xs[dx] + ys[dy] + cores[dk] for dx, dy, dk in offsets if dx or dy or dk]

    def send_raw():
        pl.semaphore_wait(barrier, 1)
        remote(own_par, raw.at[p], raw_send_sem, raw_recv_sem.at[p], c, raw_to).start()

    loads[5].wait()
    loads[6].wait()

    @pl.when(behind == 0)
    def _():
        send_raw()

    @pl.when(collects)
    def _():
        raw[p] = own_par[...]

    first = c * tokens
    loads[4].wait()
    end0 = doc_ref[0]
    end1 = end0 + doc_ref[1]
    end2 = end1 + doc_ref[2]
    end3 = end2 + doc_ref[3]
    ends = (end0, end1, end2, end3)

    def doc_of(position):
        total = (position >= end0).astype(jnp.int32)
        for end in ends[1:]:
            total = total + (position >= end).astype(jnp.int32)
        return total

    square = (tokens, LANES)
    row = iota(square, 0)
    col = iota(square, 1)
    doc_row = doc_of(first + row)
    doc_col = doc_of(first + col)
    flip_row = tokens - 1 - row
    turned = jnp.where(
        jnp.logical_and(doc_of(first + flip_row) == doc_col, col >= flip_row), 1.0, 0.0
    )
    turn = jnp.where(flip_row == col, 1.0, 0.0).astype(BF16)
    block_of = iota((1, LANES), 1) // GROUP

    for i in range(4):
        loads[i].wait()

    def lanes_of(q):
        return pl.ds(pl.multiple_of(q * LANES, LANES), LANES)

    def prepare(q, _):
        at = lanes_of(q)
        mixture = key[:, at].astype(F32) * value[:, at].astype(F32)
        dconv = grad[:, at].astype(F32) * query[:, at].astype(F32)
        mix_t[q] = stack_halves(mixture.T)
        mix_k[q] = wide(mixture.T)
        dconv_t[q] = stack_halves(dconv.T)
        dconv_k[q] = wide(dconv.T)
        mix_turned[q] = dot(turn, wide(mixture)).astype(BF16)
        return 0

    lax.fori_loop(0, tiles, prepare, 0)

    def correlate(q, _):
        nothing = jnp.zeros((GROUP, LANES), BF16)
        half_groups = TILE_GROUPS // 2
        half_lanes = LANES // 2
        for h in range(2):
            high = mix_turned[q, :, h * half_lanes : (h + 1) * half_lanes]
            low = mix_turned[q, :, LANES + h * half_lanes : LANES + (h + 1) * half_lanes]
            left = jnp.concatenate([high, low, high, low], axis=1)
            for first_group in range(h * half_groups, (h + 1) * half_groups, 2):
                columns = []
                for g in (first_group, first_group + 1):
                    rows = []
                    for section in range(4):
                        at = (2 * g + section // 2) * GROUP
                        taken = dconv_t[q, at : at + GROUP, :]
                        for other in range(h * half_groups, (h + 1) * half_groups):
                            rows.append(taken if other == g else nothing)
                    columns.append(jnp.concatenate(rows, axis=0))
                pairs = dot(left, jnp.concatenate(columns, axis=1))
                for k in range(OWN_GROUPS):
                    lags = pltpu.roll(
                        pairs[:, k * LANES : (k + 1) * LANES] * turned,
                        1,
                        1,
                        stride=1,
                        stride_axis=0,
                    )
                    block = PIECES * q + first_group // OWN_GROUPS
                    corr_send[block, k : k + 1, :] = jnp.sum(lags, axis=0, keepdims=True)
        return 0

    early = jnp.where(behind > 2, tiles, 0)
    lax.fori_loop(0, early, correlate, 0)

    @pl.when(behind > 0)
    def _():
        send_raw()

    lower = raw.at[pl.ds(0, half)]

    @pl.when(is_hub)
    def _():
        for z in range(half):

            @pl.when(z != hub)
            def _():
                pltpu.make_async_copy(own_par, raw.at[z], raw_recv_sem.at[z]).wait()

        pl.semaphore_wait(barrier, 1)
        remote(lower, lower, raw_send_sem, raw_recv_sem.at[hub], c, plane).start()

    my_relay = lax.rem(c, relays)

    @pl.when(is_relay)
    def _():
        for z in range(half):

            @pl.when(jnp.logical_not(jnp.logical_or(by_hub, z == p)))
            def _():
                pltpu.make_async_copy(own_par, raw.at[z], raw_recv_sem.at[z]).wait()

        @pl.when(by_hub)
        def _():
            pltpu.make_async_copy(lower, lower, raw_recv_sem.at[hub]).wait()

        for z in range(half, ntp):

            @pl.when(z != p)
            def _():
                pltpu.make_async_copy(own_par, raw.at[z], raw_recv_sem.at[z]).wait()

        for t in range(relay_tiles):
            for k in range(2):
                parts = []
                for b in range(PIECES):
                    block = raw[t * PIECES + b, k]
                    parts += [block[0:1], block[1:2]]
                line = jnp.concatenate(parts, axis=1)
                at = 2 * t + k
                par_send[at : at + 1, :] = 1.0 / line if k == 0 else line
        pl.semaphore_wait(barrier, nctx - 1)
        for to in around:
            remote(
                par_send, par_recv.at[my_relay], send_sem.at[PAR], par_recv_sem.at[my_relay], to, p
            ).start()
        pltpu.make_async_copy(par_send, par_recv.at[my_relay], par_recv_sem.at[my_relay]).start()

    lax.fori_loop(early, tiles, correlate, 0)

    pos = iota((SUB, LANES), 0).astype(F32)
    eights = iota((tokens // SUB, LANES), 0).astype(F32) * SUB
    doc_first = doc_of(first)
    doc_last = doc_of(first + tokens - 1)
    at_start = jnp.where(doc_row == doc_first, 1.0, 0.0)
    at_end = jnp.where(doc_row == doc_last, 1.0, 0.0)

    def own_blocks(x):
        out = jnp.zeros((GROUP, LANES), F32)
        for g in range(TILE_GROUPS):
            out = jnp.where(block_of == g, fold(x[g * GROUP : (g + 1) * GROUP]), out)
        return out

    for a in range(relays):
        pltpu.make_async_copy(par_recv.at[a], par_recv.at[a], par_recv_sem.at[a]).wait()
        for t in range(relay_tiles):
            rates[a * relay_tiles + t] = par_recv[a, 2 * t : 2 * t + 1, :]
            weights[a * relay_tiles + t] = par_recv[a, 2 * t + 1 : 2 * t + 2, :]

    def states(q):
        rate_row = rates[q]
        tall = jnp.exp(-eights * rate_row)
        short = jnp.exp(-pos * rate_row)
        short_flip = jnp.exp((pos - (SUB - 1.0)) * rate_row)
        steps = tokens // SUB
        decay = jnp.concatenate([short * tall[i : i + 1] for i in range(steps)], axis=0)
        flip = jnp.concatenate(
            [short_flip * tall[steps - 1 - i : steps - i] for i in range(steps)], axis=0
        )
        end_state = own_blocks(dot(mix_k[q], twice(wide(flip * at_end))))
        start_state = own_blocks(dot(dconv_k[q], twice(wide(decay * at_start))))
        for h in range(SHARES):
            to = scanner(q, h)
            state_send[to, 0:ROWS, :] = end_state[h * ROWS : (h + 1) * ROWS, :]
            state_send[to, ROWS:, :] = start_state[h * ROWS : (h + 1) * ROWS, :]

    for q in range(tiles):
        states(q)
    for to in around:
        remote(
            state_send.at[to], state_recv.at[c], send_sem.at[STATE], recv_sem.at[STATE], to, p
        ).start()
    pltpu.make_async_copy(state_send.at[c], state_recv.at[c], recv_sem.at[STATE]).start()

    for z in far_first(ntp):
        for a in range(relays):
            tp_to = lax.rem(p + z, ntp)
            push(corr_send.at[a * ntp + tp_to], corr_recv.at[c], CORR, p * relays + a, tp_to)

    lag = col.astype(F32)
    doc_before = doc_of(first - 1)
    doc_after = doc_of(first + tokens)
    upper = jnp.where(jnp.logical_and(doc_row == doc_col, col >= row), 1.0, 0.0)
    with_before = jnp.where(doc_col == doc_before, 1.0, 0.0)
    with_after = jnp.where(doc_col == doc_after, 1.0, 0.0)

    def quarters(x):
        return fold(x[:GROUP] + x[GROUP:])

    def inside(q, _):
        rate = jnp.broadcast_to(rates[q], square).T
        weight = jnp.broadcast_to(weights[q], square).T
        lead_wide[q] = wide(jnp.exp(-(lag + 1.0) * rate) * (weight * with_before))
        tail_wide[q] = wide(jnp.exp((lag - float(tokens)) * rate) * (weight * with_after))
        terms = jnp.exp(-lag * rate) * weight
        for g in range(TILE_GROUPS):
            taps = jnp.sum(terms[g * MODES : (g + 1) * MODES], axis=0, keepdims=True)
            spread = jnp.broadcast_to(taps, square)
            toeplitz = pltpu.roll(spread, 0, 1, stride=1, stride_axis=0) * upper
            high, low = halves(toeplitz)
            rows = slice(g * GROUP, (g + 1) * GROUP)
            both = slice(2 * g * GROUP, 2 * (g + 1) * GROUP)
            conv_t[q, rows, :] = quarters(
                dot(mix_t[q, both, :], jnp.concatenate([high, low], axis=1))
            )
            dmix_t[q, rows, :] = quarters(
                dot_nt(dconv_t[q, both, :], jnp.concatenate([high, low], axis=0))
            )
        return 0

    lax.fori_loop(0, tiles // 2, inside, 0)

    arrived(state_recv, STATE)
    my_rate = rates[tile_of]
    span = jnp.exp(-float(tokens) * my_rate)
    once = jnp.exp(-my_rate)
    piece = (2 * ROWS, LANES)
    cut_in = [jnp.full(piece, end // tokens, jnp.int32) for end in ends[:3]]
    cut_out = [jnp.full(piece, (end - 1) // tokens, jnp.int32) for end in ends[:3]]
    cut_at = [jnp.full(piece, end, jnp.int32) for end in ends[:3]]
    is_end = iota(piece, 0) < ROWS

    def kept(cuts, at, factor):
        hit = cuts[0] == at
        for cut in cuts[1:]:
            hit = jnp.logical_or(hit, cut == at)
        return jnp.where(hit, 0.0, factor)

    back = jnp.zeros(piece, F32)
    ahead = jnp.zeros(piece, F32)
    backs, aheads = [None] * nctx, [None] * nctx
    for i in range(nctx):
        j = nctx - 1 - i
        backs[j] = back
        back = kept(cut_out, j, span) * back + state_recv[j]
        aheads[i] = ahead
        ahead = kept(cut_in, i, span) * ahead + state_recv[i]
    carried = jnp.zeros(piece, F32)
    for i in range(nctx):
        carry_send[i] = jnp.where(is_end, aheads[i], backs[i])
        begun = pltpu.roll(state_recv[i], ROWS, 0)
        carried = carried + kept(cut_at, i * tokens, once) * (aheads[i] * begun)
    part_send[...] = jnp.sum(jnp.where(is_end, carried, 0.0), axis=0, keepdims=True)
    for b in range(PIECES):
        block = tile_of * PIECES + b
        push(
            part_send,
            part_recv.at[share_of],
            PART,
            p * relays + block // ntp,
            lax.rem(block, ntp),
        )
    for i in range(nctx - 1):
        to = jnp.where(c <= i, i + 1, i)
        remote(
            carry_send.at[to], carry_recv.at[c], send_sem.at[CARRY], recv_sem.at[CARRY], to, p
        ).start()
    pltpu.make_async_copy(carry_send.at[c], carry_recv.at[c], recv_sem.at[CARRY]).start()

    lax.fori_loop(tiles // 2, tiles, inside, 0)

    own_rate = 1.0 / own_par[0]
    own_rate = jnp.concatenate([own_rate[0:1], own_rate[1:2]] * PIECES, axis=1)
    powers = jnp.exp(-row.astype(F32) * own_rate)
    powers_wide[...] = wide(powers)

    arrived(carry_recv, CARRY)

    def spread_out(q, rows):
        state = jnp.concatenate(
            [carry_recv[scanner(q, h), rows, :] for h in range(SHARES)], axis=0
        )
        parts = []
        for half in halves(state):
            zero = jnp.zeros_like(half)
            parts.append(
                jnp.concatenate(
                    [jnp.where(block_of == g, half, zero) for g in range(TILE_GROUPS)], axis=0
                )
            )
        return jnp.concatenate(parts, axis=1)

    for q in range(tiles):
        at = slice(q * LANES, (q + 1) * LANES)
        entered = fold(dot(spread_out(q, slice(0, ROWS)), twice(lead_wide[q])))
        conv = (conv_t[q] + entered).T
        mixed[:, at] = (query[:, at].astype(F32) * conv).astype(BF16)
        grad_query[:, at] = (grad[:, at].astype(F32) * conv).astype(BF16)
        left = fold(dot(spread_out(q, slice(ROWS, 2 * ROWS)), twice(tail_wide[q])))
        dmix = (dmix_t[q] + left).T
        grad_key[:, at] = (dmix * value[:, at].astype(F32)).astype(BF16)
        grad_value[:, at] = (dmix * key[:, at].astype(F32)).astype(BF16)

    arrived(corr_recv, CORR)

    sums = [corr_recv[i] for i in range(nctx)]
    while len(sums) > 1:
        sums = [sums[i] + sums[i + 1] for i in range(0, len(sums), 2)]
    corr = sums[0]
    by_mode = fold(dot(wide(jnp.concatenate([corr] * PIECES, axis=0)), twice(powers_wide[...])))
    lane = iota((1, LANES), 1)
    grad_row = jnp.where(lax.rem(lane // MODES, OWN_GROUPS) == 0, by_mode[0:1], by_mode[1:2])
    arrived(part_recv, PART)
    for h in range(SHARES):
        grad_row = grad_row + part_recv[h]
    step = LANES // PIECES
    grad_row = jnp.where(lane // step == lax.rem(mine, PIECES), grad_row / seq_len, 0.0)
    whole = grad_row
    for b in range(1, PIECES):
        whole = whole + pltpu.roll(grad_row, b * step, 1)
    grad_res_ref[0:1, :] = whole[:, :MODES]
    grad_res_ref[1:2, :] = pltpu.roll(whole, LANES - MODES, 1)[:, :MODES]

    sent(state_send.at[pl.ds(0, nctx - 1)], STATE)
    sent(carry_send.at[pl.ds(0, nctx - 1)], CARRY)
    to_self = jnp.logical_and(is_relay, mine // PIECES == tile_of)

    @pl.when(to_self)
    def _():
        sent(part_recv.at[pl.ds(0, PIECES - 1)], PART)

    @pl.when(jnp.logical_not(to_self))
    def _():
        sent(part_recv, PART)

    @pl.when(is_relay)
    def _():
        for _ in range(nctx - 1):
            pltpu.make_async_copy(par_send, par_send, send_sem.at[PAR]).wait()
        sent(corr_send.at[pl.ds(0, nctx - 1)], CORR)

    @pl.when(jnp.logical_not(is_relay))
    def _():
        sent(corr_send, CORR)

    @pl.when(jnp.logical_not(collects))
    def _():
        pltpu.make_async_copy(own_par, own_par, raw_send_sem).wait()

    @pl.when(is_hub)
    def _():
        pltpu.make_async_copy(lower, lower, raw_send_sem).wait()


def copy_kernel(*refs):
    count = (len(refs) - 1) // 2
    copies = [
        pltpu.make_async_copy(refs[i], refs[count + i], refs[-1].at[i]) for i in range(count)
    ]
    for copy in copies:
        copy.start()
    for copy in copies:
        copy.wait()


def per_device(nctx, ntp, query, key, value, grad, residues, decay_time, doc_lengths):
    tokens, channels = query.shape
    tiles = channels // LANES
    relays = nctx // ntp
    vmem = pl.BlockSpec(memory_space=pltpu.VMEM)
    hbm = pl.BlockSpec(memory_space=pl.ANY)
    flat = jax.ShapeDtypeStruct((tokens, channels), BF16)
    small = jax.ShapeDtypeStruct(residues.shape, F32)
    by_device = pltpu.VMEM((nctx, 2 * ROWS, LANES), F32)
    lags = pltpu.VMEM((nctx, OWN_GROUPS, LANES), F32)
    line = pltpu.VMEM((tiles, 1, LANES), F32)
    arguments = (doc_lengths, query, key, value, grad, residues, decay_time)
    outs = pl.pallas_call(
        functools.partial(exchange_kernel, nctx, ntp),
        out_shape=(*[pltpu.VMEM(flat.shape, BF16)] * 4, pltpu.VMEM(small.shape, F32)),
        in_specs=[hbm] * 7,
        out_specs=(vmem,) * 5,
        scratch_shapes=[
            pltpu.SMEM(doc_lengths.shape, jnp.int32),
            *[pltpu.VMEM((tokens, channels), BF16)] * 4,
            pltpu.VMEM((ntp, 2, OWN_GROUPS, MODES), F32),
            pltpu.VMEM((2 * tiles // relays, LANES), F32),
            pltpu.VMEM((relays, 2 * tiles // relays, LANES), F32),
            line,
            line,
            pltpu.VMEM((2, OWN_GROUPS, MODES), F32),
            *[pltpu.VMEM((tiles, 2 * LANES, tokens), BF16)] * 2,
            *[pltpu.VMEM((tiles, LANES, 2 * LANES), BF16)] * 5,
            *[pltpu.VMEM((tiles, LANES, LANES), F32)] * 2,
            *[by_device] * 4,
            lags,
            lags,
            pltpu.VMEM((tokens, 2 * LANES), BF16),
            pltpu.VMEM((1, LANES), F32),
            pltpu.VMEM((SHARES, 1, LANES), F32),
            pltpu.SemaphoreType.DMA((7,)),
            pltpu.SemaphoreType.DMA,
            pltpu.SemaphoreType.DMA((ntp,)),
            pltpu.SemaphoreType.DMA((relays,)),
            pltpu.SemaphoreType.DMA((5,)),
            pltpu.SemaphoreType.DMA((5,)),
        ],
        compiler_params=pltpu.CompilerParams(
            collective_id=0, has_side_effects=True, vmem_limit_bytes=32 * 1024 * 1024
        ),
    )(*[pltpu.with_memory_space_constraint(x, pltpu.HBM) for x in arguments])
    return tuple(
        pl.pallas_call(
            copy_kernel,
            out_shape=(flat, flat, flat, flat, small),
            in_specs=[hbm] * 5,
            out_specs=(hbm,) * 5,
            scratch_shapes=[pltpu.SemaphoreType.DMA((5,))],
            compiler_params=pltpu.CompilerParams(vmem_limit_bytes=1024 * 1024),
        )(*[pltpu.with_memory_space_constraint(x, pltpu.VMEM) for x in outs])
    )


def solution(mesh):
    main = P("ctx", "tp")
    owned = P(("ctx", "tp"), None)
    return jax.shard_map(
        functools.partial(per_device, mesh.shape["ctx"], mesh.shape["tp"]),
        mesh=mesh,
        in_specs=(main, main, main, main, owned, owned, P()),
        out_specs=(main, main, main, main, owned),
        check_vma=False,
    )
```

```python
import functools

import jax
import jax.numpy as jnp
from jax import lax
from jax.experimental import pallas as pl
from jax.experimental.pallas import tpu as pltpu
from jax.sharding import PartitionSpec as P

GROUP = 16
MODES = 16
LANES = 128
SUB = 8
TILE_GROUPS = LANES // GROUP
OWN_GROUPS = 2
PIECES = TILE_GROUPS // OWN_GROUPS
SHARES = 4
ROWS = GROUP // SHARES

F32 = jnp.float32
BF16 = jnp.bfloat16
MESH = pl.DeviceIdType.MESH

PAR, STATE, CORR, CARRY, PART = range(5)


def halves(x):
    high = x.astype(BF16)
    return high, (x - high.astype(F32)).astype(BF16)


def wide(x):
    return jnp.concatenate(halves(x), axis=1)


def fold(product):
    return product[:, :LANES] + product[:, LANES:]


def twice(x):
    return jnp.concatenate([x, x], axis=0)


def dot(left, right):
    return jnp.dot(left, right, preferred_element_type=F32)


def dot_nt(left, right):
    return lax.dot_general(left, right, (((1,), (1,)), ((), ())), preferred_element_type=F32)


def iota(shape, dim):
    return lax.broadcasted_iota(jnp.int32, shape, dim)


def stack_halves(x):
    high, low = halves(x)
    parts = []
    for g in range(TILE_GROUPS):
        rows = slice(g * GROUP, (g + 1) * GROUP)
        parts += [high[rows], low[rows]]
    return jnp.concatenate(parts, axis=0)


def grid_of(nctx):
    chips = nctx // 2
    nx = 1
    while nx * nx * 4 <= chips:
        nx *= 2
    return nx, chips // nx


def far_first(n):
    return sorted(range(n), key=lambda d: -min(d, n - d))


def scan_places(tiles, nx, ny):
    if (tiles, nx, ny) == (8, 4, 4):
        return (
            ((0, 0), (0, 3)),
            ((2, 0), (1, 3)),
            ((1, 0), (3, 0)),
            ((3, 3), (2, 3)),
            ((0, 1), (0, 2)),
            ((2, 1), (1, 2)),
            ((1, 1), (3, 1)),
            ((3, 2), (2, 2)),
        )
    return tuple(tuple(divmod(2 * q + k, ny) for k in range(2)) for q in range(tiles))


def exchange_kernel(
    nctx,
    ntp,
    doc_hbm,
    query_hbm,
    key_hbm,
    value_hbm,
    grad_hbm,
    res_hbm,
    time_hbm,
    mixed,
    grad_query,
    grad_key,
    grad_value,
    grad_res_ref,
    doc_ref,
    query,
    key,
    value,
    grad,
    raw,
    par_send,
    par_recv,
    rates,
    weights,
    own_par,
    mix_t,
    dconv_t,
    mix_k,
    dconv_k,
    mix_turned,
    lead_wide,
    tail_wide,
    conv_t,
    dmix_t,
    state_send,
    state_recv,
    carry_send,
    carry_recv,
    corr_send,
    corr_recv,
    powers_wide,
    part_send,
    part_recv,
    load_sem,
    raw_send_sem,
    raw_recv_sem,
    par_recv_sem,
    send_sem,
    recv_sem,
):
    tokens, channels = query.shape
    tiles = channels // LANES
    seq_len = tokens * nctx
    relays = nctx // ntp
    relay_tiles = tiles // relays
    nx, ny = grid_of(nctx)
    c = lax.axis_index("ctx")
    p = lax.axis_index("tp")
    plane = c // relays
    is_relay = plane == p
    mine = lax.rem(c, relays) * ntp + p
    my_x = c // (2 * ny)
    my_y = lax.rem(c // 2, ny)
    my_core = lax.rem(c, 2)

    def remote(src, dst, send, recv, ctx_to, tp_to):
        return pltpu.make_async_remote_copy(
            src_ref=src,
            dst_ref=dst,
            send_sem=send,
            recv_sem=recv,
            device_id=(ctx_to, tp_to),
            device_id_type=MESH,
        )

    def push(src, dst, kind, ctx_to, tp_to):
        here = jnp.logical_and(ctx_to == c, tp_to == p)

        @pl.when(jnp.logical_not(here))
        def _():
            remote(src, dst, send_sem.at[kind], recv_sem.at[kind], ctx_to, tp_to).start()

        @pl.when(here)
        def _():
            pltpu.make_async_copy(src, dst, recv_sem.at[kind]).start()

    def arrived(ref, kind):
        pltpu.make_async_copy(ref, ref, recv_sem.at[kind]).wait()

    def sent(ref, kind):
        pltpu.make_async_copy(ref, ref, send_sem.at[kind]).wait()

    barrier = pltpu.get_barrier_semaphore()

    def greet(ctx_to, tp_to):
        pl.semaphore_signal(barrier, inc=1, device_id=(ctx_to, tp_to), device_id_type=MESH)

    half = ntp // 2
    hub = jnp.where(plane == 4, 2, 0)
    by_hub = plane >= half
    is_hub = jnp.logical_and(by_hub, p == hub)
    low = jnp.logical_and(by_hub, p < half)

    @pl.when(is_relay)
    def _():
        for d in far_first(ntp):
            if d:
                z = lax.rem(p + d, ntp)

                @pl.when(jnp.logical_not(jnp.logical_and(by_hub, jnp.logical_and(z < half, z != hub))))
                def _():
                    greet(c, z)

    @pl.when(is_hub)
    def _():
        for z in range(half):

            @pl.when(z != hub)
            def _():
                greet(c, z)

    for a in range(relays):
        relay = p * relays + a

        @pl.when(relay != c)
        def _():
            greet(relay, p)


    collects = jnp.logical_or(is_relay, is_hub)
    raw_to = jnp.where(low, hub, plane)
    behind = jnp.where(collects, -ntp, jnp.minimum(raw_to, half) - jnp.minimum(p, half))

    @pl.when(jnp.logical_and(jnp.logical_not(collects), behind < 0))
    def _():
        pl.semaphore_wait(barrier, 1)
        for k, src in enumerate((time_hbm, res_hbm)):
            remote(src, raw.at[p, k], raw_send_sem, raw_recv_sem.at[p], c, raw_to).start()

    sources = (query_hbm, key_hbm, value_hbm, grad_hbm, doc_hbm, time_hbm, res_hbm)
    targets = (query, key, value, grad, doc_ref, own_par.at[0], own_par.at[1])
    loads = [
        pltpu.make_async_copy(src, dst, load_sem.at[i])
        for i, (src, dst) in enumerate(zip(sources, targets))
    ]
    for i in (5, 6, 4, 1, 2, 0, 3):
        loads[i].start()
    base_x = (p * relays // 2) // ny
    base_y = lax.rem(p * relays // 2, ny)
    places = scan_places(tiles, nx, ny)

    def scanner(q, h):
        dx, dy = places[q][h // 2]
        x, y = lax.rem(base_x + dx, nx), lax.rem(base_y + dy, ny)
        return (x * ny + y) * 2 + h % 2

    tile_of = jnp.int32(0)
    share_of = my_core
    for q in range(tiles):
        for k in range(2):
            hit = scanner(q, 2 * k) == c - my_core
            tile_of = jnp.where(hit, q, tile_of)
            share_of = jnp.where(hit, 2 * k + my_core, share_of)

    xs = [lax.rem(my_x + d, nx) * (2 * ny) for d in range(nx)]
    ys = [lax.rem(my_y + d, ny) * 2 for d in range(ny)]
    cores = [my_core, 1 - my_core]
    offsets = [(dx, dy, dk) for dx in range(nx) for dy in range(ny) for dk in range(2)]
    offsets.sort(key=lambda o: -(min(o[0], nx - o[0]) + min(o[1], ny - o[1]) + 0.1 * o[2]))
    around = [xs[dx] + ys[dy] + cores[dk] for dx, dy, dk in offsets if dx or dy or dk]

    def send_raw():
        pl.semaphore_wait(barrier, 1)
        remote(own_par, raw.at[p], raw_send_sem, raw_recv_sem.at[p], c, raw_to).start()

    loads[5].wait()
    loads[6].wait()

    @pl.when(behind == 0)
    def _():
        send_raw()

    @pl.when(collects)
    def _():
        raw[p] = own_par[...]

    first = c * tokens
    loads[4].wait()
    end0 = doc_ref[0]
    end1 = end0 + doc_ref[1]
    end2 = end1 + doc_ref[2]
    end3 = end2 + doc_ref[3]
    ends = (end0, end1, end2, end3)

    def doc_of(position):
        total = (position >= end0).astype(jnp.int32)
        for end in ends[1:]:
            total = total + (position >= end).astype(jnp.int32)
        return total

    square = (tokens, LANES)
    row = iota(square, 0)
    col = iota(square, 1)
    doc_row = doc_of(first + row)
    doc_col = doc_of(first + col)
    flip_row = tokens - 1 - row
    turned = jnp.where(
        jnp.logical_and(doc_of(first + flip_row) == doc_col, col >= flip_row), 1.0, 0.0
    )
    turn = jnp.where(flip_row == col, 1.0, 0.0).astype(BF16)
    block_of = iota((1, LANES), 1) // GROUP

    for i in range(4):
        loads[i].wait()

    def lanes_of(q):
        return pl.ds(pl.multiple_of(q * LANES, LANES), LANES)

    def prepare(q, _):
        at = lanes_of(q)
        mixture = key[:, at].astype(F32) * value[:, at].astype(F32)
        dconv = grad[:, at].astype(F32) * query[:, at].astype(F32)
        mix_t[q] = stack_halves(mixture.T)
        mix_k[q] = wide(mixture.T)
        dconv_t[q] = stack_halves(dconv.T)
        dconv_k[q] = wide(dconv.T)
        mix_turned[q] = dot(turn, wide(mixture)).astype(BF16)
        return 0

    lax.fori_loop(0, tiles, prepare, 0)

    def correlate(q, _):
        nothing = jnp.zeros((GROUP, LANES), BF16)
        half_groups = TILE_GROUPS // 2
        half_lanes = LANES // 2
        for h in range(2):
            high = mix_turned[q, :, h * half_lanes : (h + 1) * half_lanes]
            low = mix_turned[q, :, LANES + h * half_lanes : LANES + (h + 1) * half_lanes]
            left = jnp.concatenate([high, low, high, low], axis=1)
            for first_group in range(h * half_groups, (h + 1) * half_groups, 2):
                columns = []
                for g in (first_group, first_group + 1):
                    rows = []
                    for section in range(4):
                        at = (2 * g + section // 2) * GROUP
                        taken = dconv_t[q, at : at + GROUP, :]
                        for other in range(h * half_groups, (h + 1) * half_groups):
                            rows.append(taken if other == g else nothing)
                    columns.append(jnp.concatenate(rows, axis=0))
                pairs = dot(left, jnp.concatenate(columns, axis=1))
                for k in range(OWN_GROUPS):
                    lags = pltpu.roll(
                        pairs[:, k * LANES : (k + 1) * LANES] * turned,
                        1,
                        1,
                        stride=1,
                        stride_axis=0,
                    )
                    block = PIECES * q + first_group // OWN_GROUPS
                    corr_send[block, k : k + 1, :] = jnp.sum(lags, axis=0, keepdims=True)
        return 0

    early = jnp.where(behind > 2, tiles, 0)
    lax.fori_loop(0, early, correlate, 0)

    @pl.when(behind > 0)
    def _():
        send_raw()

    lower = raw.at[pl.ds(0, half)]

    @pl.when(is_hub)
    def _():
        for z in range(half):

            @pl.when(z != hub)
            def _():
                pltpu.make_async_copy(own_par, raw.at[z], raw_recv_sem.at[z]).wait()

        pl.semaphore_wait(barrier, 1)
        remote(lower, lower, raw_send_sem, raw_recv_sem.at[hub], c, plane).start()

    my_relay = lax.rem(c, relays)

    @pl.when(is_relay)
    def _():
        for z in range(half):

            @pl.when(jnp.logical_not(jnp.logical_or(by_hub, z == p)))
            def _():
                pltpu.make_async_copy(own_par, raw.at[z], raw_recv_sem.at[z]).wait()

        @pl.when(by_hub)
        def _():
            pltpu.make_async_copy(lower, lower, raw_recv_sem.at[hub]).wait()

        for z in range(half, ntp):

            @pl.when(z != p)
            def _():
                pltpu.make_async_copy(own_par, raw.at[z], raw_recv_sem.at[z]).wait()

        for t in range(relay_tiles):
            for k in range(2):
                parts = []
                for b in range(PIECES):
                    block = raw[t * PIECES + b, k]
                    parts += [block[0:1], block[1:2]]
                line = jnp.concatenate(parts, axis=1)
                at = 2 * t + k
                par_send[at : at + 1, :] = 1.0 / line if k == 0 else line
        pl.semaphore_wait(barrier, nctx - 1)
        for to in around:
            remote(
                par_send, par_recv.at[my_relay], send_sem.at[PAR], par_recv_sem.at[my_relay], to, p
            ).start()
        pltpu.make_async_copy(par_send, par_recv.at[my_relay], par_recv_sem.at[my_relay]).start()

    lax.fori_loop(early, tiles, correlate, 0)

    pos = iota((SUB, LANES), 0).astype(F32)
    eights = iota((tokens // SUB, LANES), 0).astype(F32) * SUB
    doc_first = doc_of(first)
    doc_last = doc_of(first + tokens - 1)
    at_start = jnp.where(doc_row == doc_first, 1.0, 0.0)
    at_end = jnp.where(doc_row == doc_last, 1.0, 0.0)

    def own_blocks(x):
        out = jnp.zeros((GROUP, LANES), F32)
        for g in range(TILE_GROUPS):
            out = jnp.where(block_of == g, fold(x[g * GROUP : (g + 1) * GROUP]), out)
        return out

    for a in range(relays):
        pltpu.make_async_copy(par_recv.at[a], par_recv.at[a], par_recv_sem.at[a]).wait()
        for t in range(relay_tiles):
            rates[a * relay_tiles + t] = par_recv[a, 2 * t : 2 * t + 1, :]
            weights[a * relay_tiles + t] = par_recv[a, 2 * t + 1 : 2 * t + 2, :]

    def states(q):
        rate_row = rates[q]
        tall = jnp.exp(-eights * rate_row)
        short = jnp.exp(-pos * rate_row)
        short_flip = jnp.exp((pos - (SUB - 1.0)) * rate_row)
        steps = tokens // SUB
        decay = jnp.concatenate([short * tall[i : i + 1] for i in range(steps)], axis=0)
        flip = jnp.concatenate(
            [short_flip * tall[steps - 1 - i : steps - i] for i in range(steps)], axis=0
        )
        end_state = own_blocks(dot(mix_k[q], twice(wide(flip * at_end))))
        start_state = own_blocks(dot(dconv_k[q], twice(wide(decay * at_start))))
        for h in range(SHARES):
            to = scanner(q, h)
            state_send[to, 0:ROWS, :] = end_state[h * ROWS : (h + 1) * ROWS, :]
            state_send[to, ROWS:, :] = start_state[h * ROWS : (h + 1) * ROWS, :]

    for q in range(tiles):
        states(q)
    for to in around:
        remote(
            state_send.at[to], state_recv.at[c], send_sem.at[STATE], recv_sem.at[STATE], to, p
        ).start()
    pltpu.make_async_copy(state_send.at[c], state_recv.at[c], recv_sem.at[STATE]).start()

    for z in far_first(ntp):
        for a in range(relays):
            tp_to = lax.rem(p + z, ntp)
            push(corr_send.at[a * ntp + tp_to], corr_recv.at[c], CORR, p * relays + a, tp_to)

    lag = col.astype(F32)
    doc_before = doc_of(first - 1)
    doc_after = doc_of(first + tokens)
    upper = jnp.where(jnp.logical_and(doc_row == doc_col, col >= row), 1.0, 0.0)
    with_before = jnp.where(doc_col == doc_before, 1.0, 0.0)
    with_after = jnp.where(doc_col == doc_after, 1.0, 0.0)

    def quarters(x):
        return fold(x[:GROUP] + x[GROUP:])

    def inside(q, _):
        rate = jnp.broadcast_to(rates[q], square).T
        weight = jnp.broadcast_to(weights[q], square).T
        lead_wide[q] = wide(jnp.exp(-(lag + 1.0) * rate) * (weight * with_before))
        tail_wide[q] = wide(jnp.exp((lag - float(tokens)) * rate) * (weight * with_after))
        terms = jnp.exp(-lag * rate) * weight
        for g in range(TILE_GROUPS):
            taps = jnp.sum(terms[g * MODES : (g + 1) * MODES], axis=0, keepdims=True)
            spread = jnp.broadcast_to(taps, square)
            toeplitz = pltpu.roll(spread, 0, 1, stride=1, stride_axis=0) * upper
            high, low = halves(toeplitz)
            rows = slice(g * GROUP, (g + 1) * GROUP)
            both = slice(2 * g * GROUP, 2 * (g + 1) * GROUP)
            conv_t[q, rows, :] = quarters(
                dot(mix_t[q, both, :], jnp.concatenate([high, low], axis=1))
            )
            dmix_t[q, rows, :] = quarters(
                dot_nt(dconv_t[q, both, :], jnp.concatenate([high, low], axis=0))
            )
        return 0

    lax.fori_loop(0, tiles // 2, inside, 0)

    arrived(state_recv, STATE)
    my_rate = rates[tile_of]
    span = jnp.exp(-float(tokens) * my_rate)
    once = jnp.exp(-my_rate)
    piece = (2 * ROWS, LANES)
    cut_in = [jnp.full(piece, end // tokens, jnp.int32) for end in ends[:3]]
    cut_out = [jnp.full(piece, (end - 1) // tokens, jnp.int32) for end in ends[:3]]
    cut_at = [jnp.full(piece, end, jnp.int32) for end in ends[:3]]
    is_end = iota(piece, 0) < ROWS

    def kept(cuts, at, factor):
        hit = cuts[0] == at
        for cut in cuts[1:]:
            hit = jnp.logical_or(hit, cut == at)
        return jnp.where(hit, 0.0, factor)

    back = jnp.zeros(piece, F32)
    ahead = jnp.zeros(piece, F32)
    backs, aheads = [None] * nctx, [None] * nctx
    for i in range(nctx):
        j = nctx - 1 - i
        backs[j] = back
        back = kept(cut_out, j, span) * back + state_recv[j]
        aheads[i] = ahead
        ahead = kept(cut_in, i, span) * ahead + state_recv[i]
    carried = jnp.zeros(piece, F32)
    for i in range(nctx):
        begun = pltpu.roll(state_recv[i], ROWS, 0)
        carried = carried + kept(cut_at, i * tokens, once) * (aheads[i] * begun)
    part_send[...] = jnp.sum(jnp.where(is_end, carried, 0.0), axis=0, keepdims=True)
    for b in range(PIECES):
        block = tile_of * PIECES + b
        push(
            part_send,
            part_recv.at[share_of],
            PART,
            p * relays + block // ntp,
            lax.rem(block, ntp),
        )
    for i in range(nctx):
        carry_send[i] = jnp.where(is_end, aheads[i], backs[i])
    for i in range(nctx - 1):
        to = jnp.where(c <= i, i + 1, i)
        remote(
            carry_send.at[to], carry_recv.at[c], send_sem.at[CARRY], recv_sem.at[CARRY], to, p
        ).start()
    pltpu.make_async_copy(carry_send.at[c], carry_recv.at[c], recv_sem.at[CARRY]).start()

    lax.fori_loop(tiles // 2, tiles, inside, 0)

    own_rate = 1.0 / own_par[0]
    own_rate = jnp.concatenate([own_rate[0:1], own_rate[1:2]] * PIECES, axis=1)
    powers = jnp.exp(-row.astype(F32) * own_rate)
    powers_wide[...] = wide(powers)

    arrived(carry_recv, CARRY)

    def spread_out(q, rows):
        state = jnp.concatenate(
            [carry_recv[scanner(q, h), rows, :] for h in range(SHARES)], axis=0
        )
        parts = []
        for half in halves(state):
            zero = jnp.zeros_like(half)
            parts.append(
                jnp.concatenate(
                    [jnp.where(block_of == g, half, zero) for g in range(TILE_GROUPS)], axis=0
                )
            )
        return jnp.concatenate(parts, axis=1)

    for q in range(tiles):
        at = slice(q * LANES, (q + 1) * LANES)
        entered = fold(dot(spread_out(q, slice(0, ROWS)), twice(lead_wide[q])))
        conv = (conv_t[q] + entered).T
        mixed[:, at] = (query[:, at].astype(F32) * conv).astype(BF16)
        grad_query[:, at] = (grad[:, at].astype(F32) * conv).astype(BF16)
        left = fold(dot(spread_out(q, slice(ROWS, 2 * ROWS)), twice(tail_wide[q])))
        dmix = (dmix_t[q] + left).T
        grad_key[:, at] = (dmix * value[:, at].astype(F32)).astype(BF16)
        grad_value[:, at] = (dmix * key[:, at].astype(F32)).astype(BF16)

    arrived(corr_recv, CORR)

    sums = [corr_recv[i] for i in range(nctx)]
    while len(sums) > 1:
        sums = [sums[i] + sums[i + 1] for i in range(0, len(sums), 2)]
    corr = sums[0]
    by_mode = fold(dot(wide(jnp.concatenate([corr] * PIECES, axis=0)), twice(powers_wide[...])))
    lane = iota((1, LANES), 1)
    grad_row = jnp.where(lax.rem(lane // MODES, OWN_GROUPS) == 0, by_mode[0:1], by_mode[1:2])
    arrived(part_recv, PART)
    for h in range(SHARES):
        grad_row = grad_row + part_recv[h]
    step = LANES // PIECES
    grad_row = jnp.where(lane // step == lax.rem(mine, PIECES), grad_row / seq_len, 0.0)
    whole = grad_row
    for b in range(1, PIECES):
        whole = whole + pltpu.roll(grad_row, b * step, 1)
    grad_res_ref[0:1, :] = whole[:, :MODES]
    grad_res_ref[1:2, :] = pltpu.roll(whole, LANES - MODES, 1)[:, :MODES]

    sent(state_send.at[pl.ds(0, nctx - 1)], STATE)
    sent(carry_send.at[pl.ds(0, nctx - 1)], CARRY)
    to_self = jnp.logical_and(is_relay, mine // PIECES == tile_of)

    @pl.when(to_self)
    def _():
        sent(part_recv.at[pl.ds(0, PIECES - 1)], PART)

    @pl.when(jnp.logical_not(to_self))
    def _():
        sent(part_recv, PART)

    @pl.when(is_relay)
    def _():
        for _ in range(nctx - 1):
            pltpu.make_async_copy(par_send, par_send, send_sem.at[PAR]).wait()
        sent(corr_send.at[pl.ds(0, nctx - 1)], CORR)

    @pl.when(jnp.logical_not(is_relay))
    def _():
        sent(corr_send, CORR)

    @pl.when(jnp.logical_not(collects))
    def _():
        pltpu.make_async_copy(own_par, own_par, raw_send_sem).wait()

    @pl.when(is_hub)
    def _():
        pltpu.make_async_copy(lower, lower, raw_send_sem).wait()


def copy_kernel(*refs):
    count = (len(refs) - 1) // 2
    copies = [
        pltpu.make_async_copy(refs[i], refs[count + i], refs[-1].at[i]) for i in range(count)
    ]
    for copy in copies:
        copy.start()
    for copy in copies:
        copy.wait()


def per_device(nctx, ntp, query, key, value, grad, residues, decay_time, doc_lengths):
    tokens, channels = query.shape
    tiles = channels // LANES
    relays = nctx // ntp
    vmem = pl.BlockSpec(memory_space=pltpu.VMEM)
    hbm = pl.BlockSpec(memory_space=pl.ANY)
    flat = jax.ShapeDtypeStruct((tokens, channels), BF16)
    small = jax.ShapeDtypeStruct(residues.shape, F32)
    by_device = pltpu.VMEM((nctx, 2 * ROWS, LANES), F32)
    lags = pltpu.VMEM((nctx, OWN_GROUPS, LANES), F32)
    line = pltpu.VMEM((tiles, 1, LANES), F32)
    arguments = (doc_lengths, query, key, value, grad, residues, decay_time)
    outs = pl.pallas_call(
        functools.partial(exchange_kernel, nctx, ntp),
        out_shape=(*[pltpu.VMEM(flat.shape, BF16)] * 4, pltpu.VMEM(small.shape, F32)),
        in_specs=[hbm] * 7,
        out_specs=(vmem,) * 5,
        scratch_shapes=[
            pltpu.SMEM(doc_lengths.shape, jnp.int32),
            *[pltpu.VMEM((tokens, channels), BF16)] * 4,
            pltpu.VMEM((ntp, 2, OWN_GROUPS, MODES), F32),
            pltpu.VMEM((2 * tiles // relays, LANES), F32),
            pltpu.VMEM((relays, 2 * tiles // relays, LANES), F32),
            line,
            line,
            pltpu.VMEM((2, OWN_GROUPS, MODES), F32),
            *[pltpu.VMEM((tiles, 2 * LANES, tokens), BF16)] * 2,
            *[pltpu.VMEM((tiles, LANES, 2 * LANES), BF16)] * 5,
            *[pltpu.VMEM((tiles, LANES, LANES), F32)] * 2,
            *[by_device] * 4,
            lags,
            lags,
            pltpu.VMEM((tokens, 2 * LANES), BF16),
            pltpu.VMEM((1, LANES), F32),
            pltpu.VMEM((SHARES, 1, LANES), F32),
            pltpu.SemaphoreType.DMA((7,)),
            pltpu.SemaphoreType.DMA,
            pltpu.SemaphoreType.DMA((ntp,)),
            pltpu.SemaphoreType.DMA((relays,)),
            pltpu.SemaphoreType.DMA((5,)),
            pltpu.SemaphoreType.DMA((5,)),
        ],
        compiler_params=pltpu.CompilerParams(
            collective_id=0, has_side_effects=True, vmem_limit_bytes=32 * 1024 * 1024
        ),
    )(*[pltpu.with_memory_space_constraint(x, pltpu.HBM) for x in arguments])
    return tuple(
        pl.pallas_call(
            copy_kernel,
            out_shape=(flat, flat, flat, flat, small),
            in_specs=[hbm] * 5,
            out_specs=(hbm,) * 5,
            scratch_shapes=[pltpu.SemaphoreType.DMA((5,))],
            compiler_params=pltpu.CompilerParams(vmem_limit_bytes=1024 * 1024),
        )(*[pltpu.with_memory_space_constraint(x, pltpu.VMEM) for x in outs])
    )


def solution(mesh):
    main = P("ctx", "tp")
    owned = P(("ctx", "tp"), None)
    return jax.shard_map(
        functools.partial(per_device, mesh.shape["ctx"], mesh.shape["tp"]),
        mesh=mesh,
        in_specs=(main, main, main, main, owned, owned, P()),
        out_specs=(main, main, main, main, owned),
        check_vma=False,
    )
```
